128 devices in a mesh: depth: 8 (over x_lo, y), row: 4 (over x_hi, core), col: 4 (over z).
Axes of the slice: x: 4 (x_hi: 2, x_lo: 2; x = x_hi * 2 + x_lo), y: 4, z: 4, core: 2. Of those that a mesh axis runs over, the one named last changes fastest.
Arguments:
- grad_out: bfloat16 [2048, 12288], P(('depth', 'col'), 'row'), may hold values from -6 to 6
- pre_act: bfloat16 [2048, 24576], P('col', 'depth'), may hold values from -8 to 8
- w_down: bfloat16 [24576, 12288], P(('depth', 'col'), 'row'), may hold values from -0.0546875 to 0.0546875
Outputs:
- grad_pre: bfloat16 [2048, 24576], P('row', ('depth', 'col'))
- grad_down: bfloat16 [24576, 12288], P(('depth', 'col'), 'row')
The draws below stay inside these ranges and needn't reach their ends.
All inputs are finite; a program needn't handle non-finite values.
Results may differ from the reference program's by a relative error of at most 0.0048.
Values may be sent and summed in bfloat16 or wider, within the bound.
No kernel may reach another device: no remote copies, remote signals or barrier semaphores. Data moves between devices by JAX's collectives and lax.ppermute only.
A program may use at most 128 MiB of HBM per device.

```python
import math
import jax
import jax.numpy as jnp
from jax import lax

D = 12288
FF = 24576
TOKENS = 2048


def with_spikes(drawn, stream_key, source, target, parts, factor):
    def block_of(position):
        return (jnp.arange(drawn.shape[position]) // (drawn.shape[position] // parts)).reshape((-1,) + (1,) * (drawn.ndim - 1 - position))

    one_side = jax.random.permutation(stream_key, parts)[block_of(target)]
    other_side = (block_of(target) + parts // 2) % parts
    return jnp.where((block_of(source) == one_side) | (block_of(source) == other_side), factor * drawn, drawn)


def shard_levels(key, dims, cuts, smallest, top_value):
    loudness, own = 1.0, jax.random.fold_in(key, 6)
    for axis_at, shards_of in cuts:
        steps = jnp.exp(jax.random.uniform(jax.random.fold_in(own, axis_at), (shards_of,), jnp.float32, smallest / len(cuts), top_value / len(cuts)))
        loudness = loudness * jnp.repeat(steps, dims[axis_at] // shards_of).reshape([-1 if axis == axis_at else 1 for axis in range(len(dims))])
    return loudness


def scatter_about(stream_key, extent, deviation, reach, pieces=(), dtype=jnp.bfloat16):
    gain = shard_levels(stream_key, extent, pieces, -0.22, 0.18) if pieces else 1.0
    drawn = jax.random.normal(stream_key, extent, jnp.float32) * deviation * gain
    return jnp.minimum(jnp.maximum(drawn, -reach), reach).astype(dtype)


def gaussian_with(rng, extent, deviation, limit, pieces, heavy, dtype=jnp.bfloat16):
    values = deviation * jax.random.normal(rng, extent, jnp.float32)
    if pieces:
        values = values * shard_levels(rng, extent, pieces, -0.22, 0.18)
    return jnp.clip(with_spikes(values, jax.random.fold_in(rng, 3), *heavy), -limit, limit).astype(dtype)


def setup_inputs(seed: int = 0) -> dict:
    key_list = jax.random.split(jax.random.key(seed), 4)
    return {
        "grad_out": gaussian_with(key_list[0], (TOKENS, D), 1.0, 6.0, ((0, 32), (1, 4)), (1, 0, 32, 2.75)),
        "pre_act": scatter_about(key_list[1], (TOKENS, FF), 1.5, 8.0, ((0, 4), (1, 8))),
        "w_down": scatter_about(key_list[2], (FF, D), D ** -0.5, 0.0546875, ((0, 32), (1, 4))),
    }


gelu_const = math.sqrt(2.0 / math.pi)

def gelu_parts(pre):
    inner = gelu_const * (pre + 0.044715 * pre * pre * pre)
    bend = jnp.tanh(inner)
    value = 0.5 * pre * (1.0 + bend)
    derivative = 0.5 * (1.0 + bend) + 0.5 * pre * (1.0 - bend * bend) * gelu_const * (1.0 + 3.0 * 0.044715 * pre * pre)
    return (value, derivative)

def reference(grad_out, pre_act, w_down):
    value, derivative = gelu_parts(pre_act.astype(jnp.float32))
    activated = value.astype(jnp.bfloat16)
    hidden_grad = lax.dot_general(grad_out, w_down, (((1,), (1,)), ((), ())), preferred_element_type=jnp.float32)
    grad_pre = (hidden_grad * derivative).astype(jnp.bfloat16)
    grad_down = lax.dot_general(activated, grad_out, (((0,), (0,)), ((), ())), preferred_element_type=jnp.float32)
    return (grad_pre, grad_down.astype(jnp.bfloat16))
```

```python
import functools
import math

import jax
import jax.numpy as jnp
import numpy as np
from jax import lax
from jax.experimental import pallas as pl
from jax.experimental.pallas import tpu as pltpu
from jax.sharding import PartitionSpec as P

gelu_const = math.sqrt(2.0 / math.pi)

SHARDS = 32
ROWS = 64
FEATS = 3072
HID = 768
X, Y0, Y1, Z0, Z1 = 16, 4, 12, 1, 3
DIMS = (X, Y0, Z0, Y1, Z1)
WIDTHS = (640, 512, 640, 640, 640)
OFFSETS = tuple(int(v) for v in np.cumsum((0,) + WIDTHS)[:-1])
CHAINS = len(WIDTHS)
ORDERS = tuple(tuple(DIMS[(p + k) % 5] for k in range(5)) for p in range(CHAINS))
PARTS = (48, 16)
STARTS = (0, 48)


def place_table():
    table = np.zeros((CHAINS, SHARDS), np.int32)
    for p, order in enumerate(ORDERS):
        for i in range(SHARDS):
            delta = 0
            for k, mask in enumerate(order):
                if i >> k & 1:
                    delta ^= mask
            table[p, delta] = i
    return table.reshape(-1)


def swap(x, mask):
    if mask >= 4:
        return lax.ppermute(x, "depth", [(i, i ^ (mask >> 2)) for i in range(8)])
    return lax.ppermute(x, "col", [(i, i ^ mask) for i in range(4)])


def swap_row(x, mask):
    return lax.ppermute(x, "row", [(i, i ^ mask) for i in range(4)])


def params(mib):
    return pltpu.CompilerParams(vmem_limit_bytes=mib * 1024 * 1024)


ANY = pl.BlockSpec(memory_space=pl.ANY)
VMEM = pl.BlockSpec(memory_space=pltpu.VMEM)
SMEM = pl.BlockSpec(memory_space=pltpu.SMEM)


def gelu_kernel(where, pre, got_a, got_b, got_c, other, *refs):
    outs, (buf, sems), acts = refs[:4], refs[4:6], refs[6:]
    act_t, slopes = outs[:2], outs[2:]
    row, col = where[0], where[1]
    core = row % 2
    quarter, half = SHARDS * ROWS // 4, SHARDS * ROWS // 8
    copies = [
        pltpu.make_async_copy(
            pre.at[:, pl.ds(pl.multiple_of(col * HID, HID), HID)],
            buf.at[pl.ds(pl.multiple_of(col * quarter, quarter), quarter)],
            sems.at[0],
        )
    ]
    for j, (got, mask) in enumerate(((got_a, Z0), (got_b, Z1), (got_c, Z0 ^ Z1))):
        base = (col ^ mask) * quarter
        copies.append(
            pltpu.make_async_copy(
                got, buf.at[pl.ds(pl.multiple_of(base + core * half, half), half)], sems.at[1 + 2 * j]
            )
        )
        copies.append(
            pltpu.make_async_copy(
                other.at[pl.ds(j * half, half)],
                buf.at[pl.ds(pl.multiple_of(base + (1 - core) * half, half), half)],
                sems.at[2 + 2 * j],
            )
        )
    for c in copies:
        c.start()
    for c in copies:
        c.wait()

    def one_shard(s, carry):
        v = buf[pl.ds(pl.multiple_of(s * ROWS, ROWS), ROWS), :].astype(jnp.float32)
        bend = jnp.tanh(gelu_const * (v + 0.044715 * v * v * v))
        a = (0.5 * v * (1.0 + bend)).astype(jnp.bfloat16)
        for part in range(2):
            n, at = PARTS[part], STARTS[part]
            acts[part][pl.ds(pl.multiple_of(s * n, 16), n), :] = a[at : at + n]
        return carry

    lax.fori_loop(0, SHARDS, one_shard, 0)

    def one_slope(s, carry):
        at_row = pl.multiple_of(row * quarter + s * ROWS, ROWS)
        v = buf[pl.ds(at_row, ROWS), :].astype(jnp.float32)
        bend = jnp.tanh(gelu_const * (v + 0.044715 * v * v * v))
        d = 0.5 * (1.0 + bend) + 0.5 * v * (1.0 - bend * bend) * gelu_const * (1.0 + 3.0 * 0.044715 * v * v)
        for part in range(2):
            n, at = PARTS[part], STARTS[part]
            slopes[part][s] = d[at : at + n]
        return carry

    lax.fori_loop(0, SHARDS // 4, one_slope, 0)

    for part in range(2):

        def one_turn(j, carry, part=part):
            at = pl.multiple_of(j * 128, 128)
            act_t[part][:, pl.ds(at, 128)] = acts[part][pl.ds(at, 128), :].T
            return carry

        lax.fori_loop(0, SHARDS * PARTS[part] // 128, one_turn, 0)


def gelu_call(where, pre, got, other):
    tokens = [SHARDS * n for n in PARTS]
    return pl.pallas_call(
        gelu_kernel,
        out_shape=[jax.ShapeDtypeStruct((HID, t), jnp.bfloat16) for t in tokens]
        + [jax.ShapeDtypeStruct((SHARDS // 4, n, HID), jnp.float32) for n in PARTS],
        in_specs=[SMEM] + [ANY] * 5,
        out_specs=[VMEM] * 4,
        scratch_shapes=[pltpu.VMEM((SHARDS * ROWS, HID), jnp.bfloat16), pltpu.SemaphoreType.DMA((7,))]
        + [pltpu.VMEM((t, HID), jnp.bfloat16) for t in tokens],
        compiler_params=params(32),
        cost_estimate=pl.CostEstimate(flops=2048 * HID * 40, bytes_accessed=16 << 20, transcendentals=2048 * HID),
        name="gelu",
    )(where, pre, *got, other)


def hidden_kernel(n, where, table, w, *refs):
    blocks = refs[: 2 * CHAINS]
    keep, send, gathered, g, in_sems, out_sems = refs[2 * CHAINS :]
    row, mine = where[0], where[2]
    per = SHARDS // 4
    order = [(1, 1), (0, 1), (1, 0), (0, 0)]
    quarters = [row ^ (2 * a + b) for a, b in order]

    for t, q in enumerate(quarters):

        def fetch(k, carry, t=t, q=q):
            s = q * per + k
            for p in range(CHAINS):
                i = table[p * SHARDS + (s ^ mine)]
                for side in range(2):

                    @pl.when(i // 16 == side)
                    def _(p=p, side=side, i=i):
                        pltpu.make_async_copy(
                            blocks[2 * p + side].at[i % 16],
                            g.at[s, :, pl.ds(OFFSETS[p], WIDTHS[p])],
                            in_sems.at[t],
                        ).start()

            return carry

        lax.fori_loop(0, per, fetch, 0)

    outs = []
    for t, q in enumerate(quarters):
        a, b = order[t]
        here = g.at[pl.ds(pl.multiple_of(q * per, per), per)]
        pltpu.make_async_copy(here, here, in_sems.at[t]).wait()
        out = pltpu.make_async_copy(here, gathered.at[pl.ds(pl.multiple_of(q * per, per), per)], out_sems.at[t])
        out.start()
        outs.append(out)
        lhs = here[...].reshape(per * n, FEATS)
        h = lax.dot_general(lhs, w[...], (((1,), (1,)), ((), ())), preferred_element_type=jnp.float32)
        if b:
            send[a] = h.astype(jnp.bfloat16).reshape(per, n, HID)
        else:
            keep[a] = h.reshape(per, n, HID)
    for out in outs:
        out.wait()


def hidden_call(part, where, table, w, blocks):
    n = PARTS[part]
    per = SHARDS // 4
    return pl.pallas_call(
        functools.partial(hidden_kernel, n),
        out_shape=[
            jax.ShapeDtypeStruct((2, per, n, HID), jnp.float32),
            jax.ShapeDtypeStruct((2, per, n, HID), jnp.bfloat16),
            jax.ShapeDtypeStruct((SHARDS, n, FEATS), jnp.bfloat16),
        ],
        in_specs=[SMEM, SMEM, VMEM] + [ANY] * (2 * CHAINS),
        out_specs=[VMEM, VMEM, ANY],
        scratch_shapes=[
            pltpu.VMEM((SHARDS, n, FEATS), jnp.bfloat16),
            pltpu.SemaphoreType.DMA((4,)),
            pltpu.SemaphoreType.DMA((4,)),
        ],
        compiler_params=params(40),
        cost_estimate=pl.CostEstimate(
            flops=2 * SHARDS * n * FEATS * HID, bytes_accessed=SHARDS * n * FEATS * 4, transcendentals=0
        ),
        name="hidden",
    )(where, table, w, *blocks)


def down_kernel(at_a, at_b, g_a, g_b, *refs):
    out = refs[-1]
    acc = jnp.dot(at_a[...], g_a[...], preferred_element_type=jnp.float32)
    acc += jnp.dot(at_b[...], g_b[...], preferred_element_type=jnp.float32)
    out[...] = acc.astype(jnp.bfloat16)


def down_call(acts, gathered, first, count, base=None):
    wide = 512
    tokens = [SHARDS * n for n in PARTS]
    in_specs = [pl.BlockSpec((HID, t), lambda j: (0, 0)) for t in tokens]
    in_specs += [pl.BlockSpec((t, wide), lambda j: (0, j + first)) for t in tokens]
    args = [*acts, *(g.reshape(t, FEATS) for g, t in zip(gathered, tokens))]
    aliases = {}
    if base is not None:
        in_specs.append(ANY)
        args.append(base)
        aliases = {4: 0}
    return pl.pallas_call(
        down_kernel,
        grid=(count,),
        out_shape=jax.ShapeDtypeStruct((HID, FEATS), jnp.bfloat16),
        in_specs=in_specs,
        out_specs=pl.BlockSpec((HID, wide), lambda j: (0, j + first)),
        input_output_aliases=aliases,
        compiler_params=params(40),
        cost_estimate=pl.CostEstimate(
            flops=2 * 2048 * HID * wide * count, bytes_accessed=count * wide * 2 * (2048 + HID), transcendentals=0
        ),
        name="down",
    )(*args)


def local(grad_out, pre_act, w_down):
    depth, row, col = (lax.axis_index(a) for a in ("depth", "row", "col"))
    where = jnp.stack([row, col, depth * 4 + col]).astype(jnp.int32)
    table = jnp.asarray(place_table())
    core = row % 2

    blocks = []
    for p in range(CHAINS):
        blocks.append(grad_out[:, OFFSETS[p] : OFFSETS[p] + WIDTHS[p]].reshape(1, ROWS, WIDTHS[p]))
    for k in range(3):
        got = [swap(blocks[p], ORDERS[p][k]) for p in range(CHAINS)]
        blocks = [jnp.concatenate([b, r], 0) for b, r in zip(blocks, got)]
    got = [swap(blocks[p], ORDERS[p][3]) for p in range(CHAINS)]
    own, came = ([], []), ([], [])
    for part in range(2):
        rows = slice(STARTS[part], STARTS[part] + PARTS[part])
        for p in range(CHAINS):
            own[part].append(jnp.concatenate([blocks[p][:, rows], got[p][:, rows]], 0))
    for part in range(2):
        for p in range(CHAINS):
            came[part].append(swap(own[part][p], ORDERS[p][4]))

    half = pre_act.shape[0] // 2
    fetched = []
    for mask in (Z0, Z1, Z0 ^ Z1):
        chunk = lax.dynamic_slice(pre_act, (core * half, (col ^ mask) * HID), (half, HID))
        fetched.append(swap(chunk, mask))
    other = swap_row(jnp.concatenate(fetched, 0), 1)
    act_a, act_b, slope_a, slope_b = gelu_call(where, pre_act, fetched, other)

    done, gathered = [], []
    for part in range(2):
        pairs = [b for p in range(CHAINS) for b in (own[part][p], came[part][p])]
        keep, send, g = hidden_call(part, where, table, w_down, pairs)
        gathered.append(g)
        total = keep + swap_row(send, 1).astype(jnp.float32)
        far = swap_row(total[1].astype(jnp.bfloat16), 2)
        done.append((total[0], far))
    grad_down = down_call((act_a, act_b), gathered, 0, 2)
    grad_down = down_call((act_a, act_b), gathered, 2, 4, grad_down)
    parts = [
        ((mine + far.astype(jnp.float32)) * slope).astype(jnp.bfloat16)
        for (mine, far), slope in zip(done, (slope_a, slope_b))
    ]
    grad_pre = jnp.concatenate(parts, 1).reshape(512, HID)
    return (grad_pre, grad_down)


def solution(mesh):
    placed = (P(("depth", "col"), "row"), P("col", "depth"), P(("depth", "col"), "row"))
    return jax.shard_map(
        local,
        mesh=mesh,
        in_specs=placed,
        out_specs=(P("row", ("depth", "col")), P(("depth", "col"), "row")),
        check_vma=False,
    )
```

```python
import functools
import math

import jax
import jax.numpy as jnp
import numpy as np
from jax import lax
from jax.experimental import pallas as pl
from jax.experimental.pallas import tpu as pltpu
from jax.sharding import PartitionSpec as P

gelu_const = math.sqrt(2.0 / math.pi)

SHARDS = 32
ROWS = 64
FEATS = 3072
HID = 768
X, Y0, Y1, Z0, Z1 = 16, 4, 12, 1, 3
DIMS = (Z0, Y0, Z1, Y1, X)
WIDTHS = (512, 640, 640, 640, 640)
OFFSETS = tuple(int(v) for v in np.cumsum((0,) + WIDTHS)[:-1])
CHAINS = len(WIDTHS)
ORDERS = tuple(tuple(DIMS[(p + k) % 5] for k in range(5)) for p in range(CHAINS))
PARTS = (48, 16)
STARTS = (0, 48)


def mask_of(c):
    mask = 0
    for k in range(5):
        if c >> k & 1:
            mask ^= DIMS[k]
    return mask


def swap(x, mask):
    if mask >= 4:
        return lax.ppermute(x, "depth", [(i, i ^ (mask >> 2)) for i in range(8)])
    return lax.ppermute(x, "col", [(i, i ^ mask) for i in range(4)])


def swap_row(x, mask):
    return lax.ppermute(x, "row", [(i, i ^ mask) for i in range(4)])


def params(mib):
    return pltpu.CompilerParams(vmem_limit_bytes=mib * 1024 * 1024)


ANY = pl.BlockSpec(memory_space=pl.ANY)
VMEM = pl.BlockSpec(memory_space=pltpu.VMEM)
SMEM = pl.BlockSpec(memory_space=pltpu.SMEM)


def cut_kernel(where, grad_out, pre, *refs):
    outs, chunks, sem = refs[:CHAINS], refs[CHAINS:-1], refs[-1]
    row, col = where[0], where[1]
    copies = [
        pltpu.make_async_copy(grad_out.at[:, pl.ds(OFFSETS[p], WIDTHS[p])], outs[p].at[0], sem.at[p])
        for p in range(CHAINS)
    ]
    half = SHARDS * ROWS // 8
    for j, mask in enumerate((Z0, Z1, Z0 ^ Z1)):
        here = pre.at[
            pl.ds(pl.multiple_of(row % 2 * half, half), half), pl.ds(pl.multiple_of((col ^ mask) * HID, HID), HID)
        ]
        copies.append(pltpu.make_async_copy(here, chunks[j], sem.at[CHAINS + j]))
    for c in copies:
        c.start()
    for c in copies:
        c.wait()


def cut_call(where, grad_out, pre):
    return pl.pallas_call(
        cut_kernel,
        out_shape=[jax.ShapeDtypeStruct((1, ROWS, w), jnp.bfloat16) for w in WIDTHS]
        + [jax.ShapeDtypeStruct((SHARDS * ROWS // 8, HID), jnp.bfloat16)] * 3,
        in_specs=[SMEM, ANY, ANY],
        out_specs=[ANY] * (CHAINS + 3),
        scratch_shapes=[pltpu.SemaphoreType.DMA((CHAINS + 3,))],
        compiler_params=params(1),
        name="cut",
    )(where, grad_out, pre)


def grow_kernel(rows, *refs):
    own, got, sem = refs[:CHAINS], refs[CHAINS : 2 * CHAINS], refs[-1]
    outs = refs[2 * CHAINS : -1]
    copies = []
    for part, (at, n) in enumerate(rows):
        for p in range(CHAINS):
            out = outs[part * CHAINS + p]
            blocks = own[p].shape[0]
            for side, src in enumerate((own[p], got[p])):
                copies.append(
                    pltpu.make_async_copy(
                        src.at[:, pl.ds(at, n)], out.at[pl.ds(side * blocks, blocks)], sem.at[len(copies)]
                    )
                )
    for c in copies:
        c.start()
    for c in copies:
        c.wait()


def grow_call(own, got, rows=((0, ROWS),)):
    blocks = own[0].shape[0]
    return pl.pallas_call(
        functools.partial(grow_kernel, rows),
        out_shape=[jax.ShapeDtypeStruct((2 * blocks, n, w), jnp.bfloat16) for _, n in rows for w in WIDTHS],
        in_specs=[ANY] * (2 * CHAINS),
        out_specs=[ANY] * (len(rows) * CHAINS),
        scratch_shapes=[pltpu.SemaphoreType.DMA((2 * CHAINS * len(rows),))],
        compiler_params=params(1),
        name="grow",
    )(*own, *got)


def gelu_kernel(where, table, pre, got_a, got_b, got_c, other, *refs):
    outs, (buf, sems), acts = refs[:4], refs[4:6], refs[6:]
    act_t, slopes = outs[:2], outs[2:]
    row, col, mine = where[0], where[1], where[2]
    core = row % 2
    quarter, half = SHARDS * ROWS // 4, SHARDS * ROWS // 8
    copies = [
        pltpu.make_async_copy(
            pre.at[:, pl.ds(pl.multiple_of(col * HID, HID), HID)],
            buf.at[pl.ds(pl.multiple_of(col * quarter, quarter), quarter)],
            sems.at[0],
        )
    ]
    for j, (got, mask) in enumerate(((got_a, Z0), (got_b, Z1), (got_c, Z0 ^ Z1))):
        base = (col ^ mask) * quarter
        copies.append(
            pltpu.make_async_copy(
                got, buf.at[pl.ds(pl.multiple_of(base + core * half, half), half)], sems.at[1 + 2 * j]
            )
        )
        copies.append(
            pltpu.make_async_copy(
                other.at[pl.ds(j * half, half)],
                buf.at[pl.ds(pl.multiple_of(base + (1 - core) * half, half), half)],
                sems.at[2 + 2 * j],
            )
        )
    for c in copies:
        c.start()
    for c in copies:
        c.wait()

    def one_shard(s, carry):
        v = buf[pl.ds(pl.multiple_of((mine ^ table[s]) * ROWS, ROWS), ROWS), :].astype(jnp.float32)
        bend = jnp.tanh(gelu_const * (v + 0.044715 * v * v * v))
        a = (0.5 * v * (1.0 + bend)).astype(jnp.bfloat16)
        for part in range(2):
            n, at = PARTS[part], STARTS[part]
            acts[part][pl.ds(pl.multiple_of(s * n, 16), n), :] = a[at : at + n]
        return carry

    lax.fori_loop(0, SHARDS, one_shard, 0)

    def one_slope(s, carry):
        at_row = pl.multiple_of(row * quarter + s * ROWS, ROWS)
        v = buf[pl.ds(at_row, ROWS), :].astype(jnp.float32)
        bend = jnp.tanh(gelu_const * (v + 0.044715 * v * v * v))
        d = 0.5 * (1.0 + bend) + 0.5 * v * (1.0 - bend * bend) * gelu_const * (1.0 + 3.0 * 0.044715 * v * v)
        for part in range(2):
            n, at = PARTS[part], STARTS[part]
            slopes[part][s] = d[at : at + n]
        return carry

    lax.fori_loop(0, SHARDS // 4, one_slope, 0)

    for part in range(2):

        def one_turn(j, carry, part=part):
            at = pl.multiple_of(j * 128, 128)
            act_t[part][:, pl.ds(at, 128)] = acts[part][pl.ds(at, 128), :].T
            return carry

        lax.fori_loop(0, SHARDS * PARTS[part] // 128, one_turn, 0)


def gelu_call(where, table, pre, got, other):
    tokens = [SHARDS * n for n in PARTS]
    return pl.pallas_call(
        gelu_kernel,
        out_shape=[jax.ShapeDtypeStruct((HID, t), jnp.bfloat16) for t in tokens]
        + [jax.ShapeDtypeStruct((SHARDS // 4, n, HID), jnp.float32) for n in PARTS],
        in_specs=[SMEM, SMEM] + [ANY] * 5,
        out_specs=[VMEM] * 4,
        scratch_shapes=[pltpu.VMEM((SHARDS * ROWS, HID), jnp.bfloat16), pltpu.SemaphoreType.DMA((7,))]
        + [pltpu.VMEM((t, HID), jnp.bfloat16) for t in tokens],
        compiler_params=params(20),
        cost_estimate=pl.CostEstimate(flops=2048 * HID * 40, bytes_accessed=16 << 20, transcendentals=2048 * HID),
        name="gelu",
    )(where, table, pre, *got, other)


def pieces(p, side):
    every = slice(None)
    if p == 0:
        return [((every,) * 4, (side,) + (every,) * 4)]
    if p == 1:
        return [((every,) * 4, (every,) * 4 + (side,))]
    if p == 2:
        return [((i,) + (every,) * 3, (every,) * 3 + (side, i)) for i in range(2)]
    if p == 3:
        return [((every,) * 2 + (i, j), (i, j, side) + (every,) * 2) for i in range(2) for j in range(2)]
    return [((every,) * 3 + (i,), (i, side) + (every,) * 3) for i in range(2)]


def hidden_kernel(n, where, w, *refs):
    blocks = refs[: 2 * CHAINS]
    keep, send, gathered, g, in_sem, out_sem = refs[2 * CHAINS :]
    row, mine = where[0], where[2]
    per = SHARDS // 4
    for p in range(CHAINS):
        for side in range(2):
            for src, dst in pieces(p, side):
                pltpu.make_async_copy(
                    blocks[2 * p + side].at[src],
                    g.at[dst + (slice(None), pl.ds(OFFSETS[p], WIDTHS[p]))],
                    in_sem,
                ).start()
    pltpu.make_async_copy(g, g, in_sem).wait()
    out = pltpu.make_async_copy(g, gathered, out_sem)
    out.start()
    for a, b in ((1, 1), (0, 1), (1, 0), (0, 0)):
        off_x = (mine // 16) ^ (row // 2) ^ a
        off_y = (mine // 8 % 2) ^ (row % 2) ^ b
        lhs = g[off_x, off_y].reshape(per * n, FEATS)
        h = lax.dot_general(lhs, w[...], (((1,), (1,)), ((), ())), preferred_element_type=jnp.float32)
        for j in range(per):
            slot = (mine % 8) ^ (mask_of(j) % 8) ^ (off_y * 4)
            if b:
                send[a, slot] = h[j * n : (j + 1) * n].astype(jnp.bfloat16)
            else:
                keep[a, slot] = h[j * n : (j + 1) * n]
    out.wait()


def hidden_call(part, where, w, blocks):
    n = PARTS[part]
    per = SHARDS // 4
    return pl.pallas_call(
        functools.partial(hidden_kernel, n),
        out_shape=[
            jax.ShapeDtypeStruct((2, per, n, HID), jnp.float32),
            jax.ShapeDtypeStruct((2, per, n, HID), jnp.bfloat16),
            jax.ShapeDtypeStruct((2,) * 5 + (n, FEATS), jnp.bfloat16),
        ],
        in_specs=[SMEM, VMEM] + [ANY] * (2 * CHAINS),
        out_specs=[VMEM, VMEM, ANY],
        scratch_shapes=[
            pltpu.VMEM((2,) * 5 + (n, FEATS), jnp.bfloat16),
            pltpu.SemaphoreType.DMA,
            pltpu.SemaphoreType.DMA,
        ],
        compiler_params=params(10 + n // 3),
        cost_estimate=pl.CostEstimate(
            flops=2 * SHARDS * n * FEATS * HID, bytes_accessed=SHARDS * n * FEATS * 4, transcendentals=0
        ),
        name="hidden",
    )(where, w, *(b.reshape((2,) * 4 + b.shape[1:]) for b in blocks))


def down_kernel(at_a, at_b, g_a, g_b, *refs):
    out = refs[-1]
    acc = jnp.dot(at_a[...], g_a[...], preferred_element_type=jnp.float32)
    acc += jnp.dot(at_b[...], g_b[...], preferred_element_type=jnp.float32)
    out[...] = acc.astype(jnp.bfloat16)


def down_call(acts, gathered, first, count, base=None):
    wide = 512
    tokens = [SHARDS * n for n in PARTS]
    in_specs = [pl.BlockSpec((HID, t), lambda j: (0, 0)) for t in tokens]
    in_specs += [pl.BlockSpec((t, wide), lambda j: (0, j + first)) for t in tokens]
    args = [*acts, *(g.reshape(t, FEATS) for g, t in zip(gathered, tokens))]
    aliases = {}
    if base is not None:
        in_specs.append(ANY)
        args.append(base)
        aliases = {4: 0}
    return pl.pallas_call(
        down_kernel,
        grid=(count,),
        out_shape=jax.ShapeDtypeStruct((HID, FEATS), jnp.bfloat16),
        in_specs=in_specs,
        out_specs=pl.BlockSpec((HID, wide), lambda j: (0, j + first)),
        input_output_aliases=aliases,
        compiler_params=params(24),
        cost_estimate=pl.CostEstimate(
            flops=2 * 2048 * HID * wide * count, bytes_accessed=count * wide * 2 * (2048 + HID), transcendentals=0
        ),
        name="down",
    )(*args)


def local(grad_out, pre_act, w_down):
    depth, row, col = (lax.axis_index(a) for a in ("depth", "row", "col"))
    where = jnp.stack([row, col, depth * 4 + col]).astype(jnp.int32)
    table = jnp.asarray([mask_of(c) for c in range(SHARDS)], jnp.int32)

    cuts = cut_call(where, grad_out, pre_act)
    blocks, chunks = cuts[:CHAINS], cuts[CHAINS:]
    fetched = [swap(chunk, mask) for chunk, mask in zip(chunks, (Z0, Z1, Z0 ^ Z1))]
    for k in range(3):
        got = [swap(blocks[p], ORDERS[p][k]) for p in range(CHAINS)]
        blocks = grow_call(blocks, got)
    got = [swap(blocks[p], ORDERS[p][3]) for p in range(CHAINS)]
    grown = grow_call(blocks, got, tuple(zip(STARTS, PARTS)))
    own = grown[:CHAINS], grown[CHAINS:]
    came = [[swap(own[part][p], ORDERS[p][4]) for p in range(CHAINS)] for part in range(2)]

    other = swap_row(jnp.concatenate(fetched, 0), 1)
    act_a, act_b, slope_a, slope_b = gelu_call(where, table, pre_act, fetched, other)
    came[0][0], act_a = lax.optimization_barrier((came[0][0], act_a))

    done, gathered = [], []
    for part in range(2):
        pairs = [b for p in range(CHAINS) for b in (own[part][p], came[part][p])]
        keep, send, g = hidden_call(part, where, w_down, pairs)
        gathered.append(g)
        total = keep + swap_row(send, 1).astype(jnp.float32)
        far = swap_row(total[1].astype(jnp.bfloat16), 2)
        done.append((total[0], far))
    grad_down = down_call((act_a, act_b), gathered, 0, 2)
    grad_down = down_call((act_a, act_b), gathered, 2, 4, grad_down)
    parts = [
        ((mine + far.astype(jnp.float32)) * slope).astype(jnp.bfloat16)
        for (mine, far), slope in zip(done, (slope_a, slope_b))
    ]
    grad_pre = jnp.concatenate(parts, 1).reshape(512, HID)
    return (grad_pre, grad_down)


def solution(mesh):
    placed = (P(("depth", "col"), "row"), P("col", "depth"), P(("depth", "col"), "row"))
    return jax.shard_map(
        local,
        mesh=mesh,
        in_specs=placed,
        out_specs=(P("row", ("depth", "col")), P(("depth", "col"), "row")),
        check_vma=False,
    )
```

```python
import functools
import math

import jax
import jax.numpy as jnp
import numpy as np
from jax import lax
from jax.experimental import pallas as pl
from jax.experimental.pallas import tpu as pltpu
from jax.sharding import PartitionSpec as P

gelu_const = math.sqrt(2.0 / math.pi)

SHARDS = 32
ROWS = 64
FEATS = 3072
HID = 768
X, Y0, Y1, Z0, Z1 = 16, 4, 12, 1, 3
DIMS = (Z0, Y0, Z1, Y1, X)
WIDTHS = (512, 640, 640, 640, 640)
OFFSETS = tuple(int(v) for v in np.cumsum((0,) + WIDTHS)[:-1])
CHAINS = len(WIDTHS)
ORDERS = tuple(tuple(DIMS[(p + k) % 5] for k in range(5)) for p in range(CHAINS))
PARTS = (32, 32)
STARTS = (0, 32)


def mask_of(c):
    mask = 0
    for k in range(5):
        if c >> k & 1:
            mask ^= DIMS[k]
    return mask


def swap(x, mask):
    if mask >= 4:
        return lax.ppermute(x, "depth", [(i, i ^ (mask >> 2)) for i in range(8)])
    return lax.ppermute(x, "col", [(i, i ^ mask) for i in range(4)])


def swap_row(x, mask):
    return lax.ppermute(x, "row", [(i, i ^ mask) for i in range(4)])


def in_hbm(x):
    return pltpu.with_memory_space_constraint(x, pltpu.HBM)


def params(mib):
    return pltpu.CompilerParams(vmem_limit_bytes=mib * 1024 * 1024)


TINY = pl.CostEstimate(flops=1, bytes_accessed=1, transcendentals=0)
ANY = pl.BlockSpec(memory_space=pl.ANY)
VMEM = pl.BlockSpec(memory_space=pltpu.VMEM)
SMEM = pl.BlockSpec(memory_space=pltpu.SMEM)


def cut_kernel(where, grad_out, pre, *refs):
    outs, chunks, sem = refs[:CHAINS], refs[CHAINS], refs[-1]
    row = where[0]
    copies = [
        pltpu.make_async_copy(grad_out.at[:, pl.ds(OFFSETS[p], WIDTHS[p])], outs[p].at[0], sem.at[p])
        for p in range(CHAINS)
    ]
    half = SHARDS * ROWS // 8
    for z in range(4):
        here = pre.at[pl.ds(pl.multiple_of(row % 2 * half, half), half), pl.ds(z * HID, HID)]
        copies.append(pltpu.make_async_copy(here, chunks.at[z], sem.at[CHAINS + z]))
    for c in copies:
        c.start()
    for c in copies:
        c.wait()


def cut_call(where, grad_out, pre):
    return pl.pallas_call(
        cut_kernel,
        out_shape=[jax.ShapeDtypeStruct((1, ROWS, w), jnp.bfloat16) for w in WIDTHS]
        + [jax.ShapeDtypeStruct((4, SHARDS * ROWS // 8, HID), jnp.bfloat16)],
        in_specs=[SMEM, ANY, ANY],
        out_specs=[ANY] * (CHAINS + 1),
        scratch_shapes=[pltpu.SemaphoreType.DMA((CHAINS + 4,))],
        compiler_params=params(1),
        cost_estimate=TINY,
        name="cut",
    )(where, in_hbm(grad_out), in_hbm(pre))


def grow_kernel(rows, *refs):
    own, got, sem = refs[:CHAINS], refs[CHAINS : 2 * CHAINS], refs[-1]
    outs = refs[-1 - len(rows) * CHAINS : -1]
    copies = []
    for part, (at, n) in enumerate(rows):
        for p in range(CHAINS):
            out = outs[part * CHAINS + p]
            blocks = own[p].shape[0]
            for side, src in enumerate((own[p], got[p])):
                copies.append((src.at[:, pl.ds(at, n)], out.at[pl.ds(side * blocks, blocks)]))
    copies = [pltpu.make_async_copy(*c, sem.at[i]) for i, c in enumerate(copies)]
    for c in copies:
        c.start()
    for c in copies:
        c.wait()


def grow_call(own, got, rows=((0, ROWS),), after=()):
    blocks = own[0].shape[0]
    shape = pltpu.HBM if len(rows) > 1 else jax.ShapeDtypeStruct
    return pl.pallas_call(
        functools.partial(grow_kernel, rows),
        out_shape=[shape((2 * blocks, n, w), jnp.bfloat16) for _, n in rows for w in WIDTHS],
        in_specs=[ANY] * (2 * CHAINS + len(after)),
        out_specs=[ANY] * (len(rows) * CHAINS),
        scratch_shapes=[pltpu.SemaphoreType.DMA((2 * CHAINS * len(rows),))],
        compiler_params=params(1),
        cost_estimate=TINY,
        name="grow",
    )(*own, *got, *after)


def gelu_kernel(where, table, fetched, other, *refs):
    outs, (buf, sems), acts = refs[:4], refs[4:6], refs[6:]
    act_t, slopes = outs[:2], outs[2:]
    row, mine = where[0], where[2]
    core = row % 2
    quarter, half = SHARDS * ROWS // 4, SHARDS * ROWS // 8
    copies = []
    for z in range(4):
        for side, src in ((core, fetched), (1 - core, other)):
            at = pl.multiple_of(z * quarter + side * half, half)
            copies.append(pltpu.make_async_copy(src.at[z], buf.at[pl.ds(at, half)], sems.at[len(copies)]))
    for c in copies:
        c.start()
    for c in copies:
        c.wait()

    def one_shard(s, carry):
        v = buf[pl.ds(pl.multiple_of((mine ^ table[s]) * ROWS, ROWS), ROWS), :].astype(jnp.float32)
        bend = jnp.tanh(gelu_const * (v + 0.044715 * v * v * v))
        a = (0.5 * v * (1.0 + bend)).astype(jnp.bfloat16)
        for part in range(2):
            n, at = PARTS[part], STARTS[part]
            acts[part][pl.ds(pl.multiple_of(s * n, 16), n), :] = a[at : at + n]
        return carry

    lax.fori_loop(0, SHARDS, one_shard, 0)

    def one_slope(s, carry):
        at_row = pl.multiple_of(row * quarter + s * ROWS, ROWS)
        v = buf[pl.ds(at_row, ROWS), :].astype(jnp.float32)
        bend = jnp.tanh(gelu_const * (v + 0.044715 * v * v * v))
        d = 0.5 * (1.0 + bend) + 0.5 * v * (1.0 - bend * bend) * gelu_const * (1.0 + 3.0 * 0.044715 * v * v)
        for part in range(2):
            n, at = PARTS[part], STARTS[part]
            slopes[part][s] = d[at : at + n]
        return carry

    lax.fori_loop(0, SHARDS // 4, one_slope, 0)

    for part in range(2):

        def one_turn(j, carry, part=part):
            at = pl.multiple_of(j * 128, 128)
            act_t[part][:, pl.ds(at, 128)] = acts[part][pl.ds(at, 128), :].T
            return carry

        lax.fori_loop(0, SHARDS * PARTS[part] // 128, one_turn, 0)


def gelu_call(where, table, fetched, other):
    tokens = [SHARDS * n for n in PARTS]
    return pl.pallas_call(
        gelu_kernel,
        out_shape=[jax.ShapeDtypeStruct((HID, t), jnp.bfloat16) for t in tokens]
        + [jax.ShapeDtypeStruct((SHARDS // 4, n, HID), jnp.float32) for n in PARTS],
        in_specs=[SMEM, SMEM, ANY, ANY],
        out_specs=[VMEM] * 4,
        scratch_shapes=[pltpu.VMEM((SHARDS * ROWS, HID), jnp.bfloat16), pltpu.SemaphoreType.DMA((8,))]
        + [pltpu.VMEM((t, HID), jnp.bfloat16) for t in tokens],
        compiler_params=params(20),
        cost_estimate=TINY,
        name="gelu",
    )(where, table, fetched, other)


def pieces(p, side):
    every = slice(None)
    if p == 0:
        return [((every,) * 4, (side,) + (every,) * 4)]
    if p == 1:
        return [((every,) * 4, (every,) * 4 + (side,))]
    if p == 2:
        return [((i,) + (every,) * 3, (every,) * 3 + (side, i)) for i in range(2)]
    if p == 3:
        return [((every,) * 2 + (i, j), (i, j, side) + (every,) * 2) for i in range(2) for j in range(2)]
    return [((every,) * 3 + (i,), (i, side) + (every,) * 3) for i in range(2)]


def hidden_kernel(n, where, w_far, *refs):
    blocks = refs[: 2 * CHAINS]
    keep, send, gathered, g, w, hs, sems = refs[-7:]
    row, mine = where[0], where[2]
    per = SHARDS // 4
    weights = pltpu.make_async_copy(w_far, w, sems.at[0])
    weights.start()
    for p in range(CHAINS):
        for side in range(2):
            for src, dst in pieces(p, side):
                pltpu.make_async_copy(
                    blocks[2 * p + side].at[src],
                    g.at[dst + (slice(None), pl.ds(OFFSETS[p], WIDTHS[p]))],
                    sems.at[1],
                ).start()
    pltpu.make_async_copy(g, g, sems.at[1]).wait()
    weights.wait()
    out = pltpu.make_async_copy(g, gathered, sems.at[2])
    out.start()
    for i in range(2):
        h = lax.dot_general(
            g[i].reshape(2 * per * n, FEATS), w[...], (((1,), (1,)), ((), ())), preferred_element_type=jnp.float32
        )
        hs[i] = h.reshape(2, per, n, HID)
    for a, b in ((1, 1), (0, 1), (1, 0), (0, 0)):
        off_x = (mine // 16) ^ (row // 2) ^ a
        off_y = (mine // 8 % 2) ^ (row % 2) ^ b
        for j in range(per):
            slot = (mine % 8) ^ (mask_of(j) % 8) ^ (off_y * 4)
            if b:
                send[a, slot] = hs[off_x, off_y, j].astype(jnp.bfloat16)
            else:
                keep[a, slot] = hs[off_x, off_y, j]
    out.wait()


def hidden_call(part, where, w, blocks, after=()):
    n = PARTS[part]
    per = SHARDS // 4
    return pl.pallas_call(
        functools.partial(hidden_kernel, n),
        out_shape=[
            jax.ShapeDtypeStruct((2, per, n, HID), jnp.float32),
            jax.ShapeDtypeStruct((2, per, n, HID), jnp.bfloat16),
            pltpu.HBM((2,) * 5 + (n, FEATS), jnp.bfloat16),
        ],
        in_specs=[SMEM] + [ANY] * (1 + 2 * CHAINS + len(after)),
        out_specs=[VMEM, VMEM, ANY],
        scratch_shapes=[
            pltpu.VMEM((2,) * 5 + (n, FEATS), jnp.bfloat16),
            pltpu.VMEM((HID, FEATS), jnp.bfloat16),
            pltpu.VMEM((2, 2, per, n, HID), jnp.float32),
            pltpu.SemaphoreType.DMA((3,)),
        ],
        compiler_params=params(14 + n // 2),
        cost_estimate=pl.CostEstimate(
            flops=2 * SHARDS * n * FEATS * HID, bytes_accessed=SHARDS * n * FEATS * 4, transcendentals=0
        ),
        name="hidden",
    )(where, w, *(f(b.reshape((2,) * 4 + b.shape[1:])) for b, f in zip(blocks, (in_hbm, lambda x: x) * CHAINS)), *after)


def total_kernel(keep, got, *refs):
    mine, far = refs[-2:]
    mine[...] = keep[0] + got[0].astype(jnp.float32)
    far[...] = (keep[1] + got[1].astype(jnp.float32)).astype(jnp.bfloat16)


def total_call(keep, got, after=()):
    return pl.pallas_call(
        total_kernel,
        out_shape=[
            jax.ShapeDtypeStruct(keep.shape[1:], jnp.float32),
            jax.ShapeDtypeStruct(keep.shape[1:], jnp.bfloat16),
        ],
        in_specs=[VMEM, VMEM] + [ANY] * len(after),
        out_specs=[VMEM, VMEM],
        compiler_params=params(8),
        cost_estimate=TINY,
        name="total",
    )(keep, got, *after)


def down_kernel(at_a, at_b, g_a, g_b, *refs):
    out = refs[-1]
    acc = jnp.dot(at_a[...], g_a[...], preferred_element_type=jnp.float32)
    acc += jnp.dot(at_b[...], g_b[...], preferred_element_type=jnp.float32)
    out[...] = acc.astype(jnp.bfloat16)


def down_call(acts, gathered, first, count, base=None):
    wide = 512
    tokens = [SHARDS * n for n in PARTS]
    in_specs = [pl.BlockSpec((HID, t), lambda j: (0, 0)) for t in tokens]
    in_specs += [pl.BlockSpec((t, wide), lambda j: (0, j + first)) for t in tokens]
    args = [*acts, *(in_hbm(g.reshape(t, FEATS)) for g, t in zip(gathered, tokens))]
    aliases = {}
    if base is not None:
        in_specs.append(ANY)
        args.append(in_hbm(base))
        aliases = {4: 0}
    return pl.pallas_call(
        down_kernel,
        grid=(count,),
        out_shape=pltpu.HBM((HID, FEATS), jnp.bfloat16),
        in_specs=in_specs,
        out_specs=pl.BlockSpec((HID, wide), lambda j: (0, j + first)),
        input_output_aliases=aliases,
        compiler_params=params(24),
        cost_estimate=pl.CostEstimate(
            flops=2 * 2048 * HID * wide * count, bytes_accessed=count * wide * 2 * (2048 + HID), transcendentals=0
        ),
        name="down",
    )(*args)


def local(grad_out, pre_act, w_down):
    depth, row, col = (lax.axis_index(a) for a in ("depth", "row", "col"))
    where = jnp.stack([row, col, depth * 4 + col]).astype(jnp.int32)
    table = jnp.asarray([mask_of(c) for c in range(SHARDS)], jnp.int32)

    *blocks, chunks = cut_call(where, grad_out, pre_act)
    fetched = lax.all_to_all(chunks, "col", split_axis=0, concat_axis=0, tiled=True)
    got = [swap(blocks[p], ORDERS[p][0]) for p in range(CHAINS)]
    blocks = grow_call(blocks, got)
    got = [swap(blocks[p], ORDERS[p][1]) for p in range(CHAINS)]
    blocks = grow_call(blocks, got, after=(fetched,))
    got = [swap(blocks[p], ORDERS[p][2]) for p in range(CHAINS)]
    other = swap_row(fetched, 1)
    blocks = grow_call(blocks, got, after=(other,))
    got = [swap(blocks[p], ORDERS[p][3]) for p in range(CHAINS)]
    act_a, act_b, slope_a, slope_b = gelu_call(where, table, fetched, other)
    grown = grow_call(blocks, got, tuple(zip(STARTS, PARTS)), after=(slope_a,))
    own = grown[:CHAINS], grown[CHAINS:]
    came = [[swap(own[part][p], ORDERS[p][4]) for p in range(CHAINS)] for part in range(2)]

    pairs = [[b for p in range(CHAINS) for b in (own[part][p], came[part][p])] for part in range(2)]
    keep_a, send_a, g_a = hidden_call(0, where, w_down, pairs[0])
    keep_b, send_b, g_b = hidden_call(1, where, w_down, pairs[1], after=(keep_a,))
    mine_a, far_a = total_call(keep_a, swap_row(send_a, 1), after=(keep_b,))
    far_a = swap_row(far_a, 2)
    grad_down = down_call((act_a, act_b), (g_a, g_b), 0, 2)
    mine_b, far_b = total_call(keep_b, swap_row(send_b, 1), after=(in_hbm(grad_down),))
    far_b = swap_row(far_b, 2)
    grad_down = down_call((act_a, act_b), (g_a, g_b), 2, 4, grad_down)
    done = (mine_a, far_a), (mine_b, far_b)
    parts = [
        ((mine + far.astype(jnp.float32)) * slope).astype(jnp.bfloat16)
        for (mine, far), slope in zip(done, (slope_a, slope_b))
    ]
    grad_pre = jnp.concatenate(parts, 1).reshape(512, HID)
    return (grad_pre, grad_down)


def solution(mesh):
    placed = (P(("depth", "col"), "row"), P("col", "depth"), P(("depth", "col"), "row"))
    return jax.shard_map(
        local,
        mesh=mesh,
        in_specs=placed,
        out_specs=(P("row", ("depth", "col")), P(("depth", "col"), "row")),
        check_vma=False,
    )
```

```python
import functools
import math

import jax
import jax.numpy as jnp
import numpy as np
from jax import lax
from jax.experimental import pallas as pl
from jax.experimental.pallas import tpu as pltpu
from jax.sharding import PartitionSpec as P

gelu_const = math.sqrt(2.0 / math.pi)

SHARDS = 32
ROWS = 64
FEATS = 3072
HID = 768
X, Y0, Y1, Z0, Z1 = 16, 4, 12, 1, 3
DIMS = (Z0, Y0, Z1, Y1, X)
WIDTHS = (512, 640, 640, 640, 640)
OFFSETS = tuple(int(v) for v in np.cumsum((0,) + WIDTHS)[:-1])
CHAINS = len(WIDTHS)
HOPS = (Z0, Z1, Z0 ^ Z1)
ORDERS = tuple(tuple(DIMS[(p + k) % 5] for k in range(5)) for p in range(CHAINS))
TIED = 4
PARTS = (32, 32)
STARTS = (0, 32)


def mask_of(c):
    mask = 0
    for k in range(5):
        if c >> k & 1:
            mask ^= DIMS[k]
    return mask


def swap(x, mask):
    if mask >= 4:
        return lax.ppermute(x, "depth", [(i, i ^ (mask >> 2)) for i in range(8)])
    return lax.ppermute(x, "col", [(i, i ^ mask) for i in range(4)])


def swap_row(x, mask):
    return lax.ppermute(x, "row", [(i, i ^ mask) for i in range(4)])


def in_hbm(x):
    return pltpu.with_memory_space_constraint(x, pltpu.HBM)


def params(mib):
    return pltpu.CompilerParams(vmem_limit_bytes=mib * 1024 * 1024)


TINY = pl.CostEstimate(flops=1, bytes_accessed=1, transcendentals=0)
ANY = pl.BlockSpec(memory_space=pl.ANY)
VMEM = pl.BlockSpec(memory_space=pltpu.VMEM)
SMEM = pl.BlockSpec(memory_space=pltpu.SMEM)


def cut_kernel(where, grad_out, pre, *refs):
    outs, chunks, sem = refs[:CHAINS], refs[CHAINS:-1], refs[-1]
    row, col = where[0], where[1]
    copies = [
        pltpu.make_async_copy(grad_out.at[:, pl.ds(OFFSETS[p], WIDTHS[p])], outs[p].at[0], sem.at[p])
        for p in range(CHAINS)
    ]
    half = SHARDS * ROWS // 8
    for j, mask in enumerate(HOPS):
        here = pre.at[
            pl.ds(pl.multiple_of(row % 2 * half, half), half), pl.ds(pl.multiple_of((col ^ mask) * HID, HID), HID)
        ]
        copies.append(pltpu.make_async_copy(here, chunks[j], sem.at[CHAINS + j]))
    for c in copies:
        c.start()
    for c in copies:
        c.wait()


def cut_call(where, grad_out, pre):
    return pl.pallas_call(
        cut_kernel,
        out_shape=[jax.ShapeDtypeStruct((1, ROWS, w), jnp.bfloat16) for w in WIDTHS]
        + [jax.ShapeDtypeStruct((SHARDS * ROWS // 8, HID), jnp.bfloat16)] * len(HOPS),
        in_specs=[SMEM, ANY, ANY],
        out_specs=[ANY] * (CHAINS + len(HOPS)),
        scratch_shapes=[pltpu.SemaphoreType.DMA((CHAINS + len(HOPS),))],
        compiler_params=params(1),
        cost_estimate=TINY,
        name="cut",
    )(where, in_hbm(grad_out), in_hbm(pre))


def grow_kernel(rows, own, got, *refs):
    outs, sem = refs[-1 - len(rows) : -1], refs[-1]
    blocks = own.shape[0]
    copies = []
    for out, (at, n) in zip(outs, rows):
        for side, src in enumerate((own, got)):
            copies.append(
                pltpu.make_async_copy(
                    src.at[:, pl.ds(at, n)], out.at[pl.ds(side * blocks, blocks)], sem.at[len(copies)]
                )
            )
    for c in copies:
        c.start()
    for c in copies:
        c.wait()


def grow_call(own, got, rows=((0, ROWS),), after=()):
    blocks, _, w = own.shape
    shape = pltpu.HBM if len(rows) > 1 else jax.ShapeDtypeStruct
    return pl.pallas_call(
        functools.partial(grow_kernel, rows),
        out_shape=[shape((2 * blocks, n, w), jnp.bfloat16) for _, n in rows],
        in_specs=[ANY] * (2 + len(after)),
        out_specs=[ANY] * len(rows),
        scratch_shapes=[pltpu.SemaphoreType.DMA((2 * len(rows),))],
        compiler_params=params(1),
        cost_estimate=TINY,
        name="grow",
    )(own, got, *after)


def gelu_kernel(where, table, pre, got_a, got_b, got_c, other, *refs):
    outs, (buf, sems), acts = refs[:4], refs[4:6], refs[6:]
    act_t, slopes = outs[:2], outs[2:]
    row, col, mine = where[0], where[1], where[2]
    core = row % 2
    quarter, half = SHARDS * ROWS // 4, SHARDS * ROWS // 8
    copies = [
        pltpu.make_async_copy(
            pre.at[:, pl.ds(pl.multiple_of(col * HID, HID), HID)],
            buf.at[pl.ds(pl.multiple_of(col * quarter, quarter), quarter)],
            sems.at[0],
        )
    ]
    for j, got in enumerate((got_a, got_b, got_c)):
        for side, src in ((core, got), (1 - core, other.at[pl.ds(j * half, half)])):
            at = pl.multiple_of((col ^ HOPS[j]) * quarter + side * half, half)
            copies.append(pltpu.make_async_copy(src, buf.at[pl.ds(at, half)], sems.at[len(copies)]))
    for c in copies:
        c.start()
    for c in copies:
        c.wait()

    def one_shard(s, carry):
        v = buf[pl.ds(pl.multiple_of((mine ^ table[s]) * ROWS, ROWS), ROWS), :].astype(jnp.float32)
        bend = jnp.tanh(gelu_const * (v + 0.044715 * v * v * v))
        a = (0.5 * v * (1.0 + bend)).astype(jnp.bfloat16)
        for part in range(2):
            n, at = PARTS[part], STARTS[part]
            acts[part][pl.ds(pl.multiple_of(s * n, 16), n), :] = a[at : at + n]
        return carry

    lax.fori_loop(0, SHARDS, one_shard, 0)

    def one_slope(s, carry):
        at_row = pl.multiple_of(row * quarter + s * ROWS, ROWS)
        v = buf[pl.ds(at_row, ROWS), :].astype(jnp.float32)
        bend = jnp.tanh(gelu_const * (v + 0.044715 * v * v * v))
        d = 0.5 * (1.0 + bend) + 0.5 * v * (1.0 - bend * bend) * gelu_const * (1.0 + 3.0 * 0.044715 * v * v)
        for part in range(2):
            n, at = PARTS[part], STARTS[part]
            slopes[part][s] = d[at : at + n]
        return carry

    lax.fori_loop(0, SHARDS // 4, one_slope, 0)

    for part in range(2):

        def one_turn(j, carry, part=part):
            at = pl.multiple_of(j * 128, 128)
            act_t[part][:, pl.ds(at, 128)] = acts[part][pl.ds(at, 128), :].T
            return carry

        lax.fori_loop(0, SHARDS * PARTS[part] // 128, one_turn, 0)


def gelu_call(where, table, pre, fetched, other):
    tokens = [SHARDS * n for n in PARTS]
    return pl.pallas_call(
        gelu_kernel,
        out_shape=[jax.ShapeDtypeStruct((HID, t), jnp.bfloat16) for t in tokens]
        + [jax.ShapeDtypeStruct((SHARDS // 4, n, HID), jnp.float32) for n in PARTS],
        in_specs=[SMEM, SMEM] + [ANY] * 5,
        out_specs=[VMEM] * 4,
        scratch_shapes=[pltpu.VMEM((SHARDS * ROWS, HID), jnp.bfloat16), pltpu.SemaphoreType.DMA((7,))]
        + [pltpu.VMEM((t, HID), jnp.bfloat16) for t in tokens],
        compiler_params=params(20),
        cost_estimate=TINY,
        name="gelu",
    )(where, table, in_hbm(pre), *fetched, other)


def pieces(p, side, top):
    every = slice(None)
    if p == 0:
        return [((every,) * 4, (side,) + (every,) * 4)] if side == top else []
    if p == 1:
        return [((top,) + (every,) * 3, (top,) + (every,) * 3 + (side,))]
    if p == 2:
        return [((i, top) + (every,) * 2, (top,) + (every,) * 2 + (side, i)) for i in range(2)]
    if p == 3:
        return [((every,) * 2 + (top, j), (top, j, side) + (every,) * 2) for j in range(2)]
    return [((every,) * 3 + (top,), (top, side) + (every,) * 3)]


def hidden_kernel(n, where, w_far, *refs):
    blocks = refs[: 2 * CHAINS]
    keep, send, gathered, g, w, hs, sems = refs[-7:]
    row, mine = where[0], where[2]
    per = SHARDS // 4
    step = HID // 3
    weights = [
        pltpu.make_async_copy(w_far.at[pl.ds(k * step, step)], w.at[pl.ds(k * step, step)], sems.at[3 + k])
        for k in range(3)
    ]
    for top in range(2):
        for p in range(CHAINS):
            for side in range(2):
                for src, dst in pieces(p, side, top):
                    pltpu.make_async_copy(
                        blocks[2 * p + side].at[src],
                        g.at[dst + (slice(None), pl.ds(OFFSETS[p], WIDTHS[p]))],
                        sems.at[top],
                    ).start()
        if top == 0:
            for c in weights:
                c.start()
    outs = []
    for i in range(2):
        pltpu.make_async_copy(g.at[i], g.at[i], sems.at[i]).wait()
        outs.append(pltpu.make_async_copy(g.at[i], gathered.at[i], sems.at[2 if i else 6]))
        outs[-1].start()
        for k in range(3):
            if i == 0:
                weights[k].wait()
            h = lax.dot_general(
                g[i].reshape(2 * per * n, FEATS),
                w[k * step : (k + 1) * step, :],
                (((1,), (1,)), ((), ())),
                preferred_element_type=jnp.float32,
            )
            hs[i, :, :, :, k * step : (k + 1) * step] = h.reshape(2, per, n, step)
    for a, b in ((1, 1), (0, 1), (1, 0), (0, 0)):
        off_x = (mine // 16) ^ (row // 2) ^ a
        off_y = (mine // 8 % 2) ^ (row % 2) ^ b
        for j in range(per):
            slot = (mine % 8) ^ (mask_of(j) % 8) ^ (off_y * 4)
            if b:
                send[a, slot] = hs[off_x, off_y, j].astype(jnp.bfloat16)
            else:
                keep[a, slot] = hs[off_x, off_y, j]
    for out in outs:
        out.wait()


def hidden_call(part, where, w, blocks, after=()):
    n = PARTS[part]
    per = SHARDS // 4
    return pl.pallas_call(
        functools.partial(hidden_kernel, n),
        out_shape=[
            jax.ShapeDtypeStruct((2, per, n, HID), jnp.float32),
            jax.ShapeDtypeStruct((2, per, n, HID), jnp.bfloat16),
            pltpu.HBM((2,) * 5 + (n, FEATS), jnp.bfloat16),
        ],
        in_specs=[SMEM] + [ANY] * (1 + 2 * CHAINS + len(after)),
        out_specs=[VMEM, VMEM, ANY],
        scratch_shapes=[
            pltpu.VMEM((2,) * 5 + (n, FEATS), jnp.bfloat16),
            pltpu.VMEM((HID, FEATS), jnp.bfloat16),
            pltpu.VMEM((2, 2, per, n, HID), jnp.float32),
            pltpu.SemaphoreType.DMA((7,)),
        ],
        compiler_params=params(14 + n // 2),
        cost_estimate=pl.CostEstimate(
            flops=2 * SHARDS * n * FEATS * HID, bytes_accessed=SHARDS * n * FEATS * 4, transcendentals=0
        ),
        name="hidden",
    )(where, w, *(f(b.reshape((2,) * 4 + b.shape[1:])) for b, f in zip(blocks, (in_hbm, lambda x: x) * CHAINS)), *after)


def total_kernel(keep, got, *refs):
    mine, far = refs[-2:]
    mine[...] = keep[0] + got[0].astype(jnp.float32)
    far[...] = (keep[1] + got[1].astype(jnp.float32)).astype(jnp.bfloat16)


def total_call(keep, got, after=()):
    return pl.pallas_call(
        total_kernel,
        out_shape=[
            jax.ShapeDtypeStruct(keep.shape[1:], jnp.float32),
            jax.ShapeDtypeStruct(keep.shape[1:], jnp.bfloat16),
        ],
        in_specs=[VMEM, VMEM] + [ANY] * len(after),
        out_specs=[VMEM, VMEM],
        compiler_params=params(8),
        cost_estimate=TINY,
        name="total",
    )(keep, got, *after)


def down_kernel(at_a, at_b, g_a, g_b, *refs):
    out = refs[-1]
    acc = jnp.dot(at_a[...], g_a[...], preferred_element_type=jnp.float32)
    acc += jnp.dot(at_b[...], g_b[...], preferred_element_type=jnp.float32)
    out[...] = acc.astype(jnp.bfloat16)


def down_call(acts, gathered, first, count, base=None):
    wide = 512
    tokens = [SHARDS * n for n in PARTS]
    in_specs = [pl.BlockSpec((HID, t), lambda j: (0, 0)) for t in tokens]
    in_specs += [pl.BlockSpec((t, wide), lambda j: (0, j + first)) for t in tokens]
    args = [*acts, *(in_hbm(g.reshape(t, FEATS)) for g, t in zip(gathered, tokens))]
    aliases = {}
    if base is not None:
        in_specs.append(ANY)
        args.append(in_hbm(base))
        aliases = {4: 0}
    return pl.pallas_call(
        down_kernel,
        grid=(count,),
        out_shape=pltpu.HBM((HID, FEATS), jnp.bfloat16),
        in_specs=in_specs,
        out_specs=pl.BlockSpec((HID, wide), lambda j: (0, j + first)),
        input_output_aliases=aliases,
        compiler_params=params(24),
        cost_estimate=pl.CostEstimate(
            flops=2 * 2048 * HID * wide * count, bytes_accessed=count * wide * 2 * (2048 + HID), transcendentals=0
        ),
        name="down",
    )(*args)


def local(grad_out, pre_act, w_down):
    depth, row, col = (lax.axis_index(a) for a in ("depth", "row", "col"))
    where = jnp.stack([row, col, depth * 4 + col]).astype(jnp.int32)
    table = jnp.asarray([mask_of(c) for c in range(SHARDS)], jnp.int32)

    cuts = cut_call(where, grad_out, pre_act)
    blocks, chunks = cuts[:CHAINS], cuts[CHAINS:]
    fetched = []
    for k in range(3):
        got = [swap(blocks[p], ORDERS[p][k]) for p in range(CHAINS)]
        fetched.append(swap(chunks[k], HOPS[k]))
        blocks = [
            grow_call(b, r, after=(fetched[k],))[0] if p == TIED else jnp.concatenate([b, r], 0)
            for p, (b, r) in enumerate(zip(blocks, got))
        ]
    got = [swap(blocks[p], ORDERS[p][3]) for p in range(CHAINS)]
    other = swap_row(jnp.concatenate(fetched, 0), 1)
    grown = [
        grow_call(b, r, tuple(zip(STARTS, PARTS)), after=(other,) if p == TIED else ())
        for p, (b, r) in enumerate(zip(blocks, got))
    ]
    own = [[grown[p][part] for p in range(CHAINS)] for part in range(2)]
    came = [[swap(own[part][p], ORDERS[p][4]) for p in range(CHAINS)] for part in range(2)]
    act_a, act_b, slope_a, slope_b = gelu_call(where, table, pre_act, fetched, other)

    pairs = [[b for p in range(CHAINS) for b in (own[part][p], came[part][p])] for part in range(2)]
    keep_a, send_a, g_a = hidden_call(0, where, w_down, pairs[0], after=(slope_a,))
    keep_b, send_b, g_b = hidden_call(1, where, w_down, pairs[1], after=(keep_a,))
    mine_a, far_a = total_call(keep_a, swap_row(send_a, 1), after=(keep_b,))
    far_a = swap_row(far_a, 2)
    grad_down = down_call((act_a, act_b), (g_a, g_b), 0, 2)
    mine_b, far_b = total_call(keep_b, swap_row(send_b, 1), after=(in_hbm(grad_down),))
    far_b = swap_row(far_b, 2)
    grad_down = down_call((act_a, act_b), (g_a, g_b), 2, 4, grad_down)
    done = (mine_a, far_a), (mine_b, far_b)
    parts = [
        ((mine + far.astype(jnp.float32)) * slope).astype(jnp.bfloat16)
        for (mine, far), slope in zip(done, (slope_a, slope_b))
    ]
    grad_pre = jnp.concatenate(parts, 1).reshape(512, HID)
    return (grad_pre, grad_down)


def solution(mesh):
    placed = (P(("depth", "col"), "row"), P("col", "depth"), P(("depth", "col"), "row"))
    return jax.shard_map(
        local,
        mesh=mesh,
        in_specs=placed,
        out_specs=(P("row", ("depth", "col")), P(("depth", "col"), "row")),
        check_vma=False,
    )
```

```python
import functools
import math

import jax
import jax.numpy as jnp
import numpy as np
from jax import lax
from jax.experimental import pallas as pl
from jax.experimental.pallas import tpu as pltpu
from jax.sharding import PartitionSpec as P

gelu_const = math.sqrt(2.0 / math.pi)

SHARDS = 32
ROWS = 64
FEATS = 3072
HID = 768
X, Y0, Y1, Z0, Z1 = 16, 4, 12, 1, 3
DIMS = (X, Z0, Y0, Z1, Y1)
CHAINS = 4
WIDTH = FEATS // CHAINS
ORDERS = tuple(tuple(DIMS[1 + (p + k) % 4] for k in range(4)) for p in range(CHAINS))
HOPS = (Z0, Z1, Z0 ^ Z1)
PARTS = (32, 32)
STARTS = (0, 32)


def mask_of(c):
    mask = 0
    for k in range(5):
        if c >> k & 1:
            mask ^= DIMS[k]
    return mask


def swap(x, mask):
    if mask >= 4:
        return lax.ppermute(x, "depth", [(i, i ^ (mask >> 2)) for i in range(8)])
    return lax.ppermute(x, "col", [(i, i ^ mask) for i in range(4)])


def swap_row(x, mask):
    return lax.ppermute(x, "row", [(i, i ^ mask) for i in range(4)])


def in_hbm(x):
    return pltpu.with_memory_space_constraint(x, pltpu.HBM)


def params(mib):
    return pltpu.CompilerParams(vmem_limit_bytes=mib * 1024 * 1024)


TINY = pl.CostEstimate(flops=1, bytes_accessed=1, transcendentals=0)
ANY = pl.BlockSpec(memory_space=pl.ANY)
VMEM = pl.BlockSpec(memory_space=pltpu.VMEM)
SMEM = pl.BlockSpec(memory_space=pltpu.SMEM)


def cut_kernel(where, pre, *refs):
    chunks, sem = refs[:-1], refs[-1]
    row, col = where[0], where[1]
    half = SHARDS * ROWS // 8
    copies = []
    for j, mask in enumerate(HOPS):
        here = pre.at[
            pl.ds(pl.multiple_of(row % 2 * half, half), half), pl.ds(pl.multiple_of((col ^ mask) * HID, HID), HID)
        ]
        copies.append(pltpu.make_async_copy(here, chunks[j], sem.at[j]))
    for c in copies:
        c.start()
    for c in copies:
        c.wait()


def cut_call(where, pre):
    return pl.pallas_call(
        cut_kernel,
        out_shape=[jax.ShapeDtypeStruct((SHARDS * ROWS // 8, HID), jnp.bfloat16)] * len(HOPS),
        in_specs=[SMEM, ANY],
        out_specs=[ANY] * len(HOPS),
        scratch_shapes=[pltpu.SemaphoreType.DMA((len(HOPS),))],
        compiler_params=params(1),
        cost_estimate=TINY,
        name="cut",
    )(where, in_hbm(pre))


def split_kernel(own, got, *refs):
    outs, sem = refs[-1 - CHAINS : -1], refs[-1]
    copies = []
    for p in range(CHAINS):
        for side, src in enumerate((own, got)):
            here = src.at[:, pl.ds(p * WIDTH, WIDTH)]
            copies.append(pltpu.make_async_copy(here, outs[p].at[side], sem.at[len(copies)]))
    for c in copies:
        c.start()
    for c in copies:
        c.wait()


def split_call(own, got, after=()):
    return pl.pallas_call(
        split_kernel,
        out_shape=[jax.ShapeDtypeStruct((2, ROWS, WIDTH), jnp.bfloat16)] * CHAINS,
        in_specs=[ANY] * (2 + len(after)),
        out_specs=[ANY] * CHAINS,
        scratch_shapes=[pltpu.SemaphoreType.DMA((2 * CHAINS,))],
        compiler_params=params(1),
        cost_estimate=TINY,
        name="split",
    )(in_hbm(own), got, *after)


def grow_kernel(rows, joined, *refs):
    own, got, sem = refs[:CHAINS], refs[CHAINS : 2 * CHAINS], refs[-1]
    outs = refs[-1 - len(rows) * CHAINS - (joined > 0) : -1]
    copies = []
    for part, (at, n) in enumerate(rows):
        for p in range(CHAINS):
            blocks = own[p].shape[0]
            for side, src in enumerate((own[p], got[p])):
                there = outs[part * CHAINS + p].at[pl.ds(side * blocks, blocks)]
                copies.append(pltpu.make_async_copy(src.at[:, pl.ds(at, n)], there, sem.at[len(copies)]))
    for j in range(joined):
        src = refs[2 * CHAINS + j]
        copies.append(pltpu.make_async_copy(src, outs[-1].at[j], sem.at[len(copies)]))
    for c in copies:
        c.start()
    for c in copies:
        c.wait()


def grow_call(own, got, rows=((0, ROWS),), join=(), after=()):
    blocks = own[0].shape[0]
    shape = pltpu.HBM if len(rows) > 1 else jax.ShapeDtypeStruct
    return pl.pallas_call(
        functools.partial(grow_kernel, rows, len(join)),
        out_shape=[shape((2 * blocks, n, WIDTH), jnp.bfloat16) for _, n in rows for _ in range(CHAINS)]
        + [jax.ShapeDtypeStruct((len(join), *j.shape), jnp.bfloat16) for j in join[:1]],
        in_specs=[ANY] * (2 * CHAINS + len(join) + len(after)),
        out_specs=[ANY] * (len(rows) * CHAINS + (len(join) > 0)),
        scratch_shapes=[pltpu.SemaphoreType.DMA((2 * CHAINS * len(rows) + len(join),))],
        compiler_params=params(1),
        cost_estimate=TINY,
        name="grow",
    )(*own, *got, *join, *after)


def gelu_kernel(where, table, pre, got_a, got_b, got_c, other, *refs):
    outs, (buf, sems), acts = refs[:4], refs[4:6], refs[6:]
    act_t, slopes = outs[:2], outs[2:]
    row, col, mine = where[0], where[1], where[2]
    core = row % 2
    quarter, half = SHARDS * ROWS // 4, SHARDS * ROWS // 8
    copies = [
        pltpu.make_async_copy(
            pre.at[:, pl.ds(pl.multiple_of(col * HID, HID), HID)],
            buf.at[pl.ds(pl.multiple_of(col * quarter, quarter), quarter)],
            sems.at[0],
        )
    ]
    for j, got in enumerate((got_a, got_b, got_c)):
        for side, src in ((core, got), (1 - core, other.at[j])):
            at = pl.multiple_of((col ^ HOPS[j]) * quarter + side * half, half)
            copies.append(pltpu.make_async_copy(src, buf.at[pl.ds(at, half)], sems.at[len(copies)]))
    for c in copies:
        c.start()
    for c in copies:
        c.wait()

    def one_shard(s, carry):
        v = buf[pl.ds(pl.multiple_of((mine ^ table[s]) * ROWS, ROWS), ROWS), :].astype(jnp.float32)
        bend = jnp.tanh(gelu_const * (v + 0.044715 * v * v * v))
        a = (0.5 * v * (1.0 + bend)).astype(jnp.bfloat16)
        for part in range(2):
            n, at = PARTS[part], STARTS[part]
            acts[part][pl.ds(pl.multiple_of(s * n, 16), n), :] = a[at : at + n]
        return carry

    lax.fori_loop(0, SHARDS, one_shard, 0)

    def one_slope(s, carry):
        at_row = pl.multiple_of(row * quarter + s * ROWS, ROWS)
        v = buf[pl.ds(at_row, ROWS), :].astype(jnp.float32)
        bend = jnp.tanh(gelu_const * (v + 0.044715 * v * v * v))
        d = 0.5 * (1.0 + bend) + 0.5 * v * (1.0 - bend * bend) * gelu_const * (1.0 + 3.0 * 0.044715 * v * v)
        for part in range(2):
            n, at = PARTS[part], STARTS[part]
            slopes[part][s] = d[at : at + n]
        return carry

    lax.fori_loop(0, SHARDS // 4, one_slope, 0)

    for part in range(2):

        def one_turn(j, carry, part=part):
            at = pl.multiple_of(j * 128, 128)
            act_t[part][:, pl.ds(at, 128)] = acts[part][pl.ds(at, 128), :].T
            return carry

        lax.fori_loop(0, SHARDS * PARTS[part] // 128, one_turn, 0)


def gelu_call(where, table, pre, fetched, other):
    tokens = [SHARDS * n for n in PARTS]
    return pl.pallas_call(
        gelu_kernel,
        out_shape=[jax.ShapeDtypeStruct((HID, t), jnp.bfloat16) for t in tokens]
        + [jax.ShapeDtypeStruct((SHARDS // 4, n, HID), jnp.float32) for n in PARTS],
        in_specs=[SMEM, SMEM] + [ANY] * 5,
        out_specs=[VMEM] * 4,
        scratch_shapes=[pltpu.VMEM((SHARDS * ROWS, HID), jnp.bfloat16), pltpu.SemaphoreType.DMA((7,))]
        + [pltpu.VMEM((t, HID), jnp.bfloat16) for t in tokens],
        compiler_params=params(20),
        cost_estimate=TINY,
        name="gelu",
    )(where, table, in_hbm(pre), *fetched, other)


def pieces(p, side, top):
    every = slice(None)
    if p == 0:
        return [((every,) * 4, (side,) + (every,) * 4)] if side == top else []
    if p == 1:
        return [((top,) + (every,) * 3, (top,) + (every,) * 2 + (side, every))]
    if p == 2:
        return [((i, top) + (every,) * 2, (top, every, side, i, every)) for i in range(2)]
    return [((every,) * 2 + (top, every), (top, side) + (every,) * 3)]


def hidden_kernel(n, where, w_far, *refs):
    blocks = refs[: 2 * CHAINS]
    keep, send, gathered, g, w, hs, sems = refs[-7:]
    row, mine = where[0], where[2]
    per = SHARDS // 4
    weights = pltpu.make_async_copy(w_far, w, sems.at[4])
    weights.start()
    for top in range(2):
        for p in range(CHAINS):
            for side in range(2):
                for src, dst in pieces(p, side, top):
                    pltpu.make_async_copy(
                        blocks[2 * p + side].at[src],
                        g.at[dst + (slice(None), pl.ds(p * WIDTH, WIDTH))],
                        sems.at[top],
                    ).start()
    outs = []
    for i in range(2):
        pltpu.make_async_copy(g.at[i], g.at[i], sems.at[i]).wait()
        if i == 0:
            weights.wait()
        outs.append(pltpu.make_async_copy(g.at[i], gathered.at[i], sems.at[2 + i]))
        outs[-1].start()
        h = lax.dot_general(
            g[i].reshape(2 * per * n, FEATS), w[...], (((1,), (1,)), ((), ())), preferred_element_type=jnp.float32
        )
        hs[i] = h.reshape(2, 2, 2, 2, n, HID)
    for a, b in ((1, 1), (0, 1), (1, 0), (0, 0)):
        off_x = (mine // 16) ^ (row // 2) ^ a
        off_y = (mine // 8 % 2) ^ (row % 2) ^ b
        for j in range(per):
            slot = (mine % 8) ^ (mask_of(2 * j) % 8) ^ (off_y * 4)
            here = hs[off_y, j // 4, j // 2 % 2, j % 2, off_x]
            if b:
                send[a, slot] = here.astype(jnp.bfloat16)
            else:
                keep[a, slot] = here
    for out in outs:
        out.wait()


def hidden_call(part, where, w, blocks, after=()):
    n = PARTS[part]
    per = SHARDS // 4
    return pl.pallas_call(
        functools.partial(hidden_kernel, n),
        out_shape=[
            jax.ShapeDtypeStruct((2, per, n, HID), jnp.float32),
            jax.ShapeDtypeStruct((2, per, n, HID), jnp.bfloat16),
            pltpu.HBM((2,) * 5 + (n, FEATS), jnp.bfloat16),
        ],
        in_specs=[SMEM] + [ANY] * (1 + 2 * CHAINS + len(after)),
        out_specs=[VMEM, VMEM, ANY],
        scratch_shapes=[
            pltpu.VMEM((2,) * 5 + (n, FEATS), jnp.bfloat16),
            pltpu.VMEM((HID, FEATS), jnp.bfloat16),
            pltpu.VMEM((2,) * 5 + (n, HID), jnp.float32),
            pltpu.SemaphoreType.DMA((5,)),
        ],
        compiler_params=params(14 + n // 2),
        cost_estimate=pl.CostEstimate(
            flops=2 * SHARDS * n * FEATS * HID, bytes_accessed=SHARDS * n * FEATS * 4, transcendentals=0
        ),
        name="hidden",
    )(where, w, *(f(b.reshape((2,) * 4 + b.shape[1:])) for b, f in zip(blocks, (in_hbm, lambda x: x) * CHAINS)), *after)


def total_kernel(keep, got, *refs):
    mine, far = refs[-2:]
    mine[...] = keep[0] + got[0].astype(jnp.float32)
    far[...] = (keep[1] + got[1].astype(jnp.float32)).astype(jnp.bfloat16)


def total_call(keep, got, after=()):
    return pl.pallas_call(
        total_kernel,
        out_shape=[
            jax.ShapeDtypeStruct(keep.shape[1:], jnp.float32),
            jax.ShapeDtypeStruct(keep.shape[1:], jnp.bfloat16),
        ],
        in_specs=[VMEM, VMEM] + [ANY] * len(after),
        out_specs=[VMEM, VMEM],
        compiler_params=params(8),
        cost_estimate=TINY,
        name="total",
    )(keep, got, *after)


def down_kernel(at_a, at_b, g_a, g_b, *refs):
    out = refs[-1]
    acc = jnp.dot(at_a[...], g_a[...], preferred_element_type=jnp.float32)
    acc += jnp.dot(at_b[...], g_b[...], preferred_element_type=jnp.float32)
    out[...] = acc.astype(jnp.bfloat16)


def down_call(acts, gathered, first, count, base=None):
    wide = 512
    tokens = [SHARDS * n for n in PARTS]
    in_specs = [pl.BlockSpec((HID, t), lambda j: (0, 0)) for t in tokens]
    in_specs += [pl.BlockSpec((t, wide), lambda j: (0, j + first)) for t in tokens]
    args = [*acts, *(in_hbm(g.reshape(t, FEATS)) for g, t in zip(gathered, tokens))]
    aliases = {}
    if base is not None:
        in_specs.append(ANY)
        args.append(in_hbm(base))
        aliases = {4: 0}
    return pl.pallas_call(
        down_kernel,
        grid=(count,),
        out_shape=pltpu.HBM((HID, FEATS), jnp.bfloat16),
        in_specs=in_specs,
        out_specs=pl.BlockSpec((HID, wide), lambda j: (0, j + first)),
        input_output_aliases=aliases,
        compiler_params=params(24),
        cost_estimate=pl.CostEstimate(
            flops=2 * 2048 * HID * wide * count, bytes_accessed=count * wide * 2 * (2048 + HID), transcendentals=0
        ),
        name="down",
    )(*args)


def local(grad_out, pre_act, w_down):
    depth, row, col = (lax.axis_index(a) for a in ("depth", "row", "col"))
    where = jnp.stack([row, col, depth * 4 + col]).astype(jnp.int32)
    table = jnp.asarray([mask_of(c) for c in range(SHARDS)], jnp.int32)

    got = swap(in_hbm(grad_out), X)
    fetched = [swap(chunk, mask) for chunk, mask in zip(cut_call(where, pre_act), HOPS)]
    blocks = split_call(grad_out, got)
    got = [swap(blocks[p], ORDERS[p][0]) for p in range(CHAINS)]
    *blocks, both = grow_call(blocks, got, join=fetched)
    got = [swap(blocks[p], ORDERS[p][1]) for p in range(CHAINS)]
    other = swap_row(both, 1)
    blocks = grow_call(blocks, got, after=(other,))
    got = [swap(blocks[p], ORDERS[p][2]) for p in range(CHAINS)]
    act_a, act_b, slope_a, slope_b = gelu_call(where, table, pre_act, fetched, other)
    grown = grow_call(blocks, got, tuple(zip(STARTS, PARTS)), after=(slope_a,))
    own = grown[:CHAINS], grown[CHAINS:]
    came = [[swap(own[part][p], ORDERS[p][3]) for p in range(CHAINS)] for part in range(2)]

    pairs = [[b for p in range(CHAINS) for b in (own[part][p], came[part][p])] for part in range(2)]
    keep_a, send_a, g_a = hidden_call(0, where, w_down, pairs[0])
    keep_b, send_b, g_b = hidden_call(1, where, w_down, pairs[1], after=(keep_a,))
    mine_a, far_a = total_call(keep_a, swap_row(send_a, 1), after=(keep_b,))
    far_a = swap_row(far_a, 2)
    grad_down = down_call((act_a, act_b), (g_a, g_b), 0, 2)
    mine_b, far_b = total_call(keep_b, swap_row(send_b, 1), after=(in_hbm(grad_down),))
    far_b = swap_row(far_b, 2)
    grad_down = down_call((act_a, act_b), (g_a, g_b), 2, 4, grad_down)
    done = (mine_a, far_a), (mine_b, far_b)
    parts = [
        ((mine + far.astype(jnp.float32)) * slope).astype(jnp.bfloat16)
        for (mine, far), slope in zip(done, (slope_a, slope_b))
    ]
    grad_pre = jnp.concatenate(parts, 1).reshape(512, HID)
    return (grad_pre, grad_down)


def solution(mesh):
    placed = (P(("depth", "col"), "row"), P("col", "depth"), P(("depth", "col"), "row"))
    return jax.shard_map(
        local,
        mesh=mesh,
        in_specs=placed,
        out_specs=(P("row", ("depth", "col")), P(("depth", "col"), "row")),
        check_vma=False,
    )
```

```python
import functools
import math

import jax
import jax.numpy as jnp
import numpy as np
from jax import lax
from jax.experimental import pallas as pl
from jax.experimental.pallas import tpu as pltpu
from jax.sharding import PartitionSpec as P

gelu_const = math.sqrt(2.0 / math.pi)

SHARDS = 32
ROWS = 64
FEATS = 3072
HID = 768
X, Y0, Y1, Z0, Z1 = 16, 4, 12, 1, 3
DIMS = (X, Z0, Y0, Z1, Y1)
CHAINS = 4
WIDTH = FEATS // CHAINS
ORDERS = tuple(tuple(DIMS[1 + (p + k) % 4] for k in range(4)) for p in range(CHAINS))
HOPS = (Z0, Z1, Z0 ^ Z1)
SLICE = SHARDS * ROWS // 16
PARTS = (32, 32)
STARTS = (0, 32)


def mask_of(c):
    mask = 0
    for k in range(5):
        if c >> k & 1:
            mask ^= DIMS[k]
    return mask


def swap(x, mask):
    if mask >= 4:
        return lax.ppermute(x, "depth", [(i, i ^ (mask >> 2)) for i in range(8)])
    return lax.ppermute(x, "col", [(i, i ^ mask) for i in range(4)])


def swap_row(x, mask):
    return lax.ppermute(x, "row", [(i, i ^ mask) for i in range(4)])


def in_hbm(x):
    return pltpu.with_memory_space_constraint(x, pltpu.HBM)


def params(mib):
    return pltpu.CompilerParams(vmem_limit_bytes=mib * 1024 * 1024)


TINY = pl.CostEstimate(flops=1, bytes_accessed=1, transcendentals=0)
ANY = pl.BlockSpec(memory_space=pl.ANY)
VMEM = pl.BlockSpec(memory_space=pltpu.VMEM)
SMEM = pl.BlockSpec(memory_space=pltpu.SMEM)


def cut_kernel(where, pre, *refs):
    chunks, sem = refs[:-1], refs[-1]
    row, col = where[0], where[1]
    copies = []
    for j, mask in enumerate(HOPS):
        here = pre.at[
            pl.ds(pl.multiple_of(row * SLICE, SLICE), SLICE), pl.ds(pl.multiple_of((col ^ mask) * HID, HID), HID)
        ]
        copies.append(pltpu.make_async_copy(here, chunks[j], sem.at[j]))
    for c in copies:
        c.start()
    for c in copies:
        c.wait()


def cut_call(where, pre):
    return pl.pallas_call(
        cut_kernel,
        out_shape=[jax.ShapeDtypeStruct((SLICE, HID), jnp.bfloat16)] * len(HOPS),
        in_specs=[SMEM, ANY],
        out_specs=[ANY] * len(HOPS),
        scratch_shapes=[pltpu.SemaphoreType.DMA((len(HOPS),))],
        compiler_params=params(1),
        cost_estimate=TINY,
        name="cut",
    )(where, in_hbm(pre))


def split_kernel(own, got, *refs):
    outs, sem = refs[-1 - CHAINS : -1], refs[-1]
    copies = []
    for p in range(CHAINS):
        for side, src in enumerate((own, got)):
            here = src.at[:, pl.ds(p * WIDTH, WIDTH)]
            copies.append(pltpu.make_async_copy(here, outs[p].at[side], sem.at[len(copies)]))
    for c in copies:
        c.start()
    for c in copies:
        c.wait()


def split_call(own, got, after=()):
    return pl.pallas_call(
        split_kernel,
        out_shape=[jax.ShapeDtypeStruct((2, ROWS, WIDTH), jnp.bfloat16)] * CHAINS,
        in_specs=[ANY] * (2 + len(after)),
        out_specs=[ANY] * CHAINS,
        scratch_shapes=[pltpu.SemaphoreType.DMA((2 * CHAINS,))],
        compiler_params=params(1),
        cost_estimate=TINY,
        name="split",
    )(in_hbm(own), got, *after)


def grow_kernel(chains, at, n, joined, *refs):
    outs, sem = refs[-1 - chains - (joined > 0) : -1], refs[-1]
    pairs = []
    for p in range(chains):
        blocks = refs[2 * p].shape[0]
        for side in range(2):
            pairs.append((refs[2 * p + side].at[:, pl.ds(at, n)], outs[p].at[pl.ds(side * blocks, blocks)]))
    for j in range(joined):
        pairs.append((refs[2 * chains + j], outs[-1].at[j]))
    copies = [pltpu.make_async_copy(*pair, sem.at[i]) for i, pair in enumerate(pairs)]
    for c in copies:
        c.start()
    for c in copies:
        c.wait()


def grow_call(pairs, at=0, n=ROWS, join=(), after=()):
    blocks = pairs[0][0].shape[0]
    shape = jax.ShapeDtypeStruct if n == ROWS else pltpu.HBM
    return pl.pallas_call(
        functools.partial(grow_kernel, len(pairs), at, n, len(join)),
        out_shape=[shape((2 * blocks, n, WIDTH), jnp.bfloat16)] * len(pairs)
        + [jax.ShapeDtypeStruct((len(join), *j.shape), jnp.bfloat16) for j in join[:1]],
        in_specs=[ANY] * (2 * len(pairs) + len(join) + len(after)),
        out_specs=[ANY] * (len(pairs) + (len(join) > 0)),
        scratch_shapes=[pltpu.SemaphoreType.DMA((2 * len(pairs) + len(join),))],
        compiler_params=params(1),
        cost_estimate=TINY,
        name="grow",
    )(*(x for pair in pairs for x in pair), *join, *after)


def gelu_kernel(where, table, pre, near, far, *refs):
    outs, (buf, sems), acts = refs[:4], refs[4:6], refs[6:]
    act_t, slopes = outs[:2], outs[2:]
    row, col, mine = where[0], where[1], where[2]
    quarter = SHARDS * ROWS // 4
    copies = [
        pltpu.make_async_copy(
            pre.at[:, pl.ds(pl.multiple_of(col * HID, HID), HID)],
            buf.at[pl.ds(pl.multiple_of(col * quarter, quarter), quarter)],
            sems.at[0],
        )
    ]
    for side, src in enumerate((near, far)):
        for i in range(2):
            for j, mask in enumerate(HOPS):
                at = pl.multiple_of((col ^ mask) * quarter + (row ^ (2 * side + i)) * SLICE, SLICE)
                copies.append(pltpu.make_async_copy(src.at[i, j], buf.at[pl.ds(at, SLICE)], sems.at[len(copies)]))
    for c in copies:
        c.start()
    for c in copies:
        c.wait()

    def one_shard(s, carry):
        v = buf[pl.ds(pl.multiple_of((mine ^ table[s]) * ROWS, ROWS), ROWS), :].astype(jnp.float32)
        bend = jnp.tanh(gelu_const * (v + 0.044715 * v * v * v))
        a = (0.5 * v * (1.0 + bend)).astype(jnp.bfloat16)
        for part in range(2):
            n, at = PARTS[part], STARTS[part]
            acts[part][pl.ds(pl.multiple_of(s * n, 16), n), :] = a[at : at + n]
        return carry

    lax.fori_loop(0, SHARDS, one_shard, 0)

    def one_slope(s, carry):
        at_row = pl.multiple_of(row * quarter + s * ROWS, ROWS)
        v = buf[pl.ds(at_row, ROWS), :].astype(jnp.float32)
        bend = jnp.tanh(gelu_const * (v + 0.044715 * v * v * v))
        d = 0.5 * (1.0 + bend) + 0.5 * v * (1.0 - bend * bend) * gelu_const * (1.0 + 3.0 * 0.044715 * v * v)
        for part in range(2):
            n, at = PARTS[part], STARTS[part]
            slopes[part][s] = d[at : at + n]
        return carry

    lax.fori_loop(0, SHARDS // 4, one_slope, 0)

    for part in range(2):

        def one_turn(j, carry, part=part):
            at = pl.multiple_of(j * 128, 128)
            act_t[part][:, pl.ds(at, 128)] = acts[part][pl.ds(at, 128), :].T
            return carry

        lax.fori_loop(0, SHARDS * PARTS[part] // 128, one_turn, 0)


def gelu_call(where, table, pre, near, far):
    tokens = [SHARDS * n for n in PARTS]
    return pl.pallas_call(
        gelu_kernel,
        out_shape=[jax.ShapeDtypeStruct((HID, t), jnp.bfloat16) for t in tokens]
        + [jax.ShapeDtypeStruct((SHARDS // 4, n, HID), jnp.float32) for n in PARTS],
        in_specs=[SMEM, SMEM] + [ANY] * 3,
        out_specs=[VMEM] * 4,
        scratch_shapes=[pltpu.VMEM((SHARDS * ROWS, HID), jnp.bfloat16), pltpu.SemaphoreType.DMA((13,))]
        + [pltpu.VMEM((t, HID), jnp.bfloat16) for t in tokens],
        compiler_params=params(20),
        cost_estimate=TINY,
        name="gelu",
    )(where, table, in_hbm(pre), near, far)


def pieces(p, side, top):
    every = slice(None)
    if p == 0:
        return [((every,) * 4, (side,) + (every,) * 4)] if side == top else []
    if p == 1:
        return [((top,) + (every,) * 3, (top,) + (every,) * 2 + (side, every))]
    if p == 2:
        return [((i, top) + (every,) * 2, (top, every, side, i, every)) for i in range(2)]
    return [((every,) * 2 + (top, every), (top, side) + (every,) * 3)]


def hidden_kernel(n, where, w_far, *refs):
    blocks = refs[: 2 * CHAINS]
    keep, send, gathered, g, w, hs, sems = refs[-7:]
    row, mine = where[0], where[2]
    per = SHARDS // 4
    weights = pltpu.make_async_copy(w_far, w, sems.at[4])
    weights.start()
    for top in range(2):
        for p in range(CHAINS):
            for side in range(2):
                for src, dst in pieces(p, side, top):
                    pltpu.make_async_copy(
                        blocks[2 * p + side].at[src],
                        g.at[dst + (slice(None), pl.ds(p * WIDTH, WIDTH))],
                        sems.at[top],
                    ).start()
    outs = []
    for i in range(2):
        pltpu.make_async_copy(g.at[i], g.at[i], sems.at[i]).wait()
        if i == 0:
            weights.wait()
        outs.append(pltpu.make_async_copy(g.at[i], gathered.at[i], sems.at[2 + i]))
        outs[-1].start()
        h = lax.dot_general(
            g[i].reshape(2 * per * n, FEATS), w[...], (((1,), (1,)), ((), ())), preferred_element_type=jnp.float32
        )
        hs[i] = h.reshape(2, 2, 2, 2, n, HID)
    for a, b in ((1, 1), (0, 1), (1, 0), (0, 0)):
        off_x = (mine // 16) ^ (row // 2) ^ a
        off_y = (mine // 8 % 2) ^ (row % 2) ^ b
        for j in range(per):
            slot = (mine % 8) ^ (mask_of(2 * j) % 8) ^ (off_y * 4)
            here = hs[off_y, j // 4, j // 2 % 2, j % 2, off_x]
            if b:
                send[a, slot] = here.astype(jnp.bfloat16)
            else:
                keep[a, slot] = here
    for out in outs:
        out.wait()


def hidden_call(part, where, w, blocks, after=()):
    n = PARTS[part]
    per = SHARDS // 4
    return pl.pallas_call(
        functools.partial(hidden_kernel, n),
        out_shape=[
            jax.ShapeDtypeStruct((2, per, n, HID), jnp.float32),
            jax.ShapeDtypeStruct((2, per, n, HID), jnp.bfloat16),
            pltpu.HBM((2,) * 5 + (n, FEATS), jnp.bfloat16),
        ],
        in_specs=[SMEM] + [ANY] * (1 + 2 * CHAINS + len(after)),
        out_specs=[VMEM, VMEM, ANY],
        scratch_shapes=[
            pltpu.VMEM((2,) * 5 + (n, FEATS), jnp.bfloat16),
            pltpu.VMEM((HID, FEATS), jnp.bfloat16),
            pltpu.VMEM((2,) * 5 + (n, HID), jnp.float32),
            pltpu.SemaphoreType.DMA((5,)),
        ],
        compiler_params=params(14 + n // 2),
        cost_estimate=pl.CostEstimate(
            flops=2 * SHARDS * n * FEATS * HID, bytes_accessed=SHARDS * n * FEATS * 4, transcendentals=0
        ),
        name="hidden",
    )(where, w, *(f(b.reshape((2,) * 4 + b.shape[1:])) for b, f in zip(blocks, (in_hbm, lambda x: x) * CHAINS)), *after)


def total_kernel(keep, got, *refs):
    mine, far = refs[-2:]
    mine[...] = keep[0] + got[0].astype(jnp.float32)
    far[...] = (keep[1] + got[1].astype(jnp.float32)).astype(jnp.bfloat16)


def total_call(keep, got, after=()):
    return pl.pallas_call(
        total_kernel,
        out_shape=[
            jax.ShapeDtypeStruct(keep.shape[1:], jnp.float32),
            jax.ShapeDtypeStruct(keep.shape[1:], jnp.bfloat16),
        ],
        in_specs=[VMEM, VMEM] + [ANY] * len(after),
        out_specs=[VMEM, VMEM],
        compiler_params=params(8),
        cost_estimate=TINY,
        name="total",
    )(keep, got, *after)


def down_kernel(at_a, at_b, g_a, g_b, *refs):
    out = refs[-1]
    acc = jnp.dot(at_a[...], g_a[...], preferred_element_type=jnp.float32)
    acc += jnp.dot(at_b[...], g_b[...], preferred_element_type=jnp.float32)
    out[...] = acc.astype(jnp.bfloat16)


def down_call(acts, gathered, first, count, base=None, after=()):
    wide = 512
    tokens = [SHARDS * n for n in PARTS]
    in_specs = [pl.BlockSpec((HID, t), lambda j: (0, 0)) for t in tokens]
    in_specs += [pl.BlockSpec((t, wide), lambda j: (0, j + first)) for t in tokens]
    args = [*acts, *(in_hbm(g.reshape(t, FEATS)) for g, t in zip(gathered, tokens))]
    aliases = {}
    if base is not None:
        in_specs.append(ANY)
        args.append(in_hbm(base))
        aliases = {4: 0}
    in_specs += [ANY] * len(after)
    args += after
    return pl.pallas_call(
        down_kernel,
        grid=(count,),
        out_shape=pltpu.HBM((HID, FEATS), jnp.bfloat16),
        in_specs=in_specs,
        out_specs=pl.BlockSpec((HID, wide), lambda j: (0, j + first)),
        input_output_aliases=aliases,
        compiler_params=params(24),
        cost_estimate=pl.CostEstimate(
            flops=2 * 2048 * HID * wide * count, bytes_accessed=count * wide * 2 * (2048 + HID), transcendentals=0
        ),
        name="down",
    )(*args)


def local(grad_out, pre_act, w_down):
    depth, row, col = (lax.axis_index(a) for a in ("depth", "row", "col"))
    where = jnp.stack([row, col, depth * 4 + col]).astype(jnp.int32)
    table = jnp.asarray([mask_of(c) for c in range(SHARDS)], jnp.int32)

    got = swap(in_hbm(grad_out), X)
    fetched = [swap(chunk, mask) for chunk, mask in zip(cut_call(where, pre_act), HOPS)]
    blocks = split_call(grad_out, got)
    for k in range(2):
        pairs = [(b, swap(b, ORDERS[p][k])) for p, b in enumerate(blocks)]
        last = grow_call(pairs[-1:], join=fetched) if k == 0 else grow_call(pairs[-1:], join=[fetched, other])
        blocks = [grow_call([pair])[0] for pair in pairs[:-1]] + [last[0]]
        if k == 0:
            fetched = last[1]
            other = swap_row(fetched, 1)
    near = last[1]
    far = swap_row(near, 2)
    pairs = [(b, swap(b, ORDERS[p][2])) for p, b in enumerate(blocks)]
    own_a = [grow_call([pair], STARTS[0], PARTS[0])[0] for pair in pairs]
    came_a = [swap(own_a[p], ORDERS[p][3]) for p in range(CHAINS)]
    act_a, act_b, slope_a, slope_b = gelu_call(where, table, pre_act, near, far)
    own_b = grow_call(pairs, STARTS[1], PARTS[1], after=(slope_a,))
    came_b = [swap(own_b[p], ORDERS[p][3]) for p in range(CHAINS)]
    own, came = (own_a, own_b), (came_a, came_b)

    pairs = [[b for p in range(CHAINS) for b in (own[part][p], came[part][p])] for part in range(2)]
    keep_a, send_a, g_a = hidden_call(0, where, w_down, pairs[0])
    keep_b, send_b, g_b = hidden_call(1, where, w_down, pairs[1], after=(keep_a,))
    mine_a, far_a = total_call(keep_a, swap_row(send_a, 1), after=(keep_b,))
    far_a = swap_row(far_a, 2)
    grad_down = down_call((act_a, act_b), (g_a, g_b), 0, 2, after=(mine_a,))
    mine_b, far_b = total_call(keep_b, swap_row(send_b, 1), after=(in_hbm(grad_down),))
    far_b = swap_row(far_b, 2)
    grad_down = down_call((act_a, act_b), (g_a, g_b), 2, 4, grad_down)
    done = (mine_a, far_a), (mine_b, far_b)
    parts = [
        ((mine + far.astype(jnp.float32)) * slope).astype(jnp.bfloat16)
        for (mine, far), slope in zip(done, (slope_a, slope_b))
    ]
    grad_pre = jnp.concatenate(parts, 1).reshape(512, HID)
    return (grad_pre, grad_down)


def solution(mesh):
    placed = (P(("depth", "col"), "row"), P("col", "depth"), P(("depth", "col"), "row"))
    return jax.shard_map(
        local,
        mesh=mesh,
        in_specs=placed,
        out_specs=(P("row", ("depth", "col")), P(("depth", "col"), "row")),
        check_vma=False,
    )
```

```python
import functools
import math

import jax
import jax.numpy as jnp
import numpy as np
from jax import lax
from jax.experimental import pallas as pl
from jax.experimental.pallas import tpu as pltpu
from jax.sharding import PartitionSpec as P

gelu_const = math.sqrt(2.0 / math.pi)

SHARDS = 32
ROWS = 64
FEATS = 3072
HID = 768
X, Y0, Y1, Z0, Z1 = 16, 4, 12, 1, 3
DIMS = (X, Z0, Y0, Z1, Y1)
CHAINS = 4
WIDTH = FEATS // CHAINS
ORDERS = tuple(tuple(DIMS[1 + (p + k) % 4] for k in range(4)) for p in range(CHAINS))
HOPS = (Z0, Z1, Z0 ^ Z1)
SLICE = SHARDS * ROWS // 16
PARTS = (32, 32)
STARTS = (0, 32)


def mask_of(c):
    mask = 0
    for k in range(5):
        if c >> k & 1:
            mask ^= DIMS[k]
    return mask


def swap(x, mask):
    if mask >= 4:
        return lax.ppermute(x, "depth", [(i, i ^ (mask >> 2)) for i in range(8)])
    return lax.ppermute(x, "col", [(i, i ^ mask) for i in range(4)])


def swap_row(x, mask):
    return lax.ppermute(x, "row", [(i, i ^ mask) for i in range(4)])


def in_hbm(x):
    return pltpu.with_memory_space_constraint(x, pltpu.HBM)


def params(mib):
    return pltpu.CompilerParams(vmem_limit_bytes=mib * 1024 * 1024)


TINY = pl.CostEstimate(flops=1, bytes_accessed=1, transcendentals=0)
ANY = pl.BlockSpec(memory_space=pl.ANY)
VMEM = pl.BlockSpec(memory_space=pltpu.VMEM)
SMEM = pl.BlockSpec(memory_space=pltpu.SMEM)


def cut_kernel(where, pre, *refs):
    chunks, sem = refs[:-1], refs[-1]
    row, col = where[0], where[1]
    copies = []
    for j, mask in enumerate(HOPS):
        here = pre.at[
            pl.ds(pl.multiple_of(row * SLICE, SLICE), SLICE), pl.ds(pl.multiple_of((col ^ mask) * HID, HID), HID)
        ]
        copies.append(pltpu.make_async_copy(here, chunks[j], sem.at[j]))
    for c in copies:
        c.start()
    for c in copies:
        c.wait()


def cut_call(where, pre):
    return pl.pallas_call(
        cut_kernel,
        out_shape=[jax.ShapeDtypeStruct((SLICE, HID), jnp.bfloat16)] * len(HOPS),
        in_specs=[SMEM, ANY],
        out_specs=[ANY] * len(HOPS),
        scratch_shapes=[pltpu.SemaphoreType.DMA((len(HOPS),))],
        compiler_params=params(1),
        cost_estimate=TINY,
        name="cut",
    )(where, in_hbm(pre))


def split_kernel(own, got, *refs):
    joined, outs, both, sem = refs[: len(HOPS)], refs[len(HOPS) : -2], refs[-2], refs[-1]
    pairs = []
    for p in range(CHAINS):
        for side, src in enumerate((own, got)):
            pairs.append((src.at[:, pl.ds(p * WIDTH, WIDTH)], outs[p].at[side]))
    for j, src in enumerate(joined):
        pairs.append((src, both.at[j]))
    copies = [pltpu.make_async_copy(*pair, sem.at[i]) for i, pair in enumerate(pairs)]
    for c in copies:
        c.start()
    for c in copies:
        c.wait()


def split_call(own, got, join):
    return pl.pallas_call(
        split_kernel,
        out_shape=[jax.ShapeDtypeStruct((2, ROWS, WIDTH), jnp.bfloat16)] * CHAINS
        + [jax.ShapeDtypeStruct((len(HOPS), SLICE, HID), jnp.bfloat16)],
        in_specs=[ANY] * (2 + len(HOPS)),
        out_specs=[ANY] * (CHAINS + 1),
        scratch_shapes=[pltpu.SemaphoreType.DMA((2 * CHAINS + len(HOPS),))],
        compiler_params=params(1),
        cost_estimate=TINY,
        name="split",
    )(in_hbm(own), got, *join)


def grow_kernel(chains, at, n, joined, *refs):
    outs, sem = refs[-1 - chains - (joined > 0) : -1], refs[-1]
    pairs = []
    for p in range(chains):
        blocks = refs[2 * p].shape[0]
        for side in range(2):
            pairs.append((refs[2 * p + side].at[:, pl.ds(at, n)], outs[p].at[pl.ds(side * blocks, blocks)]))
    for j in range(joined):
        pairs.append((refs[2 * chains + j], outs[-1].at[j]))
    copies = [pltpu.make_async_copy(*pair, sem.at[i]) for i, pair in enumerate(pairs)]
    for c in copies:
        c.start()
    for c in copies:
        c.wait()


def grow_call(pairs, at=0, n=ROWS, join=(), after=()):
    blocks = pairs[0][0].shape[0]
    shape = jax.ShapeDtypeStruct if n == ROWS else pltpu.HBM
    return pl.pallas_call(
        functools.partial(grow_kernel, len(pairs), at, n, len(join)),
        out_shape=[shape((2 * blocks, n, WIDTH), jnp.bfloat16)] * len(pairs)
        + [jax.ShapeDtypeStruct((len(join), *j.shape), jnp.bfloat16) for j in join[:1]],
        in_specs=[ANY] * (2 * len(pairs) + len(join) + len(after)),
        out_specs=[ANY] * (len(pairs) + (len(join) > 0)),
        scratch_shapes=[pltpu.SemaphoreType.DMA((2 * len(pairs) + len(join),))],
        compiler_params=params(1),
        cost_estimate=TINY,
        name="grow",
    )(*(x for pair in pairs for x in pair), *join, *after)


def gelu_kernel(where, table, pre, near, far, *refs):
    outs, (buf, sems), acts = refs[-8:-4], refs[-4:-2], refs[-2:]
    act_t, slopes = outs[:2], outs[2:]
    row, col, mine = where[0], where[1], where[2]
    quarter = SHARDS * ROWS // 4
    copies = [
        pltpu.make_async_copy(
            pre.at[:, pl.ds(pl.multiple_of(col * HID, HID), HID)],
            buf.at[pl.ds(pl.multiple_of(col * quarter, quarter), quarter)],
            sems.at[0],
        )
    ]
    for side, src in enumerate((near, far)):
        for i in range(2):
            for j, mask in enumerate(HOPS):
                at = pl.multiple_of((col ^ mask) * quarter + (row ^ (2 * side + i)) * SLICE, SLICE)
                copies.append(pltpu.make_async_copy(src.at[i, j], buf.at[pl.ds(at, SLICE)], sems.at[len(copies)]))
    for c in copies:
        c.start()
    for c in copies:
        c.wait()

    def one_shard(s, carry):
        v = buf[pl.ds(pl.multiple_of((mine ^ table[s]) * ROWS, ROWS), ROWS), :].astype(jnp.float32)
        bend = jnp.tanh(gelu_const * (v + 0.044715 * v * v * v))
        a = (0.5 * v * (1.0 + bend)).astype(jnp.bfloat16)
        for part in range(2):
            n, at = PARTS[part], STARTS[part]
            acts[part][pl.ds(pl.multiple_of(s * n, 16), n), :] = a[at : at + n]
        return carry

    lax.fori_loop(0, SHARDS, one_shard, 0)

    def one_slope(s, carry):
        at_row = pl.multiple_of(row * quarter + s * ROWS, ROWS)
        v = buf[pl.ds(at_row, ROWS), :].astype(jnp.float32)
        bend = jnp.tanh(gelu_const * (v + 0.044715 * v * v * v))
        d = 0.5 * (1.0 + bend) + 0.5 * v * (1.0 - bend * bend) * gelu_const * (1.0 + 3.0 * 0.044715 * v * v)
        for part in range(2):
            n, at = PARTS[part], STARTS[part]
            slopes[part][s] = d[at : at + n]
        return carry

    lax.fori_loop(0, SHARDS // 4, one_slope, 0)

    for part in range(2):

        def one_turn(j, carry, part=part):
            at = pl.multiple_of(j * 128, 128)
            act_t[part][:, pl.ds(at, 128)] = acts[part][pl.ds(at, 128), :].T
            return carry

        lax.fori_loop(0, SHARDS * PARTS[part] // 128, one_turn, 0)


def gelu_call(where, table, pre, near, far, after=()):
    tokens = [SHARDS * n for n in PARTS]
    return pl.pallas_call(
        gelu_kernel,
        out_shape=[jax.ShapeDtypeStruct((HID, t), jnp.bfloat16) for t in tokens]
        + [jax.ShapeDtypeStruct((SHARDS // 4, n, HID), jnp.float32) for n in PARTS],
        in_specs=[SMEM, SMEM] + [ANY] * (3 + len(after)),
        out_specs=[VMEM] * 4,
        scratch_shapes=[pltpu.VMEM((SHARDS * ROWS, HID), jnp.bfloat16), pltpu.SemaphoreType.DMA((13,))]
        + [pltpu.VMEM((t, HID), jnp.bfloat16) for t in tokens],
        compiler_params=params(20),
        cost_estimate=TINY,
        name="gelu",
    )(where, table, in_hbm(pre), near, far, *after)


def pieces(p, side):
    every = slice(None)
    if p == 0:
        return [((every,) * 4, (side,) + (every,) * 4)]
    if p == 1:
        return [((every,) * 4, (every,) * 3 + (side, every))]
    if p == 2:
        return [((i,) + (every,) * 3, (every,) * 2 + (side, i, every)) for i in range(2)]
    return [((every,) * 2 + (i, every), (i, side) + (every,) * 3) for i in range(2)]


def hidden_kernel(n, where, w_far, *refs):
    blocks = refs[: 2 * CHAINS]
    keep, send, gathered, g, w, hs, sems = refs[-7:]
    row, mine = where[0], where[2]
    per = SHARDS // 4
    every = (slice(None),) * 6
    weights, outs = [], []
    for p in range(CHAINS):
        cols = pl.ds(p * WIDTH, WIDTH)
        weights.append(pltpu.make_async_copy(w_far.at[:, cols], w.at[:, cols], sems.at[p]))
        weights[-1].start()
        for side in range(2):
            for src, dst in pieces(p, side):
                pltpu.make_async_copy(
                    blocks[2 * p + side].at[src], g.at[dst + (slice(None), cols)], sems.at[CHAINS + p]
                ).start()
    for p in range(CHAINS):
        cols = pl.ds(p * WIDTH, WIDTH)
        here = g.at[every + (cols,)]
        weights[p].wait()
        pltpu.make_async_copy(here, here, sems.at[CHAINS + p]).wait()
        outs.append(pltpu.make_async_copy(here, gathered.at[every + (cols,)], sems.at[2 * CHAINS + p]))
        outs[-1].start()
        h = lax.dot_general(
            here[...].reshape(4 * per * n, WIDTH),
            w[:, p * WIDTH : (p + 1) * WIDTH],
            (((1,), (1,)), ((), ())),
            preferred_element_type=jnp.float32,
        ).reshape(hs.shape)
        hs[...] = h if p == 0 else hs[...] + h
    for a, b in ((1, 1), (0, 1), (1, 0), (0, 0)):
        off_x = (mine // 16) ^ (row // 2) ^ a
        off_y = (mine // 8 % 2) ^ (row % 2) ^ b
        for j in range(per):
            slot = (mine % 8) ^ (mask_of(2 * j) % 8) ^ (off_y * 4)
            here = hs[off_y, j // 4, j // 2 % 2, j % 2, off_x]
            if b:
                send[a, slot] = here.astype(jnp.bfloat16)
            else:
                keep[a, slot] = here
    for out in outs:
        out.wait()


def hidden_call(part, where, w, blocks, after=()):
    n = PARTS[part]
    per = SHARDS // 4
    return pl.pallas_call(
        functools.partial(hidden_kernel, n),
        out_shape=[
            jax.ShapeDtypeStruct((2, per, n, HID), jnp.float32),
            jax.ShapeDtypeStruct((2, per, n, HID), jnp.bfloat16),
            pltpu.HBM((2,) * 5 + (n, FEATS), jnp.bfloat16),
        ],
        in_specs=[SMEM] + [ANY] * (1 + 2 * CHAINS + len(after)),
        out_specs=[VMEM, VMEM, ANY],
        scratch_shapes=[
            pltpu.VMEM((2,) * 5 + (n, FEATS), jnp.bfloat16),
            pltpu.VMEM((HID, FEATS), jnp.bfloat16),
            pltpu.VMEM((2,) * 5 + (n, HID), jnp.float32),
            pltpu.SemaphoreType.DMA((3 * CHAINS,)),
        ],
        compiler_params=params(14 + n // 2),
        cost_estimate=pl.CostEstimate(
            flops=2 * SHARDS * n * FEATS * HID, bytes_accessed=SHARDS * n * FEATS * 4, transcendentals=0
        ),
        name="hidden",
    )(where, w, *(f(b.reshape((2,) * 4 + b.shape[1:])) for b, f in zip(blocks, (in_hbm, lambda x: x) * CHAINS)), *after)


def total_kernel(keep, got, *refs):
    mine, far = refs[-2:]
    mine[...] = keep[0] + got[0].astype(jnp.float32)
    far[...] = (keep[1] + got[1].astype(jnp.float32)).astype(jnp.bfloat16)


def total_call(keep, got, after=()):
    return pl.pallas_call(
        total_kernel,
        out_shape=[
            jax.ShapeDtypeStruct(keep.shape[1:], jnp.float32),
            jax.ShapeDtypeStruct(keep.shape[1:], jnp.bfloat16),
        ],
        in_specs=[VMEM, VMEM] + [ANY] * len(after),
        out_specs=[VMEM, VMEM],
        compiler_params=params(8),
        cost_estimate=TINY,
        name="total",
    )(keep, got, *after)


def down_kernel(at_a, at_b, g_a, g_b, *refs):
    out = refs[-1]
    acc = jnp.dot(at_a[...], g_a[...], preferred_element_type=jnp.float32)
    acc += jnp.dot(at_b[...], g_b[...], preferred_element_type=jnp.float32)
    out[...] = acc.astype(jnp.bfloat16)


def down_call(acts, gathered, first, count, base=None, after=()):
    wide = 512
    tokens = [SHARDS * n for n in PARTS]
    in_specs = [pl.BlockSpec((HID, t), lambda j: (0, 0)) for t in tokens]
    in_specs += [pl.BlockSpec((t, wide), lambda j: (0, j + first)) for t in tokens]
    args = [*acts, *(in_hbm(g.reshape(t, FEATS)) for g, t in zip(gathered, tokens))]
    aliases = {}
    if base is not None:
        in_specs.append(ANY)
        args.append(in_hbm(base))
        aliases = {4: 0}
    in_specs += [ANY] * len(after)
    args += after
    return pl.pallas_call(
        down_kernel,
        grid=(count,),
        out_shape=pltpu.HBM((HID, FEATS), jnp.bfloat16),
        in_specs=in_specs,
        out_specs=pl.BlockSpec((HID, wide), lambda j: (0, j + first)),
        input_output_aliases=aliases,
        compiler_params=params(24),
        cost_estimate=pl.CostEstimate(
            flops=2 * 2048 * HID * wide * count, bytes_accessed=count * wide * 2 * (2048 + HID), transcendentals=0
        ),
        name="down",
    )(*args)


def local(grad_out, pre_act, w_down):
    depth, row, col = (lax.axis_index(a) for a in ("depth", "row", "col"))
    where = jnp.stack([row, col, depth * 4 + col]).astype(jnp.int32)
    table = jnp.asarray([mask_of(c) for c in range(SHARDS)], jnp.int32)

    got = swap(in_hbm(grad_out), X)
    fetched = [swap(chunk, mask) for chunk, mask in zip(cut_call(where, pre_act), HOPS)]
    *blocks, fetched = split_call(grad_out, got, fetched)
    other = swap_row(fetched, 1)
    pairs = [(b, swap(b, ORDERS[p][0])) for p, b in enumerate(blocks)]
    blocks = [grow_call([pair])[0] for pair in pairs]
    near = jnp.stack([fetched, other])
    far = swap_row(near, 2)
    pairs = [(b, swap(b, ORDERS[p][1])) for p, b in enumerate(blocks)]
    blocks = [grow_call([pair])[0] for pair in pairs]
    pairs = [(b, swap(b, ORDERS[p][2])) for p, b in enumerate(blocks)]
    own_a = [
        grow_call([pair], STARTS[0], PARTS[0], after=(far,) if p == CHAINS - 1 else ())[0]
        for p, pair in enumerate(pairs)
    ]
    came_a = [swap(own_a[p], ORDERS[p][3]) for p in range(CHAINS)]
    own_b = grow_call(pairs, STARTS[1], PARTS[1], after=(in_hbm(own_a[-1]),))
    came_b = [swap(own_b[p], ORDERS[p][3]) for p in range(CHAINS)]
    own, came = (own_a, own_b), (came_a, came_b)

    pairs = [[b for p in range(CHAINS) for b in (own[part][p], came[part][p])] for part in range(2)]
    keep_a, send_a, g_a = hidden_call(0, where, w_down, pairs[0])
    act_a, act_b, slope_a, slope_b = gelu_call(where, table, pre_act, near, far, after=(keep_a,))
    keep_b, send_b, g_b = hidden_call(1, where, w_down, pairs[1], after=(slope_a,))
    mine_a, far_a = total_call(keep_a, swap_row(send_a, 1), after=(keep_b,))
    far_a = swap_row(far_a, 2)
    grad_down = down_call((act_a, act_b), (g_a, g_b), 0, 2, after=(mine_a,))
    mine_b, far_b = total_call(keep_b, swap_row(send_b, 1), after=(in_hbm(grad_down),))
    far_b = swap_row(far_b, 2)
    grad_down = down_call((act_a, act_b), (g_a, g_b), 2, 4, grad_down)
    done = (mine_a, far_a), (mine_b, far_b)
    parts = [
        ((mine + far.astype(jnp.float32)) * slope).astype(jnp.bfloat16)
        for (mine, far), slope in zip(done, (slope_a, slope_b))
    ]
    grad_pre = jnp.concatenate(parts, 1).reshape(512, HID)
    return (grad_pre, grad_down)


def solution(mesh):
    placed = (P(("depth", "col"), "row"), P("col", "depth"), P(("depth", "col"), "row"))
    return jax.shard_map(
        local,
        mesh=mesh,
        in_specs=placed,
        out_specs=(P("row", ("depth", "col")), P(("depth", "col"), "row")),
        check_vma=False,
    )
```

```python
import functools
import math

import jax
import jax.numpy as jnp
import numpy as np
from jax import lax
from jax.experimental import pallas as pl
from jax.experimental.pallas import tpu as pltpu
from jax.sharding import PartitionSpec as P

gelu_const = math.sqrt(2.0 / math.pi)

SHARDS = 32
ROWS = 64
FEATS = 3072
HID = 768
X, Y0, Y1, Z0, Z1 = 16, 4, 12, 1, 3
DIMS = (X, Z0, Y0, Z1, Y1)
CHAINS = 4
WIDTH = FEATS // CHAINS
ORDERS = tuple(tuple(DIMS[1 + (p + k) % 4] for k in range(4)) for p in range(CHAINS))
HOPS = (Z0, Z1, Z0 ^ Z1)
SLICE = SHARDS * ROWS // 16
PARTS = (48, 16)
STARTS = (0, 48)


def mask_of(c):
    mask = 0
    for k in range(5):
        if c >> k & 1:
            mask ^= DIMS[k]
    return mask


def swap(x, mask):
    if mask >= 4:
        return lax.ppermute(x, "depth", [(i, i ^ (mask >> 2)) for i in range(8)])
    return lax.ppermute(x, "col", [(i, i ^ mask) for i in range(4)])


def swap_row(x, mask):
    return lax.ppermute(x, "row", [(i, i ^ mask) for i in range(4)])


def in_hbm(x):
    return pltpu.with_memory_space_constraint(x, pltpu.HBM)


def params(mib):
    return pltpu.CompilerParams(vmem_limit_bytes=mib * 1024 * 1024)


TINY = pl.CostEstimate(flops=1, bytes_accessed=1, transcendentals=0)
ANY = pl.BlockSpec(memory_space=pl.ANY)
VMEM = pl.BlockSpec(memory_space=pltpu.VMEM)
SMEM = pl.BlockSpec(memory_space=pltpu.SMEM)


def cut_kernel(where, pre, *refs):
    chunks, sem = refs[:-1], refs[-1]
    row, col = where[0], where[1]
    copies = []
    for j, mask in enumerate(HOPS):
        here = pre.at[
            pl.ds(pl.multiple_of(row * SLICE, SLICE), SLICE), pl.ds(pl.multiple_of((col ^ mask) * HID, HID), HID)
        ]
        copies.append(pltpu.make_async_copy(here, chunks[j], sem.at[j]))
    for c in copies:
        c.start()
    for c in copies:
        c.wait()


def cut_call(where, pre):
    return pl.pallas_call(
        cut_kernel,
        out_shape=[jax.ShapeDtypeStruct((SLICE, HID), jnp.bfloat16)] * len(HOPS),
        in_specs=[SMEM, ANY],
        out_specs=[ANY] * len(HOPS),
        scratch_shapes=[pltpu.SemaphoreType.DMA((len(HOPS),))],
        compiler_params=params(1),
        cost_estimate=TINY,
        name="cut",
    )(where, in_hbm(pre))


def split_kernel(own, got, *refs):
    joined, outs, both, sem = refs[: len(HOPS)], refs[len(HOPS) : -2], refs[-2], refs[-1]
    pairs = []
    for p in range(CHAINS):
        for side, src in enumerate((own, got)):
            pairs.append((src.at[:, pl.ds(p * WIDTH, WIDTH)], outs[p].at[side]))
    for j, src in enumerate(joined):
        pairs.append((src, both.at[j]))
    copies = [pltpu.make_async_copy(*pair, sem.at[i]) for i, pair in enumerate(pairs)]
    for c in copies:
        c.start()
    for c in copies:
        c.wait()


def split_call(own, got, join):
    return pl.pallas_call(
        split_kernel,
        out_shape=[jax.ShapeDtypeStruct((2, ROWS, WIDTH), jnp.bfloat16)] * CHAINS
        + [jax.ShapeDtypeStruct((len(HOPS), SLICE, HID), jnp.bfloat16)],
        in_specs=[ANY] * (2 + len(HOPS)),
        out_specs=[ANY] * (CHAINS + 1),
        scratch_shapes=[pltpu.SemaphoreType.DMA((2 * CHAINS + len(HOPS),))],
        compiler_params=params(1),
        cost_estimate=TINY,
        name="split",
    )(in_hbm(own), got, *join)


def grow_kernel(chains, at, n, joined, *refs):
    outs, sem = refs[-1 - chains - (joined > 0) : -1], refs[-1]
    pairs = []
    for p in range(chains):
        blocks = refs[2 * p].shape[0]
        for side in range(2):
            pairs.append((refs[2 * p + side].at[:, pl.ds(at, n)], outs[p].at[pl.ds(side * blocks, blocks)]))
    for j in range(joined):
        pairs.append((refs[2 * chains + j], outs[-1].at[j]))
    copies = [pltpu.make_async_copy(*pair, sem.at[i]) for i, pair in enumerate(pairs)]
    for c in copies:
        c.start()
    for c in copies:
        c.wait()


def grow_call(pairs, at=0, n=ROWS, join=(), after=()):
    blocks = pairs[0][0].shape[0]
    shape = jax.ShapeDtypeStruct if n == ROWS else pltpu.HBM
    return pl.pallas_call(
        functools.partial(grow_kernel, len(pairs), at, n, len(join)),
        out_shape=[shape((2 * blocks, n, WIDTH), jnp.bfloat16)] * len(pairs)
        + [jax.ShapeDtypeStruct((len(join), *j.shape), jnp.bfloat16) for j in join[:1]],
        in_specs=[ANY] * (2 * len(pairs) + len(join) + len(after)),
        out_specs=[ANY] * (len(pairs) + (len(join) > 0)),
        scratch_shapes=[pltpu.SemaphoreType.DMA((2 * len(pairs) + len(join),))],
        compiler_params=params(1),
        cost_estimate=TINY,
        name="grow",
    )(*(x for pair in pairs for x in pair), *join, *after)


def gelu_kernel(where, table, pre, near, far, *refs):
    outs, (buf, sems), acts = refs[-8:-4], refs[-4:-2], refs[-2:]
    act_t, slopes = outs[:2], outs[2:]
    row, col, mine = where[0], where[1], where[2]
    quarter = SHARDS * ROWS // 4
    copies = [
        pltpu.make_async_copy(
            pre.at[:, pl.ds(pl.multiple_of(col * HID, HID), HID)],
            buf.at[pl.ds(pl.multiple_of(col * quarter, quarter), quarter)],
            sems.at[0],
        )
    ]
    for side, src in enumerate((near, far)):
        for i in range(2):
            for j, mask in enumerate(HOPS):
                at = pl.multiple_of((col ^ mask) * quarter + (row ^ (2 * side + i)) * SLICE, SLICE)
                copies.append(pltpu.make_async_copy(src.at[i, j], buf.at[pl.ds(at, SLICE)], sems.at[len(copies)]))
    for c in copies:
        c.start()
    for c in copies:
        c.wait()

    def one_shard(s, carry):
        v = buf[pl.ds(pl.multiple_of((mine ^ table[s]) * ROWS, ROWS), ROWS), :].astype(jnp.float32)
        bend = jnp.tanh(gelu_const * (v + 0.044715 * v * v * v))
        a = (0.5 * v * (1.0 + bend)).astype(jnp.bfloat16)
        for part in range(2):
            n, at = PARTS[part], STARTS[part]
            acts[part][pl.ds(pl.multiple_of(s * n, 16), n), :] = a[at : at + n]
        return carry

    lax.fori_loop(0, SHARDS, one_shard, 0)

    def one_slope(s, carry):
        at_row = pl.multiple_of(row * quarter + s * ROWS, ROWS)
        v = buf[pl.ds(at_row, ROWS), :].astype(jnp.float32)
        bend = jnp.tanh(gelu_const * (v + 0.044715 * v * v * v))
        d = 0.5 * (1.0 + bend) + 0.5 * v * (1.0 - bend * bend) * gelu_const * (1.0 + 3.0 * 0.044715 * v * v)
        for part in range(2):
            n, at = PARTS[part], STARTS[part]
            slopes[part][s] = d[at : at + n]
        return carry

    lax.fori_loop(0, SHARDS // 4, one_slope, 0)

    for part in range(2):

        def one_turn(j, carry, part=part):
            at = pl.multiple_of(j * 128, 128)
            act_t[part][:, pl.ds(at, 128)] = acts[part][pl.ds(at, 128), :].T
            return carry

        lax.fori_loop(0, SHARDS * PARTS[part] // 128, one_turn, 0)


def gelu_call(where, table, pre, near, far, after=()):
    tokens = [SHARDS * n for n in PARTS]
    return pl.pallas_call(
        gelu_kernel,
        out_shape=[jax.ShapeDtypeStruct((HID, t), jnp.bfloat16) for t in tokens]
        + [jax.ShapeDtypeStruct((SHARDS // 4, n, HID), jnp.float32) for n in PARTS],
        in_specs=[SMEM, SMEM] + [ANY] * (3 + len(after)),
        out_specs=[VMEM] * 4,
        scratch_shapes=[pltpu.VMEM((SHARDS * ROWS, HID), jnp.bfloat16), pltpu.SemaphoreType.DMA((13,))]
        + [pltpu.VMEM((t, HID), jnp.bfloat16) for t in tokens],
        compiler_params=params(20),
        cost_estimate=TINY,
        name="gelu",
    )(where, table, in_hbm(pre), near, far, *after)


def pieces(p, side):
    every = slice(None)
    if p == 0:
        return [((every,) * 4, (side,) + (every,) * 4)]
    if p == 1:
        return [((every,) * 4, (every,) * 3 + (side, every))]
    if p == 2:
        return [((i,) + (every,) * 3, (every,) * 2 + (side, i, every)) for i in range(2)]
    return [((every,) * 2 + (i, every), (i, side) + (every,) * 3) for i in range(2)]


def hidden_kernel(n, where, w_far, *refs):
    blocks = refs[: 2 * CHAINS]
    keep, send, gathered, g, w, hs, sems = refs[-7:]
    row, mine = where[0], where[2]
    per = SHARDS // 4
    weights = pltpu.make_async_copy(w_far, w, sems.at[0])
    weights.start()
    for p in range(CHAINS):
        for side in range(2):
            for src, dst in pieces(p, side):
                pltpu.make_async_copy(
                    blocks[2 * p + side].at[src], g.at[dst + (slice(None), pl.ds(p * WIDTH, WIDTH))], sems.at[1]
                ).start()
    pltpu.make_async_copy(g, g, sems.at[1]).wait()
    weights.wait()
    outs = [pltpu.make_async_copy(g, gathered, sems.at[2])]
    outs[0].start()
    for i in range(2):
        h = lax.dot_general(
            g[i].reshape(2 * per * n, FEATS), w[...], (((1,), (1,)), ((), ())), preferred_element_type=jnp.float32
        )
        hs[i] = h.reshape(2, 2, 2, 2, n, HID)
    for a, b in ((1, 1), (0, 1), (1, 0), (0, 0)):
        off_x = (mine // 16) ^ (row // 2) ^ a
        off_y = (mine // 8 % 2) ^ (row % 2) ^ b
        for j in range(per):
            slot = (mine % 8) ^ (mask_of(2 * j) % 8) ^ (off_y * 4)
            here = hs[off_y, j // 4, j // 2 % 2, j % 2, off_x]
            if b:
                send[a, slot] = here.astype(jnp.bfloat16)
            else:
                keep[a, slot] = here
    for out in outs:
        out.wait()


def hidden_call(part, where, w, blocks, after=()):
    n = PARTS[part]
    per = SHARDS // 4
    return pl.pallas_call(
        functools.partial(hidden_kernel, n),
        out_shape=[
            jax.ShapeDtypeStruct((2, per, n, HID), jnp.float32),
            jax.ShapeDtypeStruct((2, per, n, HID), jnp.bfloat16),
            pltpu.HBM((2,) * 5 + (n, FEATS), jnp.bfloat16),
        ],
        in_specs=[SMEM] + [ANY] * (1 + 2 * CHAINS + len(after)),
        out_specs=[VMEM, VMEM, ANY],
        scratch_shapes=[
            pltpu.VMEM((2,) * 5 + (n, FEATS), jnp.bfloat16),
            pltpu.VMEM((HID, FEATS), jnp.bfloat16),
            pltpu.VMEM((2,) * 5 + (n, HID), jnp.float32),
            pltpu.SemaphoreType.DMA((3,)),
        ],
        compiler_params=params(14 + n // 2),
        cost_estimate=pl.CostEstimate(
            flops=2 * SHARDS * n * FEATS * HID, bytes_accessed=SHARDS * n * FEATS * 4, transcendentals=0
        ),
        name="hidden",
    )(where, w, *(f(b.reshape((2,) * 4 + b.shape[1:])) for b, f in zip(blocks, (in_hbm, lambda x: x) * CHAINS)), *after)


def total_kernel(keep, got, *refs):
    mine, far = refs[-2:]
    mine[...] = keep[0] + got[0].astype(jnp.float32)
    far[...] = (keep[1] + got[1].astype(jnp.float32)).astype(jnp.bfloat16)


def total_call(keep, got, after=()):
    return pl.pallas_call(
        total_kernel,
        out_shape=[
            jax.ShapeDtypeStruct(keep.shape[1:], jnp.float32),
            jax.ShapeDtypeStruct(keep.shape[1:], jnp.bfloat16),
        ],
        in_specs=[VMEM, VMEM] + [ANY] * len(after),
        out_specs=[VMEM, VMEM],
        compiler_params=params(8),
        cost_estimate=TINY,
        name="total",
    )(keep, got, *after)


def down_kernel(at_a, at_b, g_a, g_b, *refs):
    out = refs[-1]
    acc = jnp.dot(at_a[...], g_a[...], preferred_element_type=jnp.float32)
    acc += jnp.dot(at_b[...], g_b[...], preferred_element_type=jnp.float32)
    out[...] = acc.astype(jnp.bfloat16)


def down_call(acts, gathered, first, count, base=None, after=()):
    wide = 512
    tokens = [SHARDS * n for n in PARTS]
    in_specs = [pl.BlockSpec((HID, t), lambda j: (0, 0)) for t in tokens]
    in_specs += [pl.BlockSpec((t, wide), lambda j: (0, j + first)) for t in tokens]
    args = [*acts, *(in_hbm(g.reshape(t, FEATS)) for g, t in zip(gathered, tokens))]
    aliases = {}
    if base is not None:
        in_specs.append(ANY)
        args.append(in_hbm(base))
        aliases = {4: 0}
    in_specs += [ANY] * len(after)
    args += after
    return pl.pallas_call(
        down_kernel,
        grid=(count,),
        out_shape=pltpu.HBM((HID, FEATS), jnp.bfloat16),
        in_specs=in_specs,
        out_specs=pl.BlockSpec((HID, wide), lambda j: (0, j + first)),
        input_output_aliases=aliases,
        compiler_params=params(24),
        cost_estimate=pl.CostEstimate(
            flops=2 * 2048 * HID * wide * count, bytes_accessed=count * wide * 2 * (2048 + HID), transcendentals=0
        ),
        name="down",
    )(*args)


def local(grad_out, pre_act, w_down):
    depth, row, col = (lax.axis_index(a) for a in ("depth", "row", "col"))
    where = jnp.stack([row, col, depth * 4 + col]).astype(jnp.int32)
    table = jnp.asarray([mask_of(c) for c in range(SHARDS)], jnp.int32)

    got = swap(in_hbm(grad_out), X)
    fetched = [swap(chunk, mask) for chunk, mask in zip(cut_call(where, pre_act), HOPS)]
    *blocks, fetched = split_call(grad_out, got, fetched)
    other = swap_row(fetched, 1)
    pairs = [(b, swap(b, ORDERS[p][0])) for p, b in enumerate(blocks)]
    blocks = [grow_call([pair])[0] for pair in pairs]
    near = jnp.stack([fetched, other])
    far = swap_row(near, 2)
    pairs = [(b, swap(b, ORDERS[p][1])) for p, b in enumerate(blocks)]
    blocks = [grow_call([pair])[0] for pair in pairs]
    pairs = [(b, swap(b, ORDERS[p][2])) for p, b in enumerate(blocks)]
    own_a = [
        grow_call([pair], STARTS[0], PARTS[0], after=(far,) if p == CHAINS - 1 else ())[0]
        for p, pair in enumerate(pairs)
    ]
    came_a = [swap(own_a[p], ORDERS[p][3]) for p in range(CHAINS)]
    act_a, act_b, slope_a, slope_b = gelu_call(where, table, pre_act, near, far, after=(in_hbm(own_a[-1]),))
    own_b = grow_call(pairs, STARTS[1], PARTS[1], after=(slope_a,))
    came_b = [swap(own_b[p], ORDERS[p][3]) for p in range(CHAINS)]
    own, came = (own_a, own_b), (came_a, came_b)

    pairs = [[b for p in range(CHAINS) for b in (own[part][p], came[part][p])] for part in range(2)]
    keep_a, send_a, g_a = hidden_call(0, where, w_down, pairs[0])
    keep_b, send_b, g_b = hidden_call(1, where, w_down, pairs[1], after=(keep_a,))
    mine_a, far_a = total_call(keep_a, swap_row(send_a, 1), after=(keep_b,))
    far_a = swap_row(far_a, 2)
    grad_down = down_call((act_a, act_b), (g_a, g_b), 0, 2, after=(mine_a,))
    mine_b, far_b = total_call(keep_b, swap_row(send_b, 1), after=(in_hbm(grad_down),))
    far_b = swap_row(far_b, 2)
    grad_down = down_call((act_a, act_b), (g_a, g_b), 2, 4, grad_down)
    done = (mine_a, far_a), (mine_b, far_b)
    parts = [
        ((mine + far.astype(jnp.float32)) * slope).astype(jnp.bfloat16)
        for (mine, far), slope in zip(done, (slope_a, slope_b))
    ]
    grad_pre = jnp.concatenate(parts, 1).reshape(512, HID)
    return (grad_pre, grad_down)


def solution(mesh):
    placed = (P(("depth", "col"), "row"), P("col", "depth"), P(("depth", "col"), "row"))
    return jax.shard_map(
        local,
        mesh=mesh,
        in_specs=placed,
        out_specs=(P("row", ("depth", "col")), P(("depth", "col"), "row")),
        check_vma=False,
    )
```

```python
import functools
import math

import jax
import jax.numpy as jnp
import numpy as np
from jax import lax
from jax.experimental import pallas as pl
from jax.experimental.pallas import tpu as pltpu
from jax.sharding import PartitionSpec as P

gelu_const = math.sqrt(2.0 / math.pi)

SHARDS = 32
ROWS = 64
FEATS = 3072
HID = 768
X, Y0, Y1, Z0, Z1 = 16, 4, 12, 1, 3
DIMS = (X, Z0, Y0, Z1, Y1)
CHAINS = 4
WIDTH = FEATS // CHAINS
ORDERS = tuple(tuple(DIMS[1 + (p + k) % 4] for k in range(4)) for p in range(CHAINS))
HOPS = (Z0, Z1, Z0 ^ Z1)
SLICE = SHARDS * ROWS // 16
PARTS = (32, 32)
STARTS = (0, 32)


def mask_of(c):
    mask = 0
    for k in range(5):
        if c >> k & 1:
            mask ^= DIMS[k]
    return mask


def swap(x, mask):
    if mask >= 4:
        return lax.ppermute(x, "depth", [(i, i ^ (mask >> 2)) for i in range(8)])
    return lax.ppermute(x, "col", [(i, i ^ mask) for i in range(4)])


def swap_row(x, mask):
    return lax.ppermute(x, "row", [(i, i ^ mask) for i in range(4)])


def in_hbm(x):
    return pltpu.with_memory_space_constraint(x, pltpu.HBM)


def params(mib):
    return pltpu.CompilerParams(vmem_limit_bytes=mib * 1024 * 1024)


TINY = pl.CostEstimate(flops=1, bytes_accessed=1, transcendentals=0)
ANY = pl.BlockSpec(memory_space=pl.ANY)
VMEM = pl.BlockSpec(memory_space=pltpu.VMEM)
SMEM = pl.BlockSpec(memory_space=pltpu.SMEM)


def cut_kernel(where, pre, *refs):
    chunks, sem = refs[:-1], refs[-1]
    row, col = where[0], where[1]
    copies = []
    for j, mask in enumerate(HOPS):
        here = pre.at[
            pl.ds(pl.multiple_of(row * SLICE, SLICE), SLICE), pl.ds(pl.multiple_of((col ^ mask) * HID, HID), HID)
        ]
        copies.append(pltpu.make_async_copy(here, chunks[j], sem.at[j]))
    for c in copies:
        c.start()
    for c in copies:
        c.wait()


def cut_call(where, pre):
    return pl.pallas_call(
        cut_kernel,
        out_shape=[jax.ShapeDtypeStruct((SLICE, HID), jnp.bfloat16)] * len(HOPS),
        in_specs=[SMEM, ANY],
        out_specs=[ANY] * len(HOPS),
        scratch_shapes=[pltpu.SemaphoreType.DMA((len(HOPS),))],
        compiler_params=params(1),
        cost_estimate=TINY,
        name="cut",
    )(where, in_hbm(pre))


def split_kernel(own, got, *refs):
    joined, outs, both, sem = refs[: len(HOPS)], refs[len(HOPS) : -2], refs[-2], refs[-1]
    pairs = []
    for p in range(CHAINS):
        for side, src in enumerate((own, got)):
            pairs.append((src.at[:, pl.ds(p * WIDTH, WIDTH)], outs[p].at[side]))
    for j, src in enumerate(joined):
        pairs.append((src, both.at[j]))
    copies = [pltpu.make_async_copy(*pair, sem.at[i]) for i, pair in enumerate(pairs)]
    for c in copies:
        c.start()
    for c in copies:
        c.wait()


def split_call(own, got, join):
    return pl.pallas_call(
        split_kernel,
        out_shape=[jax.ShapeDtypeStruct((2, ROWS, WIDTH), jnp.bfloat16)] * CHAINS
        + [jax.ShapeDtypeStruct((len(HOPS), SLICE, HID), jnp.bfloat16)],
        in_specs=[ANY] * (2 + len(HOPS)),
        out_specs=[ANY] * (CHAINS + 1),
        scratch_shapes=[pltpu.SemaphoreType.DMA((2 * CHAINS + len(HOPS),))],
        compiler_params=params(1),
        cost_estimate=TINY,
        name="split",
    )(in_hbm(own), got, *join)


def grow_kernel(chains, at, n, joined, *refs):
    outs, sem = refs[-1 - chains - (joined > 0) : -1], refs[-1]
    pairs = []
    for p in range(chains):
        blocks = refs[2 * p].shape[0]
        for side in range(2):
            pairs.append((refs[2 * p + side].at[:, pl.ds(at, n)], outs[p].at[pl.ds(side * blocks, blocks)]))
    for j in range(joined):
        pairs.append((refs[2 * chains + j], outs[-1].at[j]))
    copies = [pltpu.make_async_copy(*pair, sem.at[i]) for i, pair in enumerate(pairs)]
    for c in copies:
        c.start()
    for c in copies:
        c.wait()


def grow_call(pairs, at=0, n=ROWS, join=(), after=()):
    blocks = pairs[0][0].shape[0]
    shape = jax.ShapeDtypeStruct if n == ROWS else pltpu.HBM
    return pl.pallas_call(
        functools.partial(grow_kernel, len(pairs), at, n, len(join)),
        out_shape=[shape((2 * blocks, n, WIDTH), jnp.bfloat16)] * len(pairs)
        + [jax.ShapeDtypeStruct((len(join), *j.shape), jnp.bfloat16) for j in join[:1]],
        in_specs=[ANY] * (2 * len(pairs) + len(join) + len(after)),
        out_specs=[ANY] * (len(pairs) + (len(join) > 0)),
        scratch_shapes=[pltpu.SemaphoreType.DMA((2 * len(pairs) + len(join),))],
        compiler_params=params(1),
        cost_estimate=TINY,
        name="grow",
    )(*(x for pair in pairs for x in pair), *join, *after)


def gelu_kernel(where, table, pre, near, far, *refs):
    outs, (buf, sems), acts = refs[-8:-4], refs[-4:-2], refs[-2:]
    act_t, slopes = outs[:2], outs[2:]
    row, col, mine = where[0], where[1], where[2]
    quarter = SHARDS * ROWS // 4
    copies = [
        pltpu.make_async_copy(
            pre.at[:, pl.ds(pl.multiple_of(col * HID, HID), HID)],
            buf.at[pl.ds(pl.multiple_of(col * quarter, quarter), quarter)],
            sems.at[0],
        )
    ]
    for side, src in enumerate((near, far)):
        for i in range(2):
            for j, mask in enumerate(HOPS):
                at = pl.multiple_of((col ^ mask) * quarter + (row ^ (2 * side + i)) * SLICE, SLICE)
                copies.append(pltpu.make_async_copy(src.at[i, j], buf.at[pl.ds(at, SLICE)], sems.at[len(copies)]))
    for c in copies:
        c.start()
    for c in copies:
        c.wait()

    def one_shard(s, carry):
        v = buf[pl.ds(pl.multiple_of((mine ^ table[s]) * ROWS, ROWS), ROWS), :].astype(jnp.float32)
        bend = jnp.tanh(gelu_const * (v + 0.044715 * v * v * v))
        a = (0.5 * v * (1.0 + bend)).astype(jnp.bfloat16)
        for part in range(2):
            n, at = PARTS[part], STARTS[part]
            acts[part][pl.ds(pl.multiple_of(s * n, 16), n), :] = a[at : at + n]
        return carry

    lax.fori_loop(0, SHARDS, one_shard, 0)

    def one_slope(s, carry):
        at_row = pl.multiple_of(row * quarter + s * ROWS, ROWS)
        v = buf[pl.ds(at_row, ROWS), :].astype(jnp.float32)
        bend = jnp.tanh(gelu_const * (v + 0.044715 * v * v * v))
        d = 0.5 * (1.0 + bend) + 0.5 * v * (1.0 - bend * bend) * gelu_const * (1.0 + 3.0 * 0.044715 * v * v)
        for part in range(2):
            n, at = PARTS[part], STARTS[part]
            slopes[part][s] = d[at : at + n]
        return carry

    lax.fori_loop(0, SHARDS // 4, one_slope, 0)

    for part in range(2):

        def one_turn(j, carry, part=part):
            at = pl.multiple_of(j * 128, 128)
            act_t[part][:, pl.ds(at, 128)] = acts[part][pl.ds(at, 128), :].T
            return carry

        lax.fori_loop(0, SHARDS * PARTS[part] // 128, one_turn, 0)


def gelu_call(where, table, pre, near, far, after=()):
    tokens = [SHARDS * n for n in PARTS]
    return pl.pallas_call(
        gelu_kernel,
        out_shape=[jax.ShapeDtypeStruct((HID, t), jnp.bfloat16) for t in tokens]
        + [jax.ShapeDtypeStruct((SHARDS // 4, n, HID), jnp.float32) for n in PARTS],
        in_specs=[SMEM, SMEM] + [ANY] * (3 + len(after)),
        out_specs=[VMEM] * 4,
        scratch_shapes=[pltpu.VMEM((SHARDS * ROWS, HID), jnp.bfloat16), pltpu.SemaphoreType.DMA((13,))]
        + [pltpu.VMEM((t, HID), jnp.bfloat16) for t in tokens],
        compiler_params=params(20),
        cost_estimate=TINY,
        name="gelu",
    )(where, table, in_hbm(pre), near, far, *after)


def pieces(p, side):
    every = slice(None)
    if p == 0:
        return [((every,) * 4, (side,) + (every,) * 4)]
    if p == 1:
        return [((every,) * 4, (every,) * 3 + (side, every))]
    if p == 2:
        return [((i,) + (every,) * 3, (every,) * 2 + (side, i, every)) for i in range(2)]
    return [((every,) * 2 + (i, every), (i, side) + (every,) * 3) for i in range(2)]


def hidden_kernel(n, where, w_far, *refs):
    blocks = refs[: 2 * CHAINS]
    keep, send, gathered, g, w, hs, sems = refs[-7:]
    row, mine = where[0], where[2]
    per = SHARDS // 4
    weights = pltpu.make_async_copy(w_far, w, sems.at[0])
    weights.start()
    for p in range(CHAINS):
        for side in range(2):
            for src, dst in pieces(p, side):
                pltpu.make_async_copy(
                    blocks[2 * p + side].at[src], g.at[dst + (slice(None), pl.ds(p * WIDTH, WIDTH))], sems.at[1]
                ).start()
    pltpu.make_async_copy(g, g, sems.at[1]).wait()
    weights.wait()
    outs = [pltpu.make_async_copy(g, gathered, sems.at[2])]
    outs[0].start()
    for i in range(2):
        h = lax.dot_general(
            g[i].reshape(2 * per * n, FEATS), w[...], (((1,), (1,)), ((), ())), preferred_element_type=jnp.float32
        )
        hs[i] = h.reshape(2, 2, 2, 2, n, HID)
    for a, b in ((1, 1), (0, 1), (1, 0), (0, 0)):
        off_x = (mine // 16) ^ (row // 2) ^ a
        off_y = (mine // 8 % 2) ^ (row % 2) ^ b
        for j in range(per):
            slot = (mine % 8) ^ (mask_of(2 * j) % 8) ^ (off_y * 4)
            here = hs[off_y, j // 4, j // 2 % 2, j % 2, off_x]
            if b:
                send[a, slot] = here.astype(jnp.bfloat16)
            else:
                keep[a, slot] = here
    for out in outs:
        out.wait()


def hidden_call(part, where, w, blocks, after=()):
    n = PARTS[part]
    per = SHARDS // 4
    return pl.pallas_call(
        functools.partial(hidden_kernel, n),
        out_shape=[
            jax.ShapeDtypeStruct((2, per, n, HID), jnp.float32),
            jax.ShapeDtypeStruct((2, per, n, HID), jnp.bfloat16),
            pltpu.HBM((2,) * 5 + (n, FEATS), jnp.bfloat16),
        ],
        in_specs=[SMEM] + [ANY] * (1 + 2 * CHAINS + len(after)),
        out_specs=[VMEM, VMEM, ANY],
        scratch_shapes=[
            pltpu.VMEM((2,) * 5 + (n, FEATS), jnp.bfloat16),
            pltpu.VMEM((HID, FEATS), jnp.bfloat16),
            pltpu.VMEM((2,) * 5 + (n, HID), jnp.float32),
            pltpu.SemaphoreType.DMA((3,)),
        ],
        compiler_params=params(14 + n // 2),
        cost_estimate=pl.CostEstimate(
            flops=2 * SHARDS * n * FEATS * HID, bytes_accessed=SHARDS * n * FEATS * 4, transcendentals=0
        ),
        name="hidden",
    )(where, w, *(f(b.reshape((2,) * 4 + b.shape[1:])) for b, f in zip(blocks, (in_hbm, lambda x: x) * CHAINS)), *after)


def total_kernel(keep, got, *refs):
    mine, far = refs[-2:]
    mine[...] = keep[0] + got[0].astype(jnp.float32)
    far[...] = (keep[1] + got[1].astype(jnp.float32)).astype(jnp.bfloat16)


def total_call(keep, got, after=()):
    return pl.pallas_call(
        total_kernel,
        out_shape=[
            jax.ShapeDtypeStruct(keep.shape[1:], jnp.float32),
            jax.ShapeDtypeStruct(keep.shape[1:], jnp.bfloat16),
        ],
        in_specs=[VMEM, VMEM] + [ANY] * len(after),
        out_specs=[VMEM, VMEM],
        compiler_params=params(8),
        cost_estimate=TINY,
        name="total",
    )(keep, got, *after)


def down_kernel(at_a, at_b, g_a, g_b, *refs):
    out = refs[-1]
    acc = jnp.dot(at_a[...], g_a[...], preferred_element_type=jnp.float32)
    acc += jnp.dot(at_b[...], g_b[...], preferred_element_type=jnp.float32)
    out[...] = acc.astype(jnp.bfloat16)


def down_call(acts, gathered, first, count, base=None, after=()):
    wide = 512
    tokens = [SHARDS * n for n in PARTS]
    in_specs = [pl.BlockSpec((HID, t), lambda j: (0, 0)) for t in tokens]
    in_specs += [pl.BlockSpec((t, wide), lambda j: (0, j + first)) for t in tokens]
    args = [*acts, *(in_hbm(g.reshape(t, FEATS)) for g, t in zip(gathered, tokens))]
    aliases = {}
    if base is not None:
        in_specs.append(ANY)
        args.append(in_hbm(base))
        aliases = {4: 0}
    in_specs += [ANY] * len(after)
    args += after
    return pl.pallas_call(
        down_kernel,
        grid=(count,),
        out_shape=pltpu.HBM((HID, FEATS), jnp.bfloat16),
        in_specs=in_specs,
        out_specs=pl.BlockSpec((HID, wide), lambda j: (0, j + first)),
        input_output_aliases=aliases,
        compiler_params=params(24),
        cost_estimate=pl.CostEstimate(
            flops=2 * 2048 * HID * wide * count, bytes_accessed=count * wide * 2 * (2048 + HID), transcendentals=0
        ),
        name="down",
    )(*args)


def local(grad_out, pre_act, w_down):
    depth, row, col = (lax.axis_index(a) for a in ("depth", "row", "col"))
    where = jnp.stack([row, col, depth * 4 + col]).astype(jnp.int32)
    table = jnp.asarray([mask_of(c) for c in range(SHARDS)], jnp.int32)

    got = swap(in_hbm(grad_out), X)
    fetched = [swap(chunk, mask) for chunk, mask in zip(cut_call(where, pre_act), HOPS)]
    *blocks, fetched = split_call(grad_out, got, fetched)
    other = swap_row(fetched, 1)
    pairs = [(b, swap(b, ORDERS[p][0])) for p, b in enumerate(blocks)]
    blocks = [grow_call([pair])[0] for pair in pairs]
    near = jnp.stack([fetched, other])
    far = swap_row(near, 2)
    pairs = [(b, swap(b, ORDERS[p][1])) for p, b in enumerate(blocks)]
    blocks = [grow_call([pair])[0] for pair in pairs]
    pairs = [(b, swap(b, ORDERS[p][2])) for p, b in enumerate(blocks)]
    own_a = [
        grow_call([pair], STARTS[0], PARTS[0], after=(far,) if p == CHAINS - 1 else ())[0]
        for p, pair in enumerate(pairs)
    ]
    came_a = [swap(own_a[p], ORDERS[p][3]) for p in range(CHAINS)]
    act_a, act_b, slope_a, slope_b = gelu_call(where, table, pre_act, near, far, after=(in_hbm(own_a[-1]),))
    own_b = grow_call(pairs, STARTS[1], PARTS[1], after=(slope_a,))
    came_b = [swap(own_b[p], ORDERS[p][3]) for p in range(CHAINS)]
    own, came = (own_a, own_b), (came_a, came_b)

    pairs = [[b for p in range(CHAINS) for b in (own[part][p], came[part][p])] for part in range(2)]
    keep_a, send_a, g_a = hidden_call(0, where, w_down, pairs[0], after=(in_hbm(own_b[0]),))
    keep_b, send_b, g_b = hidden_call(1, where, w_down, pairs[1], after=(keep_a,))
    mine_a, far_a = total_call(keep_a, swap_row(send_a, 1), after=(keep_b,))
    far_a = swap_row(far_a, 2)
    grad_down = down_call((act_a, act_b), (g_a, g_b), 0, 2, after=(mine_a,))
    mine_b, far_b = total_call(keep_b, swap_row(send_b, 1), after=(in_hbm(grad_down),))
    far_b = swap_row(far_b, 2)
    grad_down = down_call((act_a, act_b), (g_a, g_b), 2, 4, grad_down)
    done = (mine_a, far_a), (mine_b, far_b)
    parts = [
        ((mine + far.astype(jnp.float32)) * slope).astype(jnp.bfloat16)
        for (mine, far), slope in zip(done, (slope_a, slope_b))
    ]
    grad_pre = jnp.concatenate(parts, 1).reshape(512, HID)
    return (grad_pre, grad_down)


def solution(mesh):
    placed = (P(("depth", "col"), "row"), P("col", "depth"), P(("depth", "col"), "row"))
    return jax.shard_map(
        local,
        mesh=mesh,
        in_specs=placed,
        out_specs=(P("row", ("depth", "col")), P(("depth", "col"), "row")),
        check_vma=False,
    )
```

```python
import functools
import math

import jax
import jax.numpy as jnp
import numpy as np
from jax import lax
from jax.experimental import pallas as pl
from jax.experimental.pallas import tpu as pltpu
from jax.sharding import PartitionSpec as P

gelu_const = math.sqrt(2.0 / math.pi)

SHARDS = 32
ROWS = 64
FEATS = 3072
HID = 768
X, Y0, Y1, Z0, Z1 = 16, 4, 12, 1, 3
DIMS = (X, Z0, Y0, Z1, Y1)
CHAINS = 4
WIDTH = FEATS // CHAINS
ORDERS = tuple(tuple(DIMS[1 + (p + k) % 4] for k in range(4)) for p in range(CHAINS))
HOPS = (Z0, Z1, Z0 ^ Z1)
SLICE = SHARDS * ROWS // 16
PARTS = (32, 32)
STARTS = (0, 32)


def mask_of(c):
    mask = 0
    for k in range(5):
        if c >> k & 1:
            mask ^= DIMS[k]
    return mask


def swap(x, mask):
    if mask >= 4:
        return lax.ppermute(x, "depth", [(i, i ^ (mask >> 2)) for i in range(8)])
    return lax.ppermute(x, "col", [(i, i ^ mask) for i in range(4)])


def swap_row(x, mask):
    return lax.ppermute(x, "row", [(i, i ^ mask) for i in range(4)])


def in_hbm(x):
    return pltpu.with_memory_space_constraint(x, pltpu.HBM)


def params(mib):
    return pltpu.CompilerParams(vmem_limit_bytes=mib * 1024 * 1024)


TINY = pl.CostEstimate(flops=1, bytes_accessed=1, transcendentals=0)
ANY = pl.BlockSpec(memory_space=pl.ANY)
VMEM = pl.BlockSpec(memory_space=pltpu.VMEM)
SMEM = pl.BlockSpec(memory_space=pltpu.SMEM)


def cut_kernel(where, pre, *refs):
    chunks, sem = refs[:-1], refs[-1]
    row, col = where[0], where[1]
    copies = []
    for j, mask in enumerate(HOPS):
        here = pre.at[
            pl.ds(pl.multiple_of(row * SLICE, SLICE), SLICE), pl.ds(pl.multiple_of((col ^ mask) * HID, HID), HID)
        ]
        copies.append(pltpu.make_async_copy(here, chunks[j], sem.at[j]))
    for c in copies:
        c.start()
    for c in copies:
        c.wait()


def cut_call(where, pre):
    return pl.pallas_call(
        cut_kernel,
        out_shape=[jax.ShapeDtypeStruct((SLICE, HID), jnp.bfloat16)] * len(HOPS),
        in_specs=[SMEM, ANY],
        out_specs=[ANY] * len(HOPS),
        scratch_shapes=[pltpu.SemaphoreType.DMA((len(HOPS),))],
        compiler_params=params(1),
        cost_estimate=TINY,
        name="cut",
    )(where, in_hbm(pre))


def split_kernel(own, got, *refs):
    joined, outs, both, sem = refs[: len(HOPS)], refs[len(HOPS) : -2], refs[-2], refs[-1]
    pairs = []
    for p in range(CHAINS):
        for side, src in enumerate((own, got)):
            pairs.append((src.at[:, pl.ds(p * WIDTH, WIDTH)], outs[p].at[side]))
    for j, src in enumerate(joined):
        pairs.append((src, both.at[j]))
    copies = [pltpu.make_async_copy(*pair, sem.at[i]) for i, pair in enumerate(pairs)]
    for c in copies:
        c.start()
    for c in copies:
        c.wait()


def split_call(own, got, join):
    return pl.pallas_call(
        split_kernel,
        out_shape=[jax.ShapeDtypeStruct((2, ROWS, WIDTH), jnp.bfloat16)] * CHAINS
        + [jax.ShapeDtypeStruct((len(HOPS), SLICE, HID), jnp.bfloat16)],
        in_specs=[ANY] * (2 + len(HOPS)),
        out_specs=[ANY] * (CHAINS + 1),
        scratch_shapes=[pltpu.SemaphoreType.DMA((2 * CHAINS + len(HOPS),))],
        compiler_params=params(1),
        cost_estimate=TINY,
        name="split",
    )(in_hbm(own), got, *join)


def grow_kernel(chains, at, n, joined, *refs):
    outs, sem = refs[-1 - chains - (joined > 0) : -1], refs[-1]
    pairs = []
    for p in range(chains):
        blocks = refs[2 * p].shape[0]
        for side in range(2):
            pairs.append((refs[2 * p + side].at[:, pl.ds(at, n)], outs[p].at[pl.ds(side * blocks, blocks)]))
    for j in range(joined):
        pairs.append((refs[2 * chains + j], outs[-1].at[j]))
    copies = [pltpu.make_async_copy(*pair, sem.at[i]) for i, pair in enumerate(pairs)]
    for c in copies:
        c.start()
    for c in copies:
        c.wait()


def grow_call(pairs, at=0, n=ROWS, join=(), after=()):
    blocks = pairs[0][0].shape[0]
    shape = jax.ShapeDtypeStruct if n == ROWS else pltpu.HBM
    return pl.pallas_call(
        functools.partial(grow_kernel, len(pairs), at, n, len(join)),
        out_shape=[shape((2 * blocks, n, WIDTH), jnp.bfloat16)] * len(pairs)
        + [jax.ShapeDtypeStruct((len(join), *j.shape), jnp.bfloat16) for j in join[:1]],
        in_specs=[ANY] * (2 * len(pairs) + len(join) + len(after)),
        out_specs=[ANY] * (len(pairs) + (len(join) > 0)),
        scratch_shapes=[pltpu.SemaphoreType.DMA((2 * len(pairs) + len(join),))],
        compiler_params=params(1),
        cost_estimate=TINY,
        name="grow",
    )(*(x for pair in pairs for x in pair), *join, *after)


def gelu_kernel(where, table, pre, near, far, *refs):
    outs, (buf, sems), acts = refs[-8:-4], refs[-4:-2], refs[-2:]
    act_t, slopes = outs[:2], outs[2:]
    row, col, mine = where[0], where[1], where[2]
    quarter = SHARDS * ROWS // 4
    copies = [
        pltpu.make_async_copy(
            pre.at[:, pl.ds(pl.multiple_of(col * HID, HID), HID)],
            buf.at[pl.ds(pl.multiple_of(col * quarter, quarter), quarter)],
            sems.at[0],
        )
    ]
    for side, src in enumerate((near, far)):
        for i in range(2):
            for j, mask in enumerate(HOPS):
                at = pl.multiple_of((col ^ mask) * quarter + (row ^ (2 * side + i)) * SLICE, SLICE)
                copies.append(pltpu.make_async_copy(src.at[i, j], buf.at[pl.ds(at, SLICE)], sems.at[len(copies)]))
    for c in copies:
        c.start()
    for c in copies:
        c.wait()

    def one_shard(s, carry):
        v = buf[pl.ds(pl.multiple_of((mine ^ table[s]) * ROWS, ROWS), ROWS), :].astype(jnp.float32)
        bend = jnp.tanh(gelu_const * (v + 0.044715 * v * v * v))
        a = (0.5 * v * (1.0 + bend)).astype(jnp.bfloat16)
        for part in range(2):
            n, at = PARTS[part], STARTS[part]
            acts[part][pl.ds(pl.multiple_of(s * n, 16), n), :] = a[at : at + n]
        return carry

    lax.fori_loop(0, SHARDS, one_shard, 0)

    def one_slope(s, carry):
        at_row = pl.multiple_of(row * quarter + s * ROWS, ROWS)
        v = buf[pl.ds(at_row, ROWS), :].astype(jnp.float32)
        bend = jnp.tanh(gelu_const * (v + 0.044715 * v * v * v))
        d = 0.5 * (1.0 + bend) + 0.5 * v * (1.0 - bend * bend) * gelu_const * (1.0 + 3.0 * 0.044715 * v * v)
        for part in range(2):
            n, at = PARTS[part], STARTS[part]
            slopes[part][s] = d[at : at + n]
        return carry

    lax.fori_loop(0, SHARDS // 4, one_slope, 0)

    for part in range(2):

        def one_turn(j, carry, part=part):
            at = pl.multiple_of(j * 128, 128)
            act_t[part][:, pl.ds(at, 128)] = acts[part][pl.ds(at, 128), :].T
            return carry

        lax.fori_loop(0, SHARDS * PARTS[part] // 128, one_turn, 0)


def gelu_call(where, table, pre, near, far, after=()):
    tokens = [SHARDS * n for n in PARTS]
    return pl.pallas_call(
        gelu_kernel,
        out_shape=[jax.ShapeDtypeStruct((HID, t), jnp.bfloat16) for t in tokens]
        + [jax.ShapeDtypeStruct((SHARDS // 4, n, HID), jnp.float32) for n in PARTS],
        in_specs=[SMEM, SMEM] + [ANY] * (3 + len(after)),
        out_specs=[VMEM] * 4,
        scratch_shapes=[pltpu.VMEM((SHARDS * ROWS, HID), jnp.bfloat16), pltpu.SemaphoreType.DMA((13,))]
        + [pltpu.VMEM((t, HID), jnp.bfloat16) for t in tokens],
        compiler_params=params(20),
        cost_estimate=TINY,
        name="gelu",
    )(where, table, in_hbm(pre), near, far, *after)


def pieces(p, side):
    every = slice(None)
    if p == 0:
        return [((every,) * 4, (side,) + (every,) * 4)]
    if p == 1:
        return [((every,) * 4, (every,) * 3 + (side, every))]
    if p == 2:
        return [((i,) + (every,) * 3, (every,) * 2 + (side, i, every)) for i in range(2)]
    return [((every,) * 2 + (i, every), (i, side) + (every,) * 3) for i in range(2)]


def hidden_kernel(n, where, w_far, *refs):
    blocks = refs[: 2 * CHAINS]
    keeps, sends, (gathered, g, w, hs, sems) = refs[-9:-7], refs[-7:-5], refs[-5:]
    row, mine = where[0], where[2]
    per = SHARDS // 4
    weights = pltpu.make_async_copy(w_far, w, sems.at[0])
    weights.start()
    for p in range(CHAINS):
        for side in range(2):
            for src, dst in pieces(p, side):
                pltpu.make_async_copy(
                    blocks[2 * p + side].at[src], g.at[dst + (slice(None), pl.ds(p * WIDTH, WIDTH))], sems.at[1]
                ).start()
    pltpu.make_async_copy(g, g, sems.at[1]).wait()
    weights.wait()
    outs = [pltpu.make_async_copy(g, gathered, sems.at[2])]
    outs[0].start()
    for i in range(2):
        h = lax.dot_general(
            g[i].reshape(2 * per * n, FEATS), w[...], (((1,), (1,)), ((), ())), preferred_element_type=jnp.float32
        )
        hs[i] = h.reshape(2, 2, 2, 2, n, HID)
    for a, b in ((1, 1), (0, 1), (1, 0), (0, 0)):
        off_x = (mine // 16) ^ (row // 2) ^ a
        off_y = (mine // 8 % 2) ^ (row % 2) ^ b
        for j in range(per):
            slot = (mine % 8) ^ (mask_of(2 * j) % 8) ^ (off_y * 4)
            here = hs[off_y, j // 4, j // 2 % 2, j % 2, off_x]
            if b:
                sends[a][slot] = here.astype(jnp.bfloat16)
            else:
                keeps[a][slot] = here
    for out in outs:
        out.wait()


def hidden_call(part, where, w, blocks, after=()):
    n = PARTS[part]
    per = SHARDS // 4
    return pl.pallas_call(
        functools.partial(hidden_kernel, n),
        out_shape=[
            jax.ShapeDtypeStruct((per, n, HID), jnp.float32),
            jax.ShapeDtypeStruct((per, n, HID), jnp.float32),
            jax.ShapeDtypeStruct((per, n, HID), jnp.bfloat16),
            jax.ShapeDtypeStruct((per, n, HID), jnp.bfloat16),
            pltpu.HBM((2,) * 5 + (n, FEATS), jnp.bfloat16),
        ],
        in_specs=[SMEM] + [ANY] * (1 + 2 * CHAINS + len(after)),
        out_specs=[VMEM] * 4 + [ANY],
        scratch_shapes=[
            pltpu.VMEM((2,) * 5 + (n, FEATS), jnp.bfloat16),
            pltpu.VMEM((HID, FEATS), jnp.bfloat16),
            pltpu.VMEM((2,) * 5 + (n, HID), jnp.float32),
            pltpu.SemaphoreType.DMA((3,)),
        ],
        compiler_params=params(14 + n // 2),
        cost_estimate=pl.CostEstimate(
            flops=2 * SHARDS * n * FEATS * HID, bytes_accessed=SHARDS * n * FEATS * 4, transcendentals=0
        ),
        name="hidden",
    )(where, w, *(f(b.reshape((2,) * 4 + b.shape[1:])) for b, f in zip(blocks, (in_hbm, lambda x: x) * CHAINS)), *after)


def total_kernel(keep, got, *refs):
    refs[-1][...] = (keep[...].astype(jnp.float32) + got[...].astype(jnp.float32)).astype(jnp.bfloat16)


def total_call(keep, got, after=()):
    return pl.pallas_call(
        total_kernel,
        out_shape=jax.ShapeDtypeStruct(keep.shape, jnp.bfloat16),
        in_specs=[VMEM, VMEM] + [ANY] * len(after),
        out_specs=VMEM,
        compiler_params=params(8),
        cost_estimate=TINY,
        name="total",
    )(keep, got, *after)


def down_kernel(at_a, at_b, g_a, g_b, *refs):
    out = refs[-1]
    acc = jnp.dot(at_a[...], g_a[...], preferred_element_type=jnp.float32)
    acc += jnp.dot(at_b[...], g_b[...], preferred_element_type=jnp.float32)
    out[...] = acc.astype(jnp.bfloat16)


def down_call(acts, gathered, first, count, base=None, after=()):
    wide = 512
    tokens = [SHARDS * n for n in PARTS]
    in_specs = [pl.BlockSpec((HID, t), lambda j: (0, 0)) for t in tokens]
    in_specs += [pl.BlockSpec((t, wide), lambda j: (0, j + first)) for t in tokens]
    args = [*acts, *(in_hbm(g.reshape(t, FEATS)) for g, t in zip(gathered, tokens))]
    aliases = {}
    if base is not None:
        in_specs.append(ANY)
        args.append(in_hbm(base))
        aliases = {4: 0}
    in_specs += [ANY] * len(after)
    args += after
    return pl.pallas_call(
        down_kernel,
        grid=(count,),
        out_shape=pltpu.HBM((HID, FEATS), jnp.bfloat16),
        in_specs=in_specs,
        out_specs=pl.BlockSpec((HID, wide), lambda j: (0, j + first)),
        input_output_aliases=aliases,
        compiler_params=params(24),
        cost_estimate=pl.CostEstimate(
            flops=2 * 2048 * HID * wide * count, bytes_accessed=count * wide * 2 * (2048 + HID), transcendentals=0
        ),
        name="down",
    )(*args)


def local(grad_out, pre_act, w_down):
    depth, row, col = (lax.axis_index(a) for a in ("depth", "row", "col"))
    where = jnp.stack([row, col, depth * 4 + col]).astype(jnp.int32)
    table = jnp.asarray([mask_of(c) for c in range(SHARDS)], jnp.int32)

    got = swap(in_hbm(grad_out), X)
    fetched = [swap(chunk, mask) for chunk, mask in zip(cut_call(where, pre_act), HOPS)]
    *blocks, fetched = split_call(grad_out, got, fetched)
    other = swap_row(fetched, 1)
    pairs = [(b, swap(b, ORDERS[p][0])) for p, b in enumerate(blocks)]
    blocks = [grow_call([pair])[0] for pair in pairs]
    near = jnp.stack([fetched, other])
    far = swap_row(near, 2)
    pairs = [(b, swap(b, ORDERS[p][1])) for p, b in enumerate(blocks)]
    blocks = [grow_call([pair])[0] for pair in pairs]
    pairs = [(b, swap(b, ORDERS[p][2])) for p, b in enumerate(blocks)]
    own_a = [
        grow_call([pair], STARTS[0], PARTS[0], after=(far,) if p == CHAINS - 1 else ())[0]
        for p, pair in enumerate(pairs)
    ]
    came_a = [swap(own_a[p], ORDERS[p][3]) for p in range(CHAINS)]
    act_a, act_b, slope_a, slope_b = gelu_call(where, table, pre_act, near, far, after=(in_hbm(own_a[-1]),))
    own_b = grow_call(pairs, STARTS[1], PARTS[1], after=(slope_a,))
    came_b = [swap(own_b[p], ORDERS[p][3]) for p in range(CHAINS)]
    own, came = (own_a, own_b), (came_a, came_b)

    pairs = [[b for p in range(CHAINS) for b in (own[part][p], came[part][p])] for part in range(2)]
    keep_a, keep_far, send_a, send_far, g_a = hidden_call(0, where, w_down, pairs[0], after=(in_hbm(own_b[0]),))
    leave_a = total_call(keep_far, swap_row(send_far, 1))
    keep_b, keep_far, send_b, send_far, g_b = hidden_call(1, where, w_down, pairs[1], after=(leave_a,))
    far_a, near_a = swap_row(leave_a, 2), swap_row(send_a, 1)
    near_b = swap_row(send_b, 1)
    grad_down = down_call((act_a, act_b), (g_a, g_b), 0, 1, after=(far_a,))
    leave_b = total_call(keep_far, swap_row(send_far, 1), after=(in_hbm(grad_down),))
    far_b = swap_row(leave_b, 2)
    grad_down = down_call((act_a, act_b), (g_a, g_b), 1, 5, grad_down)
    done = (keep_a, near_a, far_a), (keep_b, near_b, far_b)
    parts = [
        ((mine + near.astype(jnp.float32) + far.astype(jnp.float32)) * slope).astype(jnp.bfloat16)
        for (mine, near, far), slope in zip(done, (slope_a, slope_b))
    ]
    grad_pre = jnp.concatenate(parts, 1).reshape(512, HID)
    return (grad_pre, grad_down)


def solution(mesh):
    placed = (P(("depth", "col"), "row"), P("col", "depth"), P(("depth", "col"), "row"))
    return jax.shard_map(
        local,
        mesh=mesh,
        in_specs=placed,
        out_specs=(P("row", ("depth", "col")), P(("depth", "col"), "row")),
        check_vma=False,
    )
```

```python
import functools
import math

import jax
import jax.numpy as jnp
import numpy as np
from jax import lax
from jax.experimental import pallas as pl
from jax.experimental.pallas import tpu as pltpu
from jax.sharding import PartitionSpec as P

gelu_const = math.sqrt(2.0 / math.pi)

SHARDS = 32
ROWS = 64
FEATS = 3072
HID = 768
X, Y0, Y1, Z0, Z1 = 16, 4, 12, 1, 3
DIMS = (X, Z0, Y0, Z1, Y1)
CHAINS = 4
WIDTH = FEATS // CHAINS
ORDERS = tuple(tuple(DIMS[1 + (p + k) % 4] for k in range(4)) for p in range(CHAINS))
HOPS = (Z0, Z1, Z0 ^ Z1)
SLICE = SHARDS * ROWS // 16
PARTS = (32, 32)
STARTS = (0, 32)


def mask_of(c):
    mask = 0
    for k in range(5):
        if c >> k & 1:
            mask ^= DIMS[k]
    return mask


def swap(x, mask):
    if mask >= 4:
        return lax.ppermute(x, "depth", [(i, i ^ (mask >> 2)) for i in range(8)])
    return lax.ppermute(x, "col", [(i, i ^ mask) for i in range(4)])


def swap_row(x, mask):
    return lax.ppermute(x, "row", [(i, i ^ mask) for i in range(4)])


def in_hbm(x):
    return pltpu.with_memory_space_constraint(x, pltpu.HBM)


def params(mib):
    return pltpu.CompilerParams(vmem_limit_bytes=mib * 1024 * 1024)


TINY = pl.CostEstimate(flops=1, bytes_accessed=1, transcendentals=0)
ANY = pl.BlockSpec(memory_space=pl.ANY)
VMEM = pl.BlockSpec(memory_space=pltpu.VMEM)
SMEM = pl.BlockSpec(memory_space=pltpu.SMEM)


def cut_kernel(where, pre, *refs):
    chunks, sem = refs[:-1], refs[-1]
    row, col = where[0], where[1]
    copies = []
    for j, mask in enumerate(HOPS):
        here = pre.at[
            pl.ds(pl.multiple_of(row * SLICE, SLICE), SLICE), pl.ds(pl.multiple_of((col ^ mask) * HID, HID), HID)
        ]
        copies.append(pltpu.make_async_copy(here, chunks[j], sem.at[j]))
    for c in copies:
        c.start()
    for c in copies:
        c.wait()


def cut_call(where, pre):
    return pl.pallas_call(
        cut_kernel,
        out_shape=[jax.ShapeDtypeStruct((SLICE, HID), jnp.bfloat16)] * len(HOPS),
        in_specs=[SMEM, ANY],
        out_specs=[ANY] * len(HOPS),
        scratch_shapes=[pltpu.SemaphoreType.DMA((len(HOPS),))],
        compiler_params=params(1),
        cost_estimate=TINY,
        name="cut",
    )(where, in_hbm(pre))


def split_kernel(own, got, *refs):
    joined, outs, both, sem = refs[: len(HOPS)], refs[len(HOPS) : -2], refs[-2], refs[-1]
    pairs = []
    for p in range(CHAINS):
        for side, src in enumerate((own, got)):
            pairs.append((src.at[:, pl.ds(p * WIDTH, WIDTH)], outs[p].at[side]))
    for j, src in enumerate(joined):
        pairs.append((src, both.at[j]))
    copies = [pltpu.make_async_copy(*pair, sem.at[i]) for i, pair in enumerate(pairs)]
    for c in copies:
        c.start()
    for c in copies:
        c.wait()


def split_call(own, got, join):
    return pl.pallas_call(
        split_kernel,
        out_shape=[jax.ShapeDtypeStruct((2, ROWS, WIDTH), jnp.bfloat16)] * CHAINS
        + [jax.ShapeDtypeStruct((len(HOPS), SLICE, HID), jnp.bfloat16)],
        in_specs=[ANY] * (2 + len(HOPS)),
        out_specs=[ANY] * (CHAINS + 1),
        scratch_shapes=[pltpu.SemaphoreType.DMA((2 * CHAINS + len(HOPS),))],
        compiler_params=params(1),
        cost_estimate=TINY,
        name="split",
    )(in_hbm(own), got, *join)


def grow_kernel(chains, at, n, joined, *refs):
    outs, sem = refs[-1 - chains - (joined > 0) : -1], refs[-1]
    pairs = []
    for p in range(chains):
        blocks = refs[2 * p].shape[0]
        for side in range(2):
            pairs.append((refs[2 * p + side].at[:, pl.ds(at, n)], outs[p].at[pl.ds(side * blocks, blocks)]))
    for j in range(joined):
        pairs.append((refs[2 * chains + j], outs[-1].at[j]))
    copies = [pltpu.make_async_copy(*pair, sem.at[i]) for i, pair in enumerate(pairs)]
    for c in copies:
        c.start()
    for c in copies:
        c.wait()


def grow_call(pairs, at=0, n=ROWS, join=(), after=()):
    blocks = pairs[0][0].shape[0]
    shape = jax.ShapeDtypeStruct if n == ROWS else pltpu.HBM
    return pl.pallas_call(
        functools.partial(grow_kernel, len(pairs), at, n, len(join)),
        out_shape=[shape((2 * blocks, n, WIDTH), jnp.bfloat16)] * len(pairs)
        + [jax.ShapeDtypeStruct((len(join), *j.shape), jnp.bfloat16) for j in join[:1]],
        in_specs=[ANY] * (2 * len(pairs) + len(join) + len(after)),
        out_specs=[ANY] * (len(pairs) + (len(join) > 0)),
        scratch_shapes=[pltpu.SemaphoreType.DMA((2 * len(pairs) + len(join),))],
        compiler_params=params(1),
        cost_estimate=TINY,
        name="grow",
    )(*(x for pair in pairs for x in pair), *join, *after)


def gelu_kernel(where, table, pre, near, far, *refs):
    outs, (buf, sems), acts = refs[-8:-4], refs[-4:-2], refs[-2:]
    act_t, slopes = outs[:2], outs[2:]
    row, col, mine = where[0], where[1], where[2]
    quarter = SHARDS * ROWS // 4
    copies = [
        pltpu.make_async_copy(
            pre.at[:, pl.ds(pl.multiple_of(col * HID, HID), HID)],
            buf.at[pl.ds(pl.multiple_of(col * quarter, quarter), quarter)],
            sems.at[0],
        )
    ]
    for side, src in enumerate((near, far)):
        for i in range(2):
            for j, mask in enumerate(HOPS):
                at = pl.multiple_of((col ^ mask) * quarter + (row ^ (2 * side + i)) * SLICE, SLICE)
                copies.append(pltpu.make_async_copy(src.at[i, j], buf.at[pl.ds(at, SLICE)], sems.at[len(copies)]))
    for c in copies:
        c.start()
    for c in copies:
        c.wait()

    def one_shard(s, carry):
        shard = mine ^ table[s]
        v = buf[pl.ds(pl.multiple_of(shard * ROWS, ROWS), ROWS), :].astype(jnp.float32)
        bend = jnp.tanh(gelu_const * (v + 0.044715 * v * v * v))
        a = (0.5 * v * (1.0 + bend)).astype(jnp.bfloat16)
        for part in range(2):
            n, at = PARTS[part], STARTS[part]
            acts[part][pl.ds(pl.multiple_of(s * n, 16), n), :] = a[at : at + n]

        @pl.when(shard // 8 == row)
        def _():
            d = 0.5 * (1.0 + bend) + 0.5 * v * (1.0 - bend * bend) * gelu_const * (1.0 + 3.0 * 0.044715 * v * v)
            for part in range(2):
                n, at = PARTS[part], STARTS[part]
                slopes[part][shard % 8] = d[at : at + n]

        return carry

    lax.fori_loop(0, SHARDS, one_shard, 0)

    for part in range(2):

        def one_turn(j, carry, part=part):
            at = pl.multiple_of(j * 128, 128)
            act_t[part][:, pl.ds(at, 128)] = acts[part][pl.ds(at, 128), :].T
            return carry

        lax.fori_loop(0, SHARDS * PARTS[part] // 128, one_turn, 0)


def gelu_call(where, table, pre, near, far, after=()):
    tokens = [SHARDS * n for n in PARTS]
    return pl.pallas_call(
        gelu_kernel,
        out_shape=[jax.ShapeDtypeStruct((HID, t), jnp.bfloat16) for t in tokens]
        + [jax.ShapeDtypeStruct((SHARDS // 4, n, HID), jnp.float32) for n in PARTS],
        in_specs=[SMEM, SMEM] + [ANY] * (3 + len(after)),
        out_specs=[VMEM] * 4,
        scratch_shapes=[pltpu.VMEM((SHARDS * ROWS, HID), jnp.bfloat16), pltpu.SemaphoreType.DMA((13,))]
        + [pltpu.VMEM((t, HID), jnp.bfloat16) for t in tokens],
        compiler_params=params(20),
        cost_estimate=TINY,
        name="gelu",
    )(where, table, in_hbm(pre), near, far, *after)


def pieces(p, side):
    every = slice(None)
    if p == 0:
        return [((every,) * 4, (side,) + (every,) * 4)]
    if p == 1:
        return [((every,) * 4, (every,) * 3 + (side, every))]
    if p == 2:
        return [((i,) + (every,) * 3, (every,) * 2 + (side, i, every)) for i in range(2)]
    return [((every,) * 2 + (i, every), (i, side) + (every,) * 3) for i in range(2)]


def hidden_kernel(n, where, w_far, *refs):
    blocks = refs[: 2 * CHAINS]
    keeps, sends, (gathered, g, w, hs, sems) = refs[-9:-7], refs[-7:-5], refs[-5:]
    row, mine = where[0], where[2]
    per = SHARDS // 4
    weights = pltpu.make_async_copy(w_far, w, sems.at[0])
    weights.start()
    for p in range(CHAINS):
        for side in range(2):
            for src, dst in pieces(p, side):
                pltpu.make_async_copy(
                    blocks[2 * p + side].at[src], g.at[dst + (slice(None), pl.ds(p * WIDTH, WIDTH))], sems.at[1]
                ).start()
    pltpu.make_async_copy(g, g, sems.at[1]).wait()
    weights.wait()
    outs = [pltpu.make_async_copy(g, gathered, sems.at[2])]
    outs[0].start()
    for i in range(2):
        h = lax.dot_general(
            g[i].reshape(2 * per * n, FEATS), w[...], (((1,), (1,)), ((), ())), preferred_element_type=jnp.float32
        )
        hs[i] = h.reshape(2, 2, 2, 2, n, HID)
    for a, b in ((1, 1), (0, 1), (1, 0), (0, 0)):
        off_x = (mine // 16) ^ (row // 2) ^ a
        off_y = (mine // 8 % 2) ^ (row % 2) ^ b
        for j in range(per):
            slot = (mine % 8) ^ (mask_of(2 * j) % 8) ^ (off_y * 4)
            here = hs[off_y, j // 4, j // 2 % 2, j % 2, off_x]
            if b:
                sends[a][slot] = here.astype(jnp.bfloat16)
            else:
                keeps[a][slot] = here
    for out in outs:
        out.wait()


def hidden_call(part, where, w, blocks, after=()):
    n = PARTS[part]
    per = SHARDS // 4
    return pl.pallas_call(
        functools.partial(hidden_kernel, n),
        out_shape=[
            jax.ShapeDtypeStruct((per, n, HID), jnp.float32),
            jax.ShapeDtypeStruct((per, n, HID), jnp.float32),
            jax.ShapeDtypeStruct((per, n, HID), jnp.bfloat16),
            jax.ShapeDtypeStruct((per, n, HID), jnp.bfloat16),
            pltpu.HBM((2,) * 5 + (n, FEATS), jnp.bfloat16),
        ],
        in_specs=[SMEM] + [ANY] * (1 + 2 * CHAINS + len(after)),
        out_specs=[VMEM] * 4 + [ANY],
        scratch_shapes=[
            pltpu.VMEM((2,) * 5 + (n, FEATS), jnp.bfloat16),
            pltpu.VMEM((HID, FEATS), jnp.bfloat16),
            pltpu.VMEM((2,) * 5 + (n, HID), jnp.float32),
            pltpu.SemaphoreType.DMA((3,)),
        ],
        compiler_params=params(14 + n // 2),
        cost_estimate=pl.CostEstimate(
            flops=2 * SHARDS * n * FEATS * HID, bytes_accessed=SHARDS * n * FEATS * 4, transcendentals=0
        ),
        name="hidden",
    )(where, w, *(f(b.reshape((2,) * 4 + b.shape[1:])) for b, f in zip(blocks, (in_hbm, lambda x: x) * CHAINS)), *after)


def total_kernel(keep, got, *refs):
    refs[-1][...] = (keep[...].astype(jnp.float32) + got[...].astype(jnp.float32)).astype(jnp.bfloat16)


def total_call(keep, got, after=()):
    return pl.pallas_call(
        total_kernel,
        out_shape=jax.ShapeDtypeStruct(keep.shape, jnp.bfloat16),
        in_specs=[VMEM, VMEM] + [ANY] * len(after),
        out_specs=VMEM,
        compiler_params=params(8),
        cost_estimate=TINY,
        name="total",
    )(keep, got, *after)


def down_kernel(at_a, at_b, g_a, g_b, *refs):
    out = refs[-1]
    acc = jnp.dot(at_a[...], g_a[...], preferred_element_type=jnp.float32)
    acc += jnp.dot(at_b[...], g_b[...], preferred_element_type=jnp.float32)
    out[...] = acc.astype(jnp.bfloat16)


def down_call(acts, gathered, first, count, base=None, after=()):
    wide = 768
    tokens = [SHARDS * n for n in PARTS]
    in_specs = [pl.BlockSpec((HID, t), lambda j: (0, 0)) for t in tokens]
    in_specs += [pl.BlockSpec((t, wide), lambda j: (0, j + first)) for t in tokens]
    args = [*acts, *(in_hbm(g.reshape(t, FEATS)) for g, t in zip(gathered, tokens))]
    aliases = {}
    if base is not None:
        in_specs.append(ANY)
        args.append(in_hbm(base))
        aliases = {4: 0}
    in_specs += [ANY] * len(after)
    args += after
    return pl.pallas_call(
        down_kernel,
        grid=(count,),
        out_shape=pltpu.HBM((HID, FEATS), jnp.bfloat16),
        in_specs=in_specs,
        out_specs=pl.BlockSpec((HID, wide), lambda j: (0, j + first)),
        input_output_aliases=aliases,
        compiler_params=params(24),
        cost_estimate=pl.CostEstimate(
            flops=2 * 2048 * HID * wide * count, bytes_accessed=count * wide * 2 * (2048 + HID), transcendentals=0
        ),
        name="down",
    )(*args)


def local(grad_out, pre_act, w_down):
    depth, row, col = (lax.axis_index(a) for a in ("depth", "row", "col"))
    where = jnp.stack([row, col, depth * 4 + col]).astype(jnp.int32)
    table = jnp.asarray([mask_of(c) for c in range(SHARDS)], jnp.int32)

    got = swap(in_hbm(grad_out), X)
    fetched = [swap(chunk, mask) for chunk, mask in zip(cut_call(where, pre_act), HOPS)]
    *blocks, fetched = split_call(grad_out, got, fetched)
    other = swap_row(fetched, 1)
    pairs = [(b, swap(b, ORDERS[p][0])) for p, b in enumerate(blocks)]
    blocks = [grow_call([pair])[0] for pair in pairs]
    near = jnp.stack([fetched, other])
    far = swap_row(near, 2)
    pairs = [(b, swap(b, ORDERS[p][1])) for p, b in enumerate(blocks)]
    blocks = [grow_call([pair])[0] for pair in pairs]
    pairs = [(b, swap(b, ORDERS[p][2])) for p, b in enumerate(blocks)]
    own_a = [
        grow_call([pair], STARTS[0], PARTS[0], after=(far,) if p == CHAINS - 1 else ())[0]
        for p, pair in enumerate(pairs)
    ]
    came_a = [swap(own_a[p], ORDERS[p][3]) for p in range(CHAINS)]
    act_a, act_b, slope_a, slope_b = gelu_call(where, table, pre_act, near, far, after=(in_hbm(own_a[-1]),))
    own_b = grow_call(pairs, STARTS[1], PARTS[1], after=(slope_a,))
    came_b = [swap(own_b[p], ORDERS[p][3]) for p in range(CHAINS)]
    own, came = (own_a, own_b), (came_a, came_b)

    pairs = [[b for p in range(CHAINS) for b in (own[part][p], came[part][p])] for part in range(2)]
    keep_a, keep_far, send_a, send_far, g_a = hidden_call(0, where, w_down, pairs[0], after=(in_hbm(own_b[0]),))
    leave_a = total_call(keep_far, swap_row(send_far, 1))
    keep_b, keep_far, send_b, send_far, g_b = hidden_call(1, where, w_down, pairs[1], after=(leave_a,))
    far_a, near_a = swap_row(leave_a, 2), swap_row(send_a, 1)
    near_b = swap_row(send_b, 1)
    grad_down = down_call((act_a, act_b), (g_a, g_b), 0, 1, after=(far_a,))
    leave_b = total_call(keep_far, swap_row(send_far, 1), after=(in_hbm(grad_down),))
    far_b = swap_row(leave_b, 2)
    grad_down = down_call((act_a, act_b), (g_a, g_b), 1, 3, grad_down)
    done = (keep_a, near_a, far_a), (keep_b, near_b, far_b)
    parts = [
        ((mine + near.astype(jnp.float32) + far.astype(jnp.float32)) * slope).astype(jnp.bfloat16)
        for (mine, near, far), slope in zip(done, (slope_a, slope_b))
    ]
    grad_pre = jnp.concatenate(parts, 1).reshape(512, HID)
    return (grad_pre, grad_down)


def solution(mesh):
    placed = (P(("depth", "col"), "row"), P("col", "depth"), P(("depth", "col"), "row"))
    return jax.shard_map(
        local,
        mesh=mesh,
        in_specs=placed,
        out_specs=(P("row", ("depth", "col")), P(("depth", "col"), "row")),
        check_vma=False,
    )
```

```python
import functools
import math

import jax
import jax.numpy as jnp
import numpy as np
from jax import lax
from jax.experimental import pallas as pl
from jax.experimental.pallas import tpu as pltpu
from jax.sharding import PartitionSpec as P

gelu_const = math.sqrt(2.0 / math.pi)

SHARDS = 32
ROWS = 64
FEATS = 3072
HID = 768
X, Y0, Y1, Z0, Z1 = 16, 4, 12, 1, 3
DIMS = (X, Z0, Y0, Z1, Y1)
CHAINS = 4
WIDTH = FEATS // CHAINS
ORDERS = tuple(tuple(DIMS[1 + (p + k) % 4] for k in range(4)) for p in range(CHAINS))
HOPS = (Z0, Z1, Z0 ^ Z1)
SLICE = SHARDS * ROWS // 16
PARTS = (32, 32)
STARTS = (0, 32)


def mask_of(c):
    mask = 0
    for k in range(5):
        if c >> k & 1:
            mask ^= DIMS[k]
    return mask


def swap(x, mask):
    if mask >= 4:
        return lax.ppermute(x, "depth", [(i, i ^ (mask >> 2)) for i in range(8)])
    return lax.ppermute(x, "col", [(i, i ^ mask) for i in range(4)])


def swap_row(x, mask):
    return lax.ppermute(x, "row", [(i, i ^ mask) for i in range(4)])


def in_hbm(x):
    return pltpu.with_memory_space_constraint(x, pltpu.HBM)


def params(mib):
    return pltpu.CompilerParams(vmem_limit_bytes=mib * 1024 * 1024)


TINY = pl.CostEstimate(flops=1, bytes_accessed=1, transcendentals=0)
ANY = pl.BlockSpec(memory_space=pl.ANY)
VMEM = pl.BlockSpec(memory_space=pltpu.VMEM)
SMEM = pl.BlockSpec(memory_space=pltpu.SMEM)


def cut_kernel(where, pre, *refs):
    chunks, sem = refs[:-1], refs[-1]
    row, col = where[0], where[1]
    copies = []
    for j, mask in enumerate(HOPS):
        here = pre.at[
            pl.ds(pl.multiple_of(row * SLICE, SLICE), SLICE), pl.ds(pl.multiple_of((col ^ mask) * HID, HID), HID)
        ]
        copies.append(pltpu.make_async_copy(here, chunks[j], sem.at[j]))
    for c in copies:
        c.start()
    for c in copies:
        c.wait()


def cut_call(where, pre):
    return pl.pallas_call(
        cut_kernel,
        out_shape=[jax.ShapeDtypeStruct((SLICE, HID), jnp.bfloat16)] * len(HOPS),
        in_specs=[SMEM, ANY],
        out_specs=[ANY] * len(HOPS),
        scratch_shapes=[pltpu.SemaphoreType.DMA((len(HOPS),))],
        compiler_params=params(1),
        cost_estimate=TINY,
        name="cut",
    )(where, in_hbm(pre))


def split_kernel(own, got, *refs):
    joined, outs, both, sem = refs[: len(HOPS)], refs[len(HOPS) : -2], refs[-2], refs[-1]
    pairs = []
    for p in range(CHAINS):
        for side, src in enumerate((own, got)):
            pairs.append((src.at[:, pl.ds(p * WIDTH, WIDTH)], outs[p].at[side]))
    for j, src in enumerate(joined):
        pairs.append((src, both.at[j]))
    copies = [pltpu.make_async_copy(*pair, sem.at[i]) for i, pair in enumerate(pairs)]
    for c in copies:
        c.start()
    for c in copies:
        c.wait()


def split_call(own, got, join):
    return pl.pallas_call(
        split_kernel,
        out_shape=[jax.ShapeDtypeStruct((2, ROWS, WIDTH), jnp.bfloat16)] * CHAINS
        + [jax.ShapeDtypeStruct((len(HOPS), SLICE, HID), jnp.bfloat16)],
        in_specs=[ANY] * (2 + len(HOPS)),
        out_specs=[ANY] * (CHAINS + 1),
        scratch_shapes=[pltpu.SemaphoreType.DMA((2 * CHAINS + len(HOPS),))],
        compiler_params=params(1),
        cost_estimate=TINY,
        name="split",
    )(in_hbm(own), got, *join)


def grow_kernel(chains, at, n, joined, *refs):
    outs, sem = refs[-1 - chains - (joined > 0) : -1], refs[-1]
    pairs = []
    for p in range(chains):
        blocks = refs[2 * p].shape[0]
        for side in range(2):
            pairs.append((refs[2 * p + side].at[:, pl.ds(at, n)], outs[p].at[pl.ds(side * blocks, blocks)]))
    for j in range(joined):
        pairs.append((refs[2 * chains + j], outs[-1].at[j]))
    copies = [pltpu.make_async_copy(*pair, sem.at[i]) for i, pair in enumerate(pairs)]
    for c in copies:
        c.start()
    for c in copies:
        c.wait()


def grow_call(pairs, at=0, n=ROWS, join=(), after=()):
    blocks = pairs[0][0].shape[0]
    shape = jax.ShapeDtypeStruct if n == ROWS else pltpu.HBM
    return pl.pallas_call(
        functools.partial(grow_kernel, len(pairs), at, n, len(join)),
        out_shape=[shape((2 * blocks, n, WIDTH), jnp.bfloat16)] * len(pairs)
        + [jax.ShapeDtypeStruct((len(join), *j.shape), jnp.bfloat16) for j in join[:1]],
        in_specs=[ANY] * (2 * len(pairs) + len(join) + len(after)),
        out_specs=[ANY] * (len(pairs) + (len(join) > 0)),
        scratch_shapes=[pltpu.SemaphoreType.DMA((2 * len(pairs) + len(join),))],
        compiler_params=params(1),
        cost_estimate=TINY,
        name="grow",
    )(*(x for pair in pairs for x in pair), *join, *after)


def gelu_kernel(where, table, pre, near, far, *refs):
    outs, (buf, sems), acts = refs[-8:-4], refs[-4:-2], refs[-2:]
    act_t, slopes = outs[:2], outs[2:]
    row, col, mine = where[0], where[1], where[2]
    quarter = SHARDS * ROWS // 4
    copies = [
        pltpu.make_async_copy(
            pre.at[:, pl.ds(pl.multiple_of(col * HID, HID), HID)],
            buf.at[pl.ds(pl.multiple_of(col * quarter, quarter), quarter)],
            sems.at[0],
        )
    ]
    for side, src in enumerate((near, far)):
        for i in range(2):
            for j, mask in enumerate(HOPS):
                at = pl.multiple_of((col ^ mask) * quarter + (row ^ (2 * side + i)) * SLICE, SLICE)
                copies.append(pltpu.make_async_copy(src.at[i, j], buf.at[pl.ds(at, SLICE)], sems.at[len(copies)]))
    for c in copies:
        c.start()
    for c in copies:
        c.wait()

    def one_shard(s, carry):
        shard = mine ^ table[s]
        v = buf[pl.ds(pl.multiple_of(shard * ROWS, ROWS), ROWS), :].astype(jnp.float32)
        bend = jnp.tanh(gelu_const * (v + 0.044715 * v * v * v))
        a = (0.5 * v * (1.0 + bend)).astype(jnp.bfloat16)
        for part in range(2):
            n, at = PARTS[part], STARTS[part]
            acts[part][pl.ds(pl.multiple_of(s * n, 16), n), :] = a[at : at + n]

        @pl.when(shard // 8 == row)
        def _():
            d = 0.5 * (1.0 + bend) + 0.5 * v * (1.0 - bend * bend) * gelu_const * (1.0 + 3.0 * 0.044715 * v * v)
            for part in range(2):
                n, at = PARTS[part], STARTS[part]
                slopes[part][shard % 8] = d[at : at + n]

        return carry

    lax.fori_loop(0, SHARDS, one_shard, 0)

    for part in range(2):

        def one_turn(j, carry, part=part):
            at = pl.multiple_of(j * 128, 128)
            act_t[part][:, pl.ds(at, 128)] = acts[part][pl.ds(at, 128), :].T
            return carry

        lax.fori_loop(0, SHARDS * PARTS[part] // 128, one_turn, 0)


def gelu_call(where, table, pre, near, far, after=()):
    tokens = [SHARDS * n for n in PARTS]
    return pl.pallas_call(
        gelu_kernel,
        out_shape=[jax.ShapeDtypeStruct((HID, t), jnp.bfloat16) for t in tokens]
        + [jax.ShapeDtypeStruct((SHARDS // 4, n, HID), jnp.float32) for n in PARTS],
        in_specs=[SMEM, SMEM] + [ANY] * (3 + len(after)),
        out_specs=[VMEM] * 4,
        scratch_shapes=[pltpu.VMEM((SHARDS * ROWS, HID), jnp.bfloat16), pltpu.SemaphoreType.DMA((13,))]
        + [pltpu.VMEM((t, HID), jnp.bfloat16) for t in tokens],
        compiler_params=params(20),
        cost_estimate=TINY,
        name="gelu",
    )(where, table, in_hbm(pre), near, far, *after)


def pieces(p, side):
    every = slice(None)
    if p == 0:
        return [((every,) * 4, (side,) + (every,) * 4)]
    if p == 1:
        return [((every,) * 4, (every,) * 3 + (side, every))]
    if p == 2:
        return [((i,) + (every,) * 3, (every,) * 2 + (side, i, every)) for i in range(2)]
    return [((every,) * 2 + (i, every), (i, side) + (every,) * 3) for i in range(2)]


def hidden_kernel(n, where, w_far, *refs):
    blocks = refs[: 2 * CHAINS]
    keeps, sends, (gathered, g, w, hs, sems) = refs[-9:-7], refs[-7:-5], refs[-5:]
    row, mine = where[0], where[2]
    per = SHARDS // 4
    weights = pltpu.make_async_copy(w_far, w, sems.at[0])
    weights.start()
    for p in range(CHAINS):
        for side in range(2):
            for src, dst in pieces(p, side):
                pltpu.make_async_copy(
                    blocks[2 * p + side].at[src], g.at[dst + (slice(None), pl.ds(p * WIDTH, WIDTH))], sems.at[1]
                ).start()
    pltpu.make_async_copy(g, g, sems.at[1]).wait()
    weights.wait()
    outs = [pltpu.make_async_copy(g, gathered, sems.at[2])]
    outs[0].start()
    for i in range(2):
        h = lax.dot_general(
            g[i].reshape(2 * per * n, FEATS), w[...], (((1,), (1,)), ((), ())), preferred_element_type=jnp.float32
        )
        hs[i] = h.reshape(2, 2, 2, 2, n, HID)
    for a, b in ((1, 1), (0, 1), (1, 0), (0, 0)):
        off_x = (mine // 16) ^ (row // 2) ^ a
        off_y = (mine // 8 % 2) ^ (row % 2) ^ b
        for j in range(per):
            slot = (mine % 8) ^ (mask_of(2 * j) % 8) ^ (off_y * 4)
            here = hs[off_y, j // 4, j // 2 % 2, j % 2, off_x]
            if b:
                sends[a][slot] = here.astype(jnp.bfloat16)
            else:
                keeps[a][slot] = here
    for out in outs:
        out.wait()


def hidden_call(part, where, w, blocks, after=()):
    n = PARTS[part]
    per = SHARDS // 4
    return pl.pallas_call(
        functools.partial(hidden_kernel, n),
        out_shape=[
            jax.ShapeDtypeStruct((per, n, HID), jnp.float32),
            jax.ShapeDtypeStruct((per, n, HID), jnp.float32),
            jax.ShapeDtypeStruct((per, n, HID), jnp.bfloat16),
            jax.ShapeDtypeStruct((per, n, HID), jnp.bfloat16),
            pltpu.HBM((2,) * 5 + (n, FEATS), jnp.bfloat16),
        ],
        in_specs=[SMEM] + [ANY] * (1 + 2 * CHAINS + len(after)),
        out_specs=[VMEM] * 4 + [ANY],
        scratch_shapes=[
            pltpu.VMEM((2,) * 5 + (n, FEATS), jnp.bfloat16),
            pltpu.VMEM((HID, FEATS), jnp.bfloat16),
            pltpu.VMEM((2,) * 5 + (n, HID), jnp.float32),
            pltpu.SemaphoreType.DMA((3,)),
        ],
        compiler_params=params(14 + n // 2),
        cost_estimate=pl.CostEstimate(
            flops=2 * SHARDS * n * FEATS * HID, bytes_accessed=SHARDS * n * FEATS * 4, transcendentals=0
        ),
        name="hidden",
    )(where, w, *(f(b.reshape((2,) * 4 + b.shape[1:])) for b, f in zip(blocks, (in_hbm, lambda x: x) * CHAINS)), *after)


def total_kernel(keep, got, *refs):
    refs[-1][...] = (keep[...].astype(jnp.float32) + got[...].astype(jnp.float32)).astype(jnp.bfloat16)


def total_call(keep, got, after=()):
    return pl.pallas_call(
        total_kernel,
        out_shape=jax.ShapeDtypeStruct(keep.shape, jnp.bfloat16),
        in_specs=[VMEM, VMEM] + [ANY] * len(after),
        out_specs=VMEM,
        compiler_params=params(8),
        cost_estimate=TINY,
        name="total",
    )(keep, got, *after)


def down_kernel(at_a, at_b, g_a, g_b, *refs):
    out = refs[-1]
    acc = jnp.dot(at_a[...], g_a[...], preferred_element_type=jnp.float32)
    acc += jnp.dot(at_b[...], g_b[...], preferred_element_type=jnp.float32)
    out[...] = acc.astype(jnp.bfloat16)


def down_call(acts, gathered, first, count, base=None, after=()):
    wide = 768
    tokens = [SHARDS * n for n in PARTS]
    in_specs = [pl.BlockSpec((HID, t), lambda j: (0, 0)) for t in tokens]
    in_specs += [pl.BlockSpec((t, wide), lambda j: (0, j + first)) for t in tokens]
    args = [*acts, *(in_hbm(g.reshape(t, FEATS)) for g, t in zip(gathered, tokens))]
    aliases = {}
    if base is not None:
        in_specs.append(ANY)
        args.append(in_hbm(base))
        aliases = {4: 0}
    in_specs += [ANY] * len(after)
    args += after
    return pl.pallas_call(
        down_kernel,
        grid=(count,),
        out_shape=pltpu.HBM((HID, FEATS), jnp.bfloat16),
        in_specs=in_specs,
        out_specs=pl.BlockSpec((HID, wide), lambda j: (0, j + first)),
        input_output_aliases=aliases,
        compiler_params=params(24),
        cost_estimate=pl.CostEstimate(
            flops=2 * 2048 * HID * wide * count, bytes_accessed=count * wide * 2 * (2048 + HID), transcendentals=0
        ),
        name="down",
    )(*args)


def local(grad_out, pre_act, w_down):
    depth, row, col = (lax.axis_index(a) for a in ("depth", "row", "col"))
    where = jnp.stack([row, col, depth * 4 + col]).astype(jnp.int32)
    table = jnp.asarray([mask_of(c) for c in range(SHARDS)], jnp.int32)

    got = swap(in_hbm(grad_out), X)
    fetched = [swap(chunk, mask) for chunk, mask in zip(cut_call(where, pre_act), HOPS)]
    *blocks, fetched = split_call(grad_out, got, fetched)
    other = swap_row(fetched, 1)
    pairs = [(b, swap(b, ORDERS[p][0])) for p, b in enumerate(blocks)]
    blocks = [grow_call([pair])[0] for pair in pairs]
    near = jnp.stack([fetched, other])
    far = swap_row(near, 2)
    pairs = [(b, swap(b, ORDERS[p][1])) for p, b in enumerate(blocks)]
    blocks = [grow_call([pair])[0] for pair in pairs]
    pairs = [(b, swap(b, ORDERS[p][2])) for p, b in enumerate(blocks)]
    own_a = [
        grow_call([pair], STARTS[0], PARTS[0], after=(far,) if p == 0 else ())[0]
        for p, pair in enumerate(pairs)
    ]
    came_a = [swap(own_a[p], ORDERS[p][3]) for p in range(CHAINS)]
    act_a, act_b, slope_a, slope_b = gelu_call(where, table, pre_act, near, far, after=(in_hbm(own_a[-1]),))
    own_b = grow_call(pairs, STARTS[1], PARTS[1], after=(slope_a,))
    came_b = [swap(own_b[p], ORDERS[p][3]) for p in range(CHAINS)]
    own, came = (own_a, own_b), (came_a, came_b)

    pairs = [[b for p in range(CHAINS) for b in (own[part][p], came[part][p])] for part in range(2)]
    keep_a, keep_far, send_a, send_far, g_a = hidden_call(0, where, w_down, pairs[0], after=(in_hbm(own_b[0]),))
    leave_a = total_call(keep_far, swap_row(send_far, 1))
    keep_b, keep_far, send_b, send_far, g_b = hidden_call(1, where, w_down, pairs[1], after=(leave_a,))
    far_a, near_a = swap_row(leave_a, 2), swap_row(send_a, 1)
    near_b = swap_row(send_b, 1)
    grad_down = down_call((act_a, act_b), (g_a, g_b), 0, 1, after=(far_a,))
    leave_b = total_call(keep_far, swap_row(send_far, 1), after=(in_hbm(grad_down),))
    far_b = swap_row(leave_b, 2)
    grad_down = down_call((act_a, act_b), (g_a, g_b), 1, 3, grad_down)
    done = (keep_a, near_a, far_a), (keep_b, near_b, far_b)
    parts = [
        ((mine + near.astype(jnp.float32) + far.astype(jnp.float32)) * slope).astype(jnp.bfloat16)
        for (mine, near, far), slope in zip(done, (slope_a, slope_b))
    ]
    grad_pre = jnp.concatenate(parts, 1).reshape(512, HID)
    return (grad_pre, grad_down)


def solution(mesh):
    placed = (P(("depth", "col"), "row"), P("col", "depth"), P(("depth", "col"), "row"))
    return jax.shard_map(
        local,
        mesh=mesh,
        in_specs=placed,
        out_specs=(P("row", ("depth", "col")), P(("depth", "col"), "row")),
        check_vma=False,
    )
```
